32 devices in a mesh: wide: 16 (over z, x, core), blk: 2 (over y).
Axes of the slice: x: 2, y: 2, z: 4, core: 2. Of those that a mesh axis runs over, the one named last changes fastest.
Arguments:
- tokens: bfloat16 [32768, 768], P(('wide', 'blk')), may hold values from -6 to 6
- lengths: int32 [16, 6], P('wide'), may hold values from 1 to 1536, as said below
- ln1_gain: float32 [768], replicated, may hold values from 0.5 to 1.5
- ln1_bias: float32 [768], replicated, may hold values from -3 to 3
- w_qkv: bfloat16 [768, 2304], replicated, may hold values from -0.21875 to 0.21875
- q_gain: float32 [768], replicated, may hold values from 0.5 to 1.5
- k_gain: float32 [768], replicated, may hold values from 0.5 to 1.5
- w_out: bfloat16 [768, 768], replicated, may hold values from -6 to 6
- ln2_gain: float32 [768], replicated, may hold values from 0.5 to 1.5
- ln2_bias: float32 [768], replicated, may hold values from -3 to 3
- w_up: bfloat16 [768, 3072], replicated, may hold values from -0.21875 to 0.21875
- w_down: bfloat16 [3072, 768], replicated, may hold values from -0.109375 to 0.109375
- cotangent: bfloat16 [32768, 768], P(('wide', 'blk')), may hold values from -6 to 6
Outputs:
- output: bfloat16 [32768, 768], P(('wide', 'blk'))
- grad_tokens: bfloat16 [32768, 768], P(('wide', 'blk'))
- grad_ln1_gain: float32 [768], P(('wide', 'blk'))
- grad_ln1_bias: float32 [768], P(('wide', 'blk'))
- grad_w_qkv: float32 [768, 2304], P(('wide', 'blk'))
- grad_q_gain: float32 [768], P(('wide', 'blk'))
- grad_k_gain: float32 [768], P(('wide', 'blk'))
- grad_w_out: float32 [768, 768], P(('wide', 'blk'))
- grad_ln2_gain: float32 [768], P(('wide', 'blk'))
- grad_ln2_bias: float32 [768], P(('wide', 'blk'))
- grad_w_up: float32 [768, 3072], P(('wide', 'blk'))
- grad_w_down: float32 [3072, 768], P(('wide', 'blk'))
The draws below stay inside these ranges and needn't reach their ends.
Inputs may be any that keep to these rules, and one draw needn't show every extreme that they name: Each row of lengths sums to 2048. The second image of every group begins within its first 1024 patches and ends within its last 1024.
All inputs are finite; a program needn't handle non-finite values.
Results may differ from the reference program's by a relative error of at most 0.02.
Values may be sent and summed in bfloat16 or wider, within the bound.
A program may use at most 320 MiB of HBM per device.

```python
import math
import jax
import jax.numpy as jnp
from jax import lax

D = 768
H = 12
HD = 64
FF = 3072
SEQS = 6
TOK_DEV = 1024
GROUP = 2048
GROUPS = 16
TOKENS = 32768


def draw_lengths(key, part):
    key = jax.random.fold_in(key, 11)
    first_key, second_key = jax.random.split(key, 2)
    extra = jax.random.randint(first_key, (GROUPS,), 0, TOK_DEV // 4)
    extra = extra * (jnp.arange(GROUPS) > 0).astype(jnp.int32)
    rest = TOK_DEV // 2 + extra
    longest = GROUP - rest
    spread = jnp.maximum((rest - SEQS + 1) // (SEQS - 1), 0) + 1
    raw = jax.random.randint(second_key, (GROUPS, SEQS - 2), 0, 1 << 20)
    pieces = 1 + raw % spread[:, None]
    final = rest - jnp.sum(pieces, axis=1)
    table = jnp.concatenate([pieces[:, :1], longest[:, None], pieces[:, 1:], final[:, None]], axis=1)
    return table.astype(jnp.int32)


def levels(key, extent, cuts, least, largest):
    loudness = 1.0
    for axis_at, blocks in cuts:
        steps = jax.random.uniform(jax.random.fold_in(jax.random.fold_in(key, 6), axis_at), (blocks,), jnp.float32, least / len(cuts), largest / len(cuts))
        loudness = loudness * jnp.repeat(jnp.exp(steps), extent[axis_at] // blocks).reshape((-1,) + (1,) * (len(extent) - 1 - axis_at))
    return loudness


def scatter_about(key, extent, deviation, limit, cuts=(), kind=jnp.bfloat16):
    result = deviation * jax.random.normal(key, extent, jnp.float32)
    if cuts:
        result = result * levels(key, extent, cuts, -0.22, 0.18)
    return jnp.clip(result, -limit, limit).astype(kind)


def setup_inputs(seed: int = 0) -> dict:
    streams_of = jax.random.split(jax.random.key(seed), 14)
    tokens = scatter_about(streams_of[0], (TOKENS, D), 1.0, 6.0, ((0, 32),))
    lengths = draw_lengths(jax.random.fold_in(streams_of[13], 71), 0)
    ln1_gain = jnp.clip(1.0 + 0.1 * jax.random.normal(streams_of[2], (D,), jnp.float32), 0.5, 1.5)
    ln1_bias = scatter_about(streams_of[3], (D,), 0.5, 3.0, (), jnp.float32)
    w_qkv = scatter_about(streams_of[4], (D, 3 * D), D ** -0.5, 0.21875)
    q_gain = jnp.clip(1.0 + 0.1 * jax.random.normal(streams_of[5], (D,), jnp.float32), 0.5, 1.5)
    k_gain = jnp.clip(1.0 + 0.1 * jax.random.normal(streams_of[6], (D,), jnp.float32), 0.5, 1.5)
    w_out = scatter_about(streams_of[7], (D, D), (max(1, 2 * D // GROUP)) ** -0.5, 6.0)
    ln2_gain = jnp.clip(1.0 + 0.1 * jax.random.normal(streams_of[8], (D,), jnp.float32), 0.5, 1.5)
    ln2_bias = scatter_about(streams_of[9], (D,), 0.5, 3.0, (), jnp.float32)
    w_up = scatter_about(streams_of[10], (D, FF), D ** -0.5, 0.21875)
    w_down = scatter_about(streams_of[11], (FF, D), FF ** -0.5, 0.109375)
    cotangent = scatter_about(streams_of[12], (TOKENS, D), 1.0, 6.0, ((0, 32),))
    return {"tokens": tokens, "lengths": lengths, "ln1_gain": ln1_gain, "ln1_bias": ln1_bias, "w_qkv": w_qkv, "q_gain": q_gain, "k_gain": k_gain, "w_out": w_out, "ln2_gain": ln2_gain, "ln2_bias": ln2_bias, "w_up": w_up, "w_down": w_down, "cotangent": cotangent}


@jax.custom_vjp
def low(v):
    return lax.optimization_barrier(v.astype(jnp.bfloat16)).astype(jnp.float32)

@jax.custom_vjp
def low_back(v):
    return v

def low_keep(v):
    return (low(v), None)

def low_pass(kept, grad):
    return (grad,)

def back_keep(v):
    return (v, None)

def back_low(kept, grad):
    return (low(grad),)
low.defvjp(low_keep, low_pass)
low_back.defvjp(back_keep, back_low)
EPS = 1e-06
MASKED = -1e+30
HIGH = lax.Precision.HIGHEST

def layer_norm(value, gain, shift):
    mean = lax.optimization_barrier(jnp.mean(value, axis=-1, keepdims=True))
    centred = value - mean
    spread = lax.optimization_barrier(jnp.mean(centred * centred, axis=-1, keepdims=True))
    return centred * lax.rsqrt(spread + EPS) * gain + shift

def head_norm(value, gain):
    mean = lax.optimization_barrier(jnp.mean(value, axis=-1, keepdims=True))
    centred = value - mean
    spread = lax.optimization_barrier(jnp.mean(centred * centred, axis=-1, keepdims=True))
    return centred * lax.rsqrt(spread + EPS) * gain.reshape(value.shape[1], value.shape[2])

def segment_ids(lengths_row, count):
    ends = jnp.cumsum(lengths_row).astype(jnp.int32)
    places = jnp.arange(count, dtype=jnp.int32)
    return lax.optimization_barrier(jnp.sum((places[:, None] >= ends[None, :]).astype(jnp.int32), axis=1)).astype(jnp.int32)

def attend_block(q_blk, seg_blk, keys, values, seg_all):
    raw = jnp.einsum('qhd,khd->hqk', q_blk, keys, precision=HIGH) * (1.0 / math.sqrt(HD))
    raw = low_back(raw)
    same = seg_blk[:, None] == seg_all[None, :]
    masked = jnp.where(same[None], raw, MASKED)
    top = lax.optimization_barrier(jnp.max(masked, axis=-1, keepdims=True))
    weights = jnp.exp(masked - top)
    total = lax.optimization_barrier(jnp.sum(weights, axis=-1, keepdims=True))
    mixed = jnp.einsum('hqk,khd->hqd', low(weights), values, precision=HIGH) / total
    return jnp.transpose(mixed, (1, 0, 2))

def group_forward(x, seg, params):
    ln1_gain, ln1_bias, w_qkv, q_gain, k_gain, w_out, ln2_gain, ln2_bias, w_up, w_down = params
    h = low(layer_norm(x, ln1_gain, ln1_bias))
    qkv = low_back(jnp.dot(h, w_qkv, precision=HIGH))
    queries = low(head_norm(qkv[:, :D].reshape(GROUP, H, HD), q_gain))
    keys = low(head_norm(qkv[:, D:2 * D].reshape(GROUP, H, HD), k_gain))
    values = low(qkv[:, 2 * D:].reshape(GROUP, H, HD))
    size = math.gcd(GROUP, 512)
    attend = jax.checkpoint(attend_block)
    mixed = lax.map(lambda item: attend(item[0], item[1], keys, values, seg), (queries.reshape(GROUP // size, size, H, HD), seg.reshape(GROUP // size, size)))
    mixed = low(low_back(mixed.reshape(GROUP, D)))
    x1 = x + low_back(jnp.dot(mixed, w_out, precision=HIGH))
    h2 = low(layer_norm(x1, ln2_gain, ln2_bias))
    up = low_back(jnp.dot(h2, w_up, precision=HIGH))
    act = low(jax.nn.gelu(up))
    return x1 + jnp.dot(act, w_down, precision=HIGH)

def reference(tokens, lengths, ln1_gain, ln1_bias, w_qkv, q_gain, k_gain, w_out, ln2_gain, ln2_bias, w_up, w_down, cotangent):
    params = (ln1_gain, ln1_bias, w_qkv.astype(jnp.float32), q_gain, k_gain, w_out.astype(jnp.float32), ln2_gain, ln2_bias, w_up.astype(jnp.float32), w_down.astype(jnp.float32))
    seg = jax.vmap(lambda row: segment_ids(row, GROUP))(lengths)

    def forward(weights, x):

        def step(carry, item):
            return (carry, jax.checkpoint(group_forward)(item[0], item[1], weights))
        _, out = lax.scan(step, jnp.zeros((), jnp.float32), (x.reshape(GROUPS, GROUP, D), seg))
        return out.reshape(TOKENS, D)
    output, pullback = jax.vjp(forward, params, tokens.astype(jnp.float32))
    grads, grad_x = pullback(cotangent.astype(jnp.float32))
    g_ln1_gain, g_ln1_bias, g_w_qkv, g_q_gain, g_k_gain, g_w_out, g_ln2_gain, g_ln2_bias, g_w_up, g_w_down = grads
    return (output.astype(jnp.bfloat16), grad_x.astype(jnp.bfloat16), g_ln1_gain, g_ln1_bias, g_w_qkv, g_q_gain, g_k_gain, g_w_out, g_ln2_gain, g_ln2_bias, g_w_up, g_w_down)
```

```python
import functools
import math

import jax
import jax.numpy as jnp
from jax import lax
from jax.experimental import pallas as pl
from jax.experimental.pallas import tpu as pltpu
from jax.sharding import PartitionSpec as P

H = 12
HD = 64
EPS = 1e-06
AXES = ("wide", "blk")
AUG = 16
BLOCKED = -512.0
LOG2E = math.log2(math.e)
NN = (((1,), (0,)), ((), ()))
NT = (((1,), (1,)), ((), ()))
TN = (((0,), (0,)), ((), ()))
TT = (((0,), (1,)), ((), ()))
BF16 = jnp.bfloat16
F32 = jnp.float32
VMEM_LIMIT = 56 * 2**20


def mul(left, right, dims, kind=F32):
    return lax.dot_general(left, right, dims, preferred_element_type=F32).astype(kind)


def forward_kernel(bk, first, *refs):
    if first:
        q_ref, k_ref, v_ref, mq_ref, mk_ref, ones_ref, acc_ref, e_ref = refs
    else:
        q_ref, k_ref, v_ref, mq_ref, mk_ref, ones_ref, had_ref, e_ref, o_ref, linv_ref = refs
    keys = k_ref.shape[2]
    q = jnp.concatenate([q_ref[0], mq_ref[...]], axis=0)
    acc = None if first else had_ref[0]
    for i in range(keys // bk):
        cut = slice(i * bk, (i + 1) * bk)
        k = jnp.concatenate([k_ref[0, :, cut], mk_ref[:, cut]], axis=0)
        v = jnp.concatenate([v_ref[0, :, cut], ones_ref[:, cut]], axis=0)
        e = jnp.exp2(mul(k, q, TN)).astype(BF16)
        e_ref[0, cut, :] = e
        part = mul(v, e, NN)
        acc = part if acc is None else acc + part
    if first:
        acc_ref[0] = acc
    else:
        linv = 1.0 / acc[HD : HD + 1]
        o_ref[0] = (acc[:HD] * linv).astype(BF16)
        linv_ref[0] = jnp.broadcast_to(linv, linv_ref.shape[1:])


def head_block(*tail):
    return pl.BlockSpec((1,) + tail, lambda h: (h,) + (0,) * len(tail))


def whole_block(shape):
    return pl.BlockSpec(shape, lambda h: (0,) * len(shape))


def key_block(keys):
    return math.gcd(keys, 512)


def attend(q, k, v, mask_q, mask_k, ones, had=None):
    heads, _, rows = q.shape
    keys = k.shape[2]
    first = had is None
    ins = [q, k, v, mask_q, mask_k, ones]
    specs = [head_block(HD, rows), head_block(HD, keys), head_block(HD, keys)]
    specs += [whole_block(a.shape) for a in (mask_q, mask_k, ones)]
    e_shape = jax.ShapeDtypeStruct((heads, keys, rows), BF16)
    e_spec = head_block(keys, rows)
    if first:
        outs = [jax.ShapeDtypeStruct((heads, HD + AUG, rows), F32), e_shape]
        out_specs = [head_block(HD + AUG, rows), e_spec]
    else:
        ins.append(had)
        specs.append(head_block(HD + AUG, rows))
        outs = [
            e_shape,
            jax.ShapeDtypeStruct((heads, HD, rows), BF16),
            jax.ShapeDtypeStruct((heads, 8, rows), F32),
        ]
        out_specs = [e_spec, head_block(HD, rows), head_block(8, rows)]
    return pl.pallas_call(
        functools.partial(forward_kernel, key_block(keys), first),
        grid=(heads,),
        in_specs=specs,
        out_specs=out_specs,
        out_shape=outs,
        compiler_params=pltpu.CompilerParams(vmem_limit_bytes=VMEM_LIMIT),
        cost_estimate=pl.CostEstimate(
            flops=heads * rows * keys * 1024,
            bytes_accessed=heads * rows * keys * 2,
            transcendentals=heads * rows * keys,
        ),
        name="attend_first" if first else "attend_last",
    )(*ins)


def backward_kernel(bk, first, *refs):
    if first:
        e_ref, do_ref, o_ref, linv_ref, q_ref, k_ref, v_ref, ones_ref, dq_ref, dk_ref, dv_ref = refs
    else:
        e_ref, do_ref, o_ref, linv_ref, q_ref, k_ref, v_ref, ones_ref, had_ref, dq_ref, dk_ref, dv_ref = refs
    keys = k_ref.shape[2]
    low = (do_ref[0] * linv_ref[0, :1]).astype(BF16)
    delta = -jnp.sum(low.astype(F32) * o_ref[0].astype(F32), axis=0, keepdims=True)
    top = delta.astype(BF16).astype(F32)
    row = lax.broadcasted_iota(jnp.int32, (AUG, delta.shape[1]), 0)
    extra = jnp.where(row == 0, top, jnp.where(row == 1, delta - top, 0.0)).astype(BF16)
    do = jnp.concatenate([low, extra], axis=0)
    q = q_ref[0]
    acc = None if first else had_ref[0]
    for i in range(keys // bk):
        cut = slice(i * bk, (i + 1) * bk)
        k = k_ref[0, :, cut]
        v = jnp.concatenate([v_ref[0, :, cut], ones_ref[:, cut]], axis=0)
        e = e_ref[0, cut, :]
        ds = (e.astype(F32) * mul(v, do, TN)).astype(BF16)
        part = mul(k, ds, NN)
        acc = part if acc is None else acc + part
        dk_ref[0, :, cut] = mul(q, ds, NT).astype(dk_ref.dtype)
        dv_ref[0, :, cut] = mul(low, e, NT).astype(dv_ref.dtype)
    dq_ref[0] = acc


def attend_back(e, do, o, linv, q, k, v, ones, start, heads, kind, had=None):
    _, keys, rows = e.shape
    first = had is None

    def block(*tail):
        return pl.BlockSpec((1,) + tail, lambda h: (h + start,) + (0,) * len(tail))

    ins = [e, do, o, linv, q, k, v, ones]
    specs = [block(keys, rows), block(HD, rows), block(HD, rows), block(8, rows), block(HD, rows)]
    specs += [block(HD, keys), block(HD, keys), whole_block(ones.shape)]
    if not first:
        ins.append(had)
        specs.append(head_block(HD, rows))
    return pl.pallas_call(
        functools.partial(backward_kernel, key_block(keys), first),
        grid=(heads,),
        in_specs=specs,
        out_specs=[head_block(HD, rows), head_block(HD, keys), head_block(HD, keys)],
        out_shape=[
            jax.ShapeDtypeStruct((heads, HD, rows), F32),
            jax.ShapeDtypeStruct((heads, HD, keys), kind),
            jax.ShapeDtypeStruct((heads, HD, keys), kind),
        ],
        compiler_params=pltpu.CompilerParams(vmem_limit_bytes=VMEM_LIMIT),
        cost_estimate=pl.CostEstimate(
            flops=heads * rows * keys * 2300,
            bytes_accessed=heads * rows * keys * 2,
            transcendentals=0,
        ),
        name="attend_back_first" if first else "attend_back_last",
    )(*ins)


def norm(value, axis):
    mean = jnp.mean(value, axis=axis, keepdims=True)
    centred = value - mean
    scale = lax.rsqrt(jnp.mean(centred * centred, axis=axis, keepdims=True) + EPS)
    return centred * scale, scale


def norm_back(grad, unit, scale, axis):
    mean = jnp.mean(grad, axis=axis, keepdims=True)
    along = jnp.mean(grad * unit, axis=axis, keepdims=True)
    return scale * (grad - mean - unit * along)


def gelu_parts(u):
    root = math.sqrt(2.0 / math.pi)
    square = u * u
    t = jnp.tanh(root * (u + 0.044715 * u * square))
    value = 0.5 * u * (1.0 + t)
    slope = 0.5 * (1.0 + t) + 0.5 * u * (1.0 - t * t) * root * (1.0 + 3 * 0.044715 * square)
    return value, slope


def place(index):
    return index // 8, index // 4 % 2, index // 2 % 2, index % 2


def device(z, x, core, y):
    return ((z * 2 + x) * 2 + core) * 2 + y


def pairs(other):
    return [(i, device(*other(*place(i)))) for i in range(32)]


SWAP = pairs(lambda z, x, c, y: (z, x, y, c))
ACROSS = {
    "c": pairs(lambda z, x, c, y: (z, x, 1 - c, y)),
    "x": pairs(lambda z, x, c, y: (z, 1 - x, c, y)),
    "y": pairs(lambda z, x, c, y: (z, x, c, 1 - y)),
    "l": pairs(lambda z, x, c, y: (z // 2 * 2 + 1 - z % 2, x, c, y)),
    "h": pairs(lambda z, x, c, y: (3 - (z // 2 * 2 + 1 - z % 2), x, c, y)),
}
ACROSS["h"] = pairs(lambda z, x, c, y: ((z + 2) % 4, x, c, y))


def summed(piece, order, at):
    names = ["h", "l", "x", "c", "y"]
    shape = piece.shape
    part = piece.reshape((2,) * 5 + (shape[0] // 32,) + shape[1:])
    for step, name in enumerate(order):
        axis = names.index(name)
        names.pop(axis)
        give = lax.dynamic_index_in_dim(part, 1 - at[name], axis, keepdims=False)
        keep = lax.dynamic_index_in_dim(part, at[name], axis, keepdims=False)
        came = lax.ppermute(give, AXES, ACROSS[name])
        part = keep.astype(F32) + came.astype(F32)
        if step < 4:
            part = part.astype(BF16)
    return part


def shards(
    tokens,
    lengths,
    ln1_gain,
    ln1_bias,
    w_qkv,
    q_gain,
    k_gain,
    w_out,
    ln2_gain,
    ln2_bias,
    w_up,
    w_down,
    cotangent,
):
    rows, width = tokens.shape
    parts = lax.axis_size("blk")
    known = parts == 2 and lax.axis_size("wide") == 16
    group = rows * parts
    if known:
        wide = lax.axis_index("wide")
        at = {
            "h": wide // 8,
            "l": wide // 4 % 2,
            "x": wide // 2 % 2,
            "c": wide % 2,
            "y": lax.axis_index("blk"),
        }
        lengths = lax.ppermute(lengths, AXES, SWAP)
        tokens = lax.ppermute(tokens, AXES, SWAP)
        cotangent = lax.ppermute(cotangent, AXES, SWAP)
        mine = at["c"]
    else:
        mine = lax.axis_index("blk")

    count = lengths.shape[1]
    place_of = jnp.arange(count)
    ends = jnp.sum(jnp.where(place_of[:, None] <= place_of[None, :], lengths[0][:, None], 0), axis=0)
    spots = jnp.arange(group, dtype=jnp.int32)
    segment = jnp.sum((spots[None, :] >= ends[:, None]).astype(jnp.int32), axis=0)
    is_in = jnp.arange(AUG)[:, None] == segment[None, :]
    mask_k = is_in.astype(BF16)
    mask_q = jnp.where(is_in, 0.0, BLOCKED).astype(BF16)
    mask_q = lax.dynamic_slice_in_dim(mask_q, mine * rows, rows, axis=1)
    ones = jnp.broadcast_to((jnp.arange(AUG) < 2)[:, None], (AUG, group)).astype(BF16)

    x = tokens.astype(F32)
    unit1, scale1 = norm(x, -1)
    h = (unit1 * ln1_gain + ln1_bias).astype(BF16)
    qkv = mul(w_qkv, h, TT).reshape(3, H, HD, rows)
    gain_q = q_gain.reshape(H, HD, 1)
    gain_k = k_gain.reshape(H, HD, 1)
    unit_k, scale_k = norm(qkv[1], 1)
    k = (unit_k * gain_k).astype(BF16)
    v = qkv[2].astype(BF16)
    unit_q, scale_q = norm(qkv[0], 1)
    q = (unit_q * (gain_q * (LOG2E / math.sqrt(HD)))).astype(BF16)
    if known:
        theirs = lax.ppermute(jnp.stack([k, v]), AXES, ACROSS["c"])
        k_far, v_far = theirs[0], theirs[1]
        mask_near = lax.dynamic_slice_in_dim(mask_k, mine * rows, rows, axis=1)
        mask_far = lax.dynamic_slice_in_dim(mask_k, (1 - mine) * rows, rows, axis=1)
        ones_half = ones[:, :rows]
        had, e_near = attend(q, k, v, mask_q, mask_near, ones_half)
        e_far, o, linv = attend(q, k_far, v_far, mask_q, mask_far, ones_half, had)
    else:
        k_all = lax.all_gather(k, "blk", axis=2, tiled=True)
        v_all = lax.all_gather(v, "blk", axis=2, tiled=True)
        had, e_all = attend(q, k_all, v_all, mask_q, mask_k, ones)
        linv = jnp.broadcast_to(1.0 / had[:, HD : HD + 1], (H, 8, rows))
        o = (had[:, :HD] * linv[:, :1]).astype(BF16)
    o_flat = o.reshape(width, rows)
    x1 = x + mul(o_flat, w_out, TN)
    unit2, scale2 = norm(x1, -1)
    h2 = (unit2 * ln2_gain + ln2_bias).astype(BF16)
    up = mul(h2, w_up, NN)
    act, slope = gelu_parts(up)
    act = act.astype(BF16)
    output = (x1 + mul(act, w_down, NN)).astype(BF16)
    if known:
        output = lax.ppermute(output, AXES, SWAP)

    grad_w_down = mul(act, cotangent, TN, BF16 if known else F32)
    d_up = (mul(cotangent, w_down, NT) * slope).astype(BF16)
    grad_w_up = mul(h2, d_up, TN, BF16 if known else F32)
    d_h2 = mul(d_up, w_up, NT)
    grad_ln2_gain = jnp.sum(d_h2 * unit2, axis=0)
    grad_ln2_bias = jnp.sum(d_h2, axis=0)
    d_x1 = cotangent.astype(F32) + norm_back(d_h2 * ln2_gain, unit2, scale2, -1)
    d_branch = d_x1.astype(BF16)
    grad_w_out = mul(o_flat, d_branch, NN, BF16 if known else F32)
    d_o = mul(w_out, d_branch, NT).reshape(H, HD, rows)

    if known:
        sum_w_down = summed(grad_w_down, "cxlhy", at)
        sum_w_up = summed(grad_w_up, "cxlhy", at)
        sum_w_out = summed(grad_w_out, "cyxlh", at)

    def back(start, heads):
        if known:
            d_q, give_k, give_v = attend_back(
                e_far, d_o, o, linv, q, k_far, v_far, ones_half, start, heads, BF16
            )
            came = lax.ppermute(jnp.stack([give_k, give_v]), AXES, ACROSS["c"]).astype(F32)
            d_q, d_k, d_v = attend_back(
                e_near, d_o, o, linv, q, k, v, ones_half, start, heads, F32, d_q
            )
            d_k, d_v = d_k + came[0], d_v + came[1]
        else:
            d_q, d_k, d_v = attend_back(
                e_all, d_o, o, linv, q, k_all, v_all, ones, start, heads, F32
            )
            pair = jnp.stack([d_k, d_v]).reshape(2, heads, HD, parts, rows)
            pair = jnp.transpose(pair, (3, 0, 1, 2, 4)).astype(BF16)
            pair = lax.psum_scatter(pair, "blk", scatter_dimension=0, tiled=False)
            d_k, d_v = pair[0].astype(F32), pair[1].astype(F32)
        return d_q, d_k, d_v

    def back_norms(start, heads, d_q, d_k, d_v):
        cut = slice(start, start + heads)
        d_q = d_q * (1.0 / math.sqrt(HD))
        d_k = d_k * (1.0 / LOG2E)
        g_q = jnp.sum(d_q * unit_q[cut], axis=2)
        g_k = jnp.sum(d_k * unit_k[cut], axis=2)
        d_q = norm_back(d_q * gain_q[cut], unit_q[cut], scale_q[cut], 1)
        d_k = norm_back(d_k * gain_k[cut], unit_k[cut], scale_k[cut], 1)
        return jnp.stack([d_q, d_k, d_v]).astype(BF16), g_q, g_k

    if known:
        half = H // 2
        first = back_norms(0, half, *back(0, half))
        second = back_norms(half, half, *back(half, half))
        d_qkv = jnp.concatenate([first[0], second[0]], axis=1).reshape(3 * width, rows)
        grad_q_gain = jnp.concatenate([first[1], second[1]]).reshape(width)
        grad_k_gain = jnp.concatenate([first[2], second[2]]).reshape(width)
        half_a = mul(h, first[0].reshape(3 * width // 2, rows), TT, BF16)
        half_b = mul(h, second[0].reshape(3 * width // 2, rows), TT, BF16)
    else:
        d_qkv, grad_q_gain, grad_k_gain = back_norms(0, H, *back(0, H))
        d_qkv = d_qkv.reshape(3 * width, rows)
        grad_q_gain, grad_k_gain = grad_q_gain.reshape(width), grad_k_gain.reshape(width)
        grad_w_qkv = mul(h, d_qkv, TT)
    d_h = mul(d_qkv, w_qkv, TT)
    grad_ln1_gain = jnp.sum(d_h * unit1, axis=0)
    grad_ln1_bias = jnp.sum(d_h, axis=0)
    grad_tokens = (d_x1 + norm_back(d_h * ln1_gain, unit1, scale1, -1)).astype(BF16)
    vectors = [grad_ln1_gain, grad_ln1_bias, grad_q_gain, grad_k_gain, grad_ln2_gain, grad_ln2_bias]
    if known:
        grad_tokens = lax.ppermute(grad_tokens, AXES, SWAP)
        sum_a = summed(half_a, "cxylh", at)
        table = jnp.pad(jnp.stack(vectors, axis=1), ((0, 0), (0, 128 - len(vectors))))
        sum_b = summed(jnp.concatenate([half_b, table.astype(BF16)], axis=1), "cyxlh", at)
        sums = [sum_b[:, 3 * width // 2 + i] for i in range(len(vectors))]
        sum_a = sum_a.reshape(-1, 3, width // 2)
        sum_b = sum_b[:, : 3 * width // 2].reshape(-1, 3, width // 2)
        sum_w_qkv = jnp.concatenate([sum_a, sum_b], axis=2).reshape(-1, 3 * width)
    else:
        scatter = functools.partial(
            lax.psum_scatter, axis_name=AXES, scatter_dimension=0, tiled=True
        )
        sum_w_down, sum_w_up = scatter(grad_w_down), scatter(grad_w_up)
        sum_w_out, sum_w_qkv = scatter(grad_w_out), scatter(grad_w_qkv)
        sums = [scatter(g) for g in vectors]
    return (
        output,
        grad_tokens,
        sums[0],
        sums[1],
        sum_w_qkv,
        sums[2],
        sums[3],
        sum_w_out,
        sums[4],
        sums[5],
        sum_w_up,
        sum_w_down,
    )


def solution(mesh):
    split = P(AXES, None)
    in_specs = (split, P("wide", None)) + (P(),) * 10 + (split,)
    vector = P(AXES)
    out_specs = (
        split,
        split,
        vector,
        vector,
        split,
        vector,
        vector,
        split,
        vector,
        vector,
        split,
        split,
    )
    return jax.shard_map(shards, mesh=mesh, in_specs=in_specs, out_specs=out_specs, check_vma=False)
```

```python
import functools
import math

import jax
import jax.numpy as jnp
from jax import lax
from jax.experimental import pallas as pl
from jax.experimental.pallas import tpu as pltpu
from jax.sharding import PartitionSpec as P

H = 12
HD = 64
EPS = 1e-06
AXES = ("wide", "blk")
AUG = 16
BLOCKED = -512.0
LOG2E = math.log2(math.e)
NN = (((1,), (0,)), ((), ()))
NT = (((1,), (1,)), ((), ()))
TN = (((0,), (0,)), ((), ()))
TT = (((0,), (1,)), ((), ()))
BF16 = jnp.bfloat16
MESH = pl.DeviceIdType.MESH
F32 = jnp.float32
VMEM_LIMIT = 56 * 2**20


def mul(left, right, dims, kind=F32):
    return lax.dot_general(left, right, dims, preferred_element_type=F32).astype(kind)


def forward_kernel(bk, first, *refs):
    if first:
        q_ref, k_ref, v_ref, mq_ref, mk_ref, ones_ref, acc_ref, e_ref = refs
    else:
        q_ref, k_ref, v_ref, mq_ref, mk_ref, ones_ref, had_ref, e_ref, o_ref, linv_ref = refs
    keys = k_ref.shape[2]
    q = jnp.concatenate([q_ref[0], mq_ref[...]], axis=0)
    acc = None if first else had_ref[0]
    for i in range(keys // bk):
        cut = slice(i * bk, (i + 1) * bk)
        k = jnp.concatenate([k_ref[0, :, cut], mk_ref[:, cut]], axis=0)
        v = jnp.concatenate([v_ref[0, :, cut], ones_ref[:, cut]], axis=0)
        e = jnp.exp2(mul(k, q, TN)).astype(BF16)
        e_ref[0, cut, :] = e
        part = mul(v, e, NN)
        acc = part if acc is None else acc + part
    if first:
        acc_ref[0] = acc
    else:
        linv = 1.0 / acc[HD : HD + 1]
        o_ref[0] = (acc[:HD] * linv).astype(BF16)
        linv_ref[0] = jnp.broadcast_to(linv, linv_ref.shape[1:])


def head_block(*tail):
    return pl.BlockSpec((1,) + tail, lambda h: (h,) + (0,) * len(tail))


def whole_block(shape):
    return pl.BlockSpec(shape, lambda h: (0,) * len(shape))


def key_block(keys):
    return math.gcd(keys, 512)


def attend(q, k, v, mask_q, mask_k, ones, had=None):
    heads, _, rows = q.shape
    keys = k.shape[2]
    first = had is None
    ins = [q, k, v, mask_q, mask_k, ones]
    specs = [head_block(HD, rows), head_block(HD, keys), head_block(HD, keys)]
    specs += [whole_block(a.shape) for a in (mask_q, mask_k, ones)]
    e_shape = jax.ShapeDtypeStruct((heads, keys, rows), BF16)
    e_spec = head_block(keys, rows)
    if first:
        outs = [jax.ShapeDtypeStruct((heads, HD + AUG, rows), F32), e_shape]
        out_specs = [head_block(HD + AUG, rows), e_spec]
    else:
        ins.append(had)
        specs.append(head_block(HD + AUG, rows))
        outs = [
            e_shape,
            jax.ShapeDtypeStruct((heads, HD, rows), BF16),
            jax.ShapeDtypeStruct((heads, 8, rows), F32),
        ]
        out_specs = [e_spec, head_block(HD, rows), head_block(8, rows)]
    return pl.pallas_call(
        functools.partial(forward_kernel, key_block(keys), first),
        grid=(heads,),
        in_specs=specs,
        out_specs=out_specs,
        out_shape=outs,
        compiler_params=pltpu.CompilerParams(vmem_limit_bytes=VMEM_LIMIT),
        cost_estimate=pl.CostEstimate(
            flops=heads * rows * keys * 1024,
            bytes_accessed=heads * rows * keys * 2,
            transcendentals=heads * rows * keys,
        ),
        name="attend_first" if first else "attend_last",
    )(*ins)


def backward_kernel(bk, first, *refs):
    if first:
        e_ref, do_ref, o_ref, linv_ref, q_ref, k_ref, v_ref, ones_ref, dq_ref, dk_ref, dv_ref = refs
    else:
        e_ref, do_ref, o_ref, linv_ref, q_ref, k_ref, v_ref, ones_ref, had_ref, dq_ref, dk_ref, dv_ref = refs
    keys = k_ref.shape[2]
    low = (do_ref[0] * linv_ref[0, :1]).astype(BF16)
    delta = -jnp.sum(low.astype(F32) * o_ref[0].astype(F32), axis=0, keepdims=True)
    top = delta.astype(BF16).astype(F32)
    row = lax.broadcasted_iota(jnp.int32, (AUG, delta.shape[1]), 0)
    extra = jnp.where(row == 0, top, jnp.where(row == 1, delta - top, 0.0)).astype(BF16)
    do = jnp.concatenate([low, extra], axis=0)
    q = q_ref[0]
    acc = None if first else had_ref[0]
    for i in range(keys // bk):
        cut = slice(i * bk, (i + 1) * bk)
        k = k_ref[0, :, cut]
        v = jnp.concatenate([v_ref[0, :, cut], ones_ref[:, cut]], axis=0)
        e = e_ref[0, cut, :]
        ds = (e.astype(F32) * mul(v, do, TN)).astype(BF16)
        part = mul(k, ds, NN)
        acc = part if acc is None else acc + part
        dk_ref[0, :, cut] = mul(q, ds, NT).astype(dk_ref.dtype)
        dv_ref[0, :, cut] = mul(low, e, NT).astype(dv_ref.dtype)
    dq_ref[0] = acc


def attend_back(e, do, o, linv, q, k, v, ones, start, heads, kind, had=None):
    _, keys, rows = e.shape
    first = had is None

    def block(*tail):
        return pl.BlockSpec((1,) + tail, lambda h: (h + start,) + (0,) * len(tail))

    ins = [e, do, o, linv, q, k, v, ones]
    specs = [block(keys, rows), block(HD, rows), block(HD, rows), block(8, rows), block(HD, rows)]
    specs += [block(HD, keys), block(HD, keys), whole_block(ones.shape)]
    if not first:
        ins.append(had)
        specs.append(head_block(HD, rows))
    return pl.pallas_call(
        functools.partial(backward_kernel, key_block(keys), first),
        grid=(heads,),
        in_specs=specs,
        out_specs=[head_block(HD, rows), head_block(HD, keys), head_block(HD, keys)],
        out_shape=[
            jax.ShapeDtypeStruct((heads, HD, rows), F32),
            jax.ShapeDtypeStruct((heads, HD, keys), kind),
            jax.ShapeDtypeStruct((heads, HD, keys), kind),
        ],
        compiler_params=pltpu.CompilerParams(vmem_limit_bytes=VMEM_LIMIT),
        cost_estimate=pl.CostEstimate(
            flops=heads * rows * keys * 2300,
            bytes_accessed=heads * rows * keys * 2,
            transcendentals=0,
        ),
        name="attend_back_first" if first else "attend_back_last",
    )(*ins)


def norm(value, axis):
    mean = jnp.mean(value, axis=axis, keepdims=True)
    centred = value - mean
    scale = lax.rsqrt(jnp.mean(centred * centred, axis=axis, keepdims=True) + EPS)
    return centred * scale, scale


def norm_back(grad, unit, scale, axis):
    mean = jnp.mean(grad, axis=axis, keepdims=True)
    along = jnp.mean(grad * unit, axis=axis, keepdims=True)
    return scale * (grad - mean - unit * along)


def gelu_parts(u):
    root = math.sqrt(2.0 / math.pi)
    square = u * u
    t = jnp.tanh(u * (root + (root * 0.044715) * square))
    half = 0.5 + 0.5 * t
    slope = half + (u * (0.5 - 0.5 * t * t)) * (root + (3 * root * 0.044715) * square)
    return u * half, slope


def params(**more):
    return pltpu.CompilerParams(vmem_limit_bytes=VMEM_LIMIT, **more)


def fixed(shape):
    return pl.BlockSpec(shape, lambda *_: (0,) * len(shape))


SCALAR = pl.BlockSpec(memory_space=pltpu.SMEM)


def pre_kernel(swapped, *refs):
    if swapped:
        flag_ref, here_ref, came_ref, *refs = refs
        x_low = jnp.where(flag_ref[0] == 1, came_ref[...], here_ref[...])
        *refs, x_ref = refs
        x_ref[...] = x_low
    else:
        here_ref, *refs = refs
        x_low = here_ref[...]
    gain_ref, bias_ref, w_ref, gq_ref, gk_ref, h_ref, q_ref, k_ref, v_ref, scale_ref = refs
    rows, width = x_low.shape
    unit, _ = norm(x_low.astype(F32), -1)
    h = (unit * gain_ref[...] + bias_ref[...]).astype(BF16)
    h_ref[...] = h.T

    def heads(part):
        value = mul(w_ref[part * width : (part + 1) * width, :], h, NT)
        return value.reshape(width // HD, HD, rows)

    unit_k, scale_k = norm(heads(1), 1)
    k_ref[...] = (unit_k * gk_ref[...]).astype(BF16)
    scale_ref[1] = scale_k
    v_ref[...] = heads(2).astype(BF16)
    unit_q, scale_q = norm(heads(0), 1)
    q_ref[...] = (unit_q * gq_ref[...]).astype(BF16)
    scale_ref[0] = scale_q


def project(tokens, gain, bias, w_t, gain_q, gain_k, flag=None, came=None):
    rows, width = tokens.shape
    block = math.gcd(rows, 256)
    row = pl.BlockSpec((block, width), lambda i: (i, 0))
    head = pl.BlockSpec((H, HD, block), lambda i: (0, 0, i))
    swapped = flag is not None
    ins = ([flag, tokens, came] if swapped else [tokens]) + [gain, bias, w_t, gain_q, gain_k]
    specs = ([SCALAR, row, row] if swapped else [row]) + [fixed(a.shape) for a in ins[-5:]]
    head_shape = jax.ShapeDtypeStruct((H, HD, rows), BF16)
    outs = [jax.ShapeDtypeStruct((width, rows), BF16), head_shape, head_shape, head_shape]
    outs.append(jax.ShapeDtypeStruct((2, H, 1, rows), F32))
    out_specs = [pl.BlockSpec((width, block), lambda i: (0, i)), head, head, head]
    out_specs.append(pl.BlockSpec((2, H, 1, block), lambda i: (0, 0, 0, i)))
    if swapped:
        outs.append(jax.ShapeDtypeStruct((rows, width), BF16))
        out_specs.append(row)
    return pl.pallas_call(
        functools.partial(pre_kernel, swapped),
        grid=(rows // block,),
        in_specs=specs,
        out_specs=out_specs,
        out_shape=outs,
        compiler_params=params(),
        cost_estimate=pl.CostEstimate(
            flops=2 * rows * w_t.size, bytes_accessed=12 * rows * width, transcendentals=0
        ),
        name="project",
    )(*ins)


def fold(value):
    if value.shape[-2] % 16 == 0:
        return value
    half = value.shape[-1] // 2
    low = value[..., 16:, :]
    low = jnp.concatenate([low[..., :half], low[..., half:]], axis=-2)
    return jnp.concatenate([value[..., :16, :], low], axis=-1)


def unfold(out_ref, value, start=0):
    count = value.shape[-1] * 2 // 3
    half = count // 2
    out_ref[:16, start : start + count] = value[:, :count]
    out_ref[16:, start : start + half] = value[:8, count:]
    out_ref[16:, start + half : start + count] = value[8:, count:]


def spread(value, core, keep_ref, give_ref, lead):
    rows, columns = value.shape
    value = value.reshape((lead, 2, 2, rows // (4 * lead), columns))
    mine = core == 0
    shape = keep_ref.shape
    keep = jnp.where(mine, value[:, 0], value[:, 1])
    give = jnp.where(mine, value[:, 1], value[:, 0])
    keep_ref[...] = fold(keep).astype(BF16).reshape(shape)
    give_ref[...] = fold(give).astype(BF16).reshape(shape)


def middle_kernel(split, *refs):
    if split:
        core_ref, *refs = refs
        core = core_ref[0]
    x_ref, o_ref, dy_ref, w_out_ref, gain_ref, bias_ref, w_up_ref, w_down_ref, *refs = refs
    out_ref, dx1_ref, do_ref, dgain_ref, dbias_ref, *refs = refs
    grads, refs = (refs[:6], refs[6:]) if split else (refs[:3], refs[3:])
    x1_ref, h2_ref, h2t_ref, acc_ref, dh2_ref, g_ref, du_ref, da_ref = refs
    step = pl.program_id(0)
    rows = x_ref.shape[0]
    block = math.gcd(rows, 256)
    cuts = [slice(i, i + block) for i in range(0, rows, block)]

    def leave(value, which, lead):
        if split:
            spread(value, core, grads[2 * which], grads[2 * which + 1], lead)
        else:
            grads[which][...] = value

    @pl.when(step == 0)
    def _():
        for cut in cuts:
            x1 = x_ref[cut, :].astype(F32) + mul(o_ref[:, cut], w_out_ref[...], TN)
            x1_ref[cut, :] = x1
            acc_ref[cut, :] = x1
            h2 = (norm(x1, -1)[0] * gain_ref[...] + bias_ref[...]).astype(BF16)
            h2_ref[cut, :] = h2
            h2t_ref[:, cut] = h2.T

    for cut in cuts:
        dy = dy_ref[cut, :]
        value, slope = gelu_parts(mul(h2_ref[cut, :], w_up_ref[...], NN))
        g = value.astype(BF16)
        g_ref[cut, :] = g
        acc_ref[cut, :] += mul(g, w_down_ref[...], NN)
        du = (mul(dy, w_down_ref[...], NT) * slope).astype(BF16)
        du_ref[cut, :] = du
        part = mul(du, w_up_ref[...], NT)
        dh2_ref[cut, :] = jnp.where(step == 0, part, dh2_ref[cut, :] + part)
    leave(mul(h2t_ref[...], du_ref[...], NN), 0, 8)
    leave(mul(g_ref[...], dy_ref[...], TN), 1, 2)

    @pl.when(step == pl.num_programs(0) - 1)
    def _():
        dgain, dbias = 0.0, 0.0
        for cut in cuts:
            out_ref[cut, :] = acc_ref[cut, :].astype(BF16)
            unit, scale = norm(x1_ref[cut, :], -1)
            dh2 = dh2_ref[cut, :]
            dgain += jnp.sum(dh2 * unit, axis=0, keepdims=True)
            dbias += jnp.sum(dh2, axis=0, keepdims=True)
            dx1 = dy_ref[cut, :].astype(F32) + norm_back(dh2 * gain_ref[...], unit, scale, -1)
            dx1_ref[cut, :] = dx1
            da = dx1.astype(BF16)
            da_ref[cut, :] = da
            do_ref[:, cut] = mul(w_out_ref[...], da, NT)
        dgain_ref[...] = dgain
        dbias_ref[...] = dbias
        leave(mul(o_ref[...], da_ref[...], NN), 2, 8)


def middle(x, o, dy, w_out, gain, bias, w_up, w_down, core=None):
    rows, width = x.shape
    inner = w_up.shape[1]
    steps = 4
    chunk = inner // steps
    split = core is not None
    ins = ([core] if split else []) + [x, o, dy, w_out, gain, bias, w_up, w_down]
    specs = [SCALAR] if split else []
    specs += [fixed(a.shape) for a in ins[-8:-2]]
    specs += [pl.BlockSpec((width, chunk), lambda f: (0, f)), pl.BlockSpec((chunk, width), lambda f: (f, 0))]
    outs = [
        jax.ShapeDtypeStruct((rows, width), BF16),
        jax.ShapeDtypeStruct((rows, width), F32),
        jax.ShapeDtypeStruct((width, rows), F32),
        jax.ShapeDtypeStruct((1, width), F32),
        jax.ShapeDtypeStruct((1, width), F32),
    ]
    out_specs = [fixed(a.shape) for a in outs]
    if split:
        up = jax.ShapeDtypeStruct((4, 2, 2, 16, inner * 3 // 2), BF16)
        down = jax.ShapeDtypeStruct((4, 2, 2, inner // 32, width), BF16)
        out = jax.ShapeDtypeStruct((4, 2, 2, 16, width * 3 // 2), BF16)
        outs += [up, up, down, down, out, out]
        up_spec = pl.BlockSpec((4, 2, 2, 16, chunk * 3 // 2), lambda f: (0, 0, 0, 0, f))
        down_spec = pl.BlockSpec((1, 2, 2, inner // 32, width), lambda f: (f, 0, 0, 0, 0))
        out_specs += [up_spec, up_spec, down_spec, down_spec, fixed(out.shape), fixed(out.shape)]
    else:
        outs += [jax.ShapeDtypeStruct(a.shape, F32) for a in (w_up, w_down, w_out)]
        out_specs += [*specs[-2:], fixed(w_out.shape)]
    return pl.pallas_call(
        functools.partial(middle_kernel, split),
        grid=(steps,),
        in_specs=specs,
        out_specs=out_specs,
        out_shape=outs,
        scratch_shapes=[
            pltpu.VMEM((rows, width), F32),
            pltpu.VMEM((rows, width), BF16),
            pltpu.VMEM((width, rows), BF16),
            pltpu.VMEM((rows, width), F32),
            pltpu.VMEM((rows, width), F32),
            pltpu.VMEM((rows, chunk), BF16),
            pltpu.VMEM((rows, chunk), BF16),
            pltpu.VMEM((rows, width), BF16),
        ],
        compiler_params=params(),
        cost_estimate=pl.CostEstimate(
            flops=6 * rows * (2 * w_up.size + w_out.size),
            bytes_accessed=40 * rows * width,
            transcendentals=rows * inner,
        ),
        name="middle",
    )(*ins)


def head_backs(d_q, d_k, d_v, q, k, inv_q, inv_k, gain_q, gain_k, scale_q, scale_k):
    d_q = d_q * (1.0 / math.sqrt(HD))
    d_k = d_k * (1.0 / LOG2E)
    unit_q = q.astype(F32) * inv_q
    unit_k = k.astype(F32) * inv_k
    sum_q = jnp.sum(d_q * unit_q, axis=2, keepdims=True)
    sum_k = jnp.sum(d_k * unit_k, axis=2, keepdims=True)
    d_q = norm_back(d_q * gain_q, unit_q, scale_q, 1).astype(BF16)
    d_k = norm_back(d_k * gain_k, unit_k, scale_k, 1).astype(BF16)
    return jnp.stack([d_q, d_k, d_v.astype(BF16)]), sum_q, sum_k


def post_kernel(*refs):
    *ins, scale_ref, h_ref, d_ref, sum_q_ref, sum_k_ref, grad_ref = refs
    values = [ref[...] for ref in ins]
    d, sum_q_ref[...], sum_k_ref[...] = head_backs(*values, scale_ref[0], scale_ref[1])
    d_ref[...] = d
    grad_ref[...] = mul(h_ref[...], d.reshape(-1, d.shape[-1]), NT)


def post(d_q, d_k, d_v, q, k, inv_q, inv_k, gain_q, gain_k, scales, h_t):
    heads, _, rows = d_q.shape
    width = h_t.shape[0]
    some = 4
    here = pl.BlockSpec((some, HD, rows), lambda i: (i, 0, 0))
    gain = pl.BlockSpec((some, HD, 1), lambda i: (i, 0, 0))
    columns = 3 * some * HD
    return pl.pallas_call(
        post_kernel,
        grid=(heads // some,),
        in_specs=[here] * 5
        + [gain] * 4
        + [pl.BlockSpec((2, some, 1, rows), lambda i: (0, i, 0, 0)), fixed(h_t.shape)],
        out_specs=[
            pl.BlockSpec((3, some, HD, rows), lambda i: (0, i, 0, 0)),
            gain,
            gain,
            pl.BlockSpec((width, columns), lambda i: (0, i)),
        ],
        out_shape=[
            jax.ShapeDtypeStruct((3, heads, HD, rows), BF16),
            jax.ShapeDtypeStruct((heads, HD, 1), F32),
            jax.ShapeDtypeStruct((heads, HD, 1), F32),
            jax.ShapeDtypeStruct((width, 3 * heads * HD), F32),
        ],
        compiler_params=params(),
        cost_estimate=pl.CostEstimate(
            flops=6 * rows * width * heads * HD,
            bytes_accessed=30 * rows * heads * HD,
            transcendentals=0,
        ),
        name="post",
    )(d_q, d_k, d_v, q, k, inv_q, inv_k, gain_q, gain_k, scales, h_t)


def token_grads(d, w, x, dx1, gain):
    d_h = mul(w, d.reshape(-1, d.shape[-1]), NN).T
    unit, scale = norm(x.astype(F32), -1)
    d_x = dx1 + norm_back(d_h * gain, unit, scale, -1)
    dgain = jnp.sum(d_h * unit, axis=0, keepdims=True)
    dbias = jnp.sum(d_h, axis=0, keepdims=True)
    return d_x.astype(BF16), dgain, dbias


def last_kernel(d_ref, w_ref, x_ref, dx1_ref, gain_ref, out_ref, dgain_ref, dbias_ref):
    out_ref[...], dgain, dbias = token_grads(
        d_ref[...], w_ref[...], x_ref[...], dx1_ref[...], gain_ref[...]
    )
    first = pl.program_id(0) == 0
    dgain_ref[...] = jnp.where(first, dgain, dgain_ref[...] + dgain)
    dbias_ref[...] = jnp.where(first, dbias, dbias_ref[...] + dbias)


def last(d, w, x, dx1, gain):
    rows, width = x.shape
    block = math.gcd(rows, 256)
    row = pl.BlockSpec((block, width), lambda i: (i, 0))
    return pl.pallas_call(
        last_kernel,
        grid=(rows // block,),
        in_specs=[
            pl.BlockSpec(d.shape[:3] + (block,), lambda i: (0, 0, 0, i)),
            fixed(w.shape),
            row,
            row,
            fixed(gain.shape),
        ],
        out_specs=[row, fixed((1, width)), fixed((1, width))],
        out_shape=[
            jax.ShapeDtypeStruct((rows, width), BF16),
            jax.ShapeDtypeStruct((1, width), F32),
            jax.ShapeDtypeStruct((1, width), F32),
        ],
        compiler_params=params(),
        name="last",
    )(d, w, x, dx1, gain)


class Here:
    def __init__(self):
        wide, self.y = lax.axis_index("wide"), lax.axis_index("blk")
        self.core, self.x, self.z = wide % 2, wide // 2 % 2, wide // 4

    def device(self, z=None, x=None, core=None, y=None):
        z = self.z if z is None else z
        x = self.x if x is None else x
        core = self.core if core is None else core
        return (z * 4 + x * 2 + core, self.y if y is None else y)

    def other_core(self):
        return self.device(core=1 - self.core)

    def plane(self, k):
        x = 1 - self.x if k % 2 else self.x
        y = 1 - self.y if k // 2 else self.y
        return x, y

    def column(self, k):
        z = self.z
        return (z, z + 1 - 2 * (z % 2), (z + 2) % 4, 3 - z)[k]

    def partner(self, kind, k):
        if kind == "column":
            return self.device(z=self.column(k))
        x, y = self.plane(k)
        return self.device(x=x, y=y)

    def partners(self):
        every = [self.partner(kind, k) for kind in ("plane", "column") for k in (1, 2, 3)]
        return [self.other_core()] + every

    def part(self, ref, kind, k):
        if kind == "column":
            return ref.at[self.column(k)]
        x, y = self.plane(k)
        return ref.at[:, x, y] if len(ref.shape) == 5 else ref.at[x, y]


def greet(others):
    barrier = pltpu.get_barrier_semaphore()
    for other in others:
        pl.semaphore_signal(barrier, inc=1, device_id=other, device_id_type=MESH)
    pl.semaphore_wait(barrier, len(others))


def remote(source, target, sems, at, to):
    return pltpu.make_async_remote_copy(
        src_ref=source,
        dst_ref=target,
        send_sem=sems[0].at[at],
        recv_sem=sems[1].at[at],
        device_id=to,
        device_id_type=MESH,
    )


class Sum:
    def __init__(self, here, first, give, keep, refs, sems):
        self.here, self.give, self.keep = here, give, keep
        self.kinds = ("plane", "column") if first == "plane" else ("column", "plane")
        self.came0, self.whole, self.came1, self.some, self.came2 = refs
        self.sems = sems

    def copies(self, stage):
        here = self.here
        if stage == 0:
            return [remote(self.give, self.came0, self.sems, 0, here.other_core())]
        kind = self.kinds[stage - 1]
        source, target = ((self.whole, self.came1), (self.some, self.came2))[stage - 1]
        return [
            remote(
                here.part(source, kind, k),
                target.at[k - 1],
                self.sems,
                3 * stage - 3 + k,
                here.partner(kind, k),
            )
            for k in (1, 2, 3)
        ]

    def start(self, stage):
        for copy in self.copies(stage):
            copy.start()

    def wait(self, stage):
        for copy in self.copies(stage):
            copy.wait()

    def add_first(self):
        def body(i, _):
            total = self.keep[i].astype(F32) + self.came0[i].astype(F32)
            self.whole[i] = total.astype(self.whole.dtype)
            return 0

        self.wait(0)
        lax.fori_loop(0, 4, body, 0)
        self.start(1)

    def add_second(self):
        own = self.here.part(self.whole, self.kinds[0], 0)

        def body(i, _):
            total = own[i].astype(F32)
            for k in range(3):
                total += self.came1[k, i].astype(F32)
            self.some[i] = total.astype(self.some.dtype)
            return 0

        self.wait(1)
        lax.fori_loop(0, self.some.shape[0], body, 0)
        self.start(2)

    def add_third(self):
        self.wait(2)
        total = self.here.part(self.some, self.kinds[1], 0)[...].astype(F32)
        for k in range(3):
            total += self.came2[k].astype(F32)
        return total


def sum_scratch(first, tail, kind=BF16, in_place=True):
    lead = (4,) if first == "plane" else (2, 2)
    shapes = [(4, 2, 2), (4, 2, 2), (3,) + lead, lead, (3,)]
    return [pltpu.VMEM(shape + tail, kind) for shape in shapes] + [
        pltpu.SemaphoreType.DMA((7,)),
        pltpu.SemaphoreType.DMA((7,)),
    ]


BATCH = 4


def head_back(here, h, ins, far_out, far_in, far_sems, kept):
    e_far, e_near, do_ref, o_ref, linv_ref, q_ref, k_ref, k_far, v_far, v_near, ones_ref = ins
    low = (do_ref[0] * linv_ref[0, :1]).astype(BF16)
    delta = -jnp.sum(low.astype(F32) * o_ref[0].astype(F32), axis=0, keepdims=True)
    top = delta.astype(BF16).astype(F32)
    row = lax.broadcasted_iota(jnp.int32, (AUG, delta.shape[1]), 0)
    extra = jnp.where(row == 0, top, jnp.where(row == 1, delta - top, 0.0)).astype(BF16)
    do = jnp.concatenate([low, extra], axis=0)
    q = q_ref[h]
    slot = h % BATCH
    keys = k_far.shape[2]
    bk = key_block(keys)
    acc = None
    for which in ("far", "near"):
        for i in range(keys // bk):
            cut = slice(i * bk, (i + 1) * bk)
            k = k_far[0, :, cut] if which == "far" else k_ref[h, :, cut]
            v = (v_far if which == "far" else v_near)[0, :, cut]
            e = (e_far if which == "far" else e_near)[0, cut, :]
            v = jnp.concatenate([v, ones_ref[:, cut]], axis=0)
            ds = (e.astype(F32) * mul(v, do, TN)).astype(BF16)
            part = mul(k, ds, NN)
            acc = part if acc is None else acc + part
            d_k, d_v = mul(q, ds, NT), mul(low, e, NT)
            if which == "far":
                far_out[slot, 0, :, cut] = d_k.astype(BF16)
                far_out[slot, 1, :, cut] = d_v.astype(BF16)
            else:
                kept[slot, 1, :, cut] = d_k
                kept[slot, 2, :, cut] = d_v
        if which == "far":
            remote(far_out.at[slot], far_in.at[h], far_sems, h, here.other_core()).start()
    kept[slot, 0] = acc


def backward_all_kernel(*refs):
    attn, refs = refs[:11], refs[11:]
    gain_refs, refs = refs[:4], refs[4:]
    scale_ref, h_ref, *refs = refs
    up_keep, up_give, down_keep, down_give, out_keep, out_give, *refs = refs
    d_ref, sum_q_ref, sum_k_ref, keep_c, give_c, *refs = refs
    up_out, down_out, out_out, qkv_a, qkv_b, *refs = refs
    far_out, far_in, far_send, far_recv, kept, load_sem, *refs = refs
    here = Here()
    step = pl.program_id(0)
    far_sems = (far_send, far_recv)

    def take(first, give, keep=None):
        nonlocal refs
        mine, sems, refs = refs[:5], refs[5:7], refs[7:]
        return Sum(here, first, give, mine[1] if keep is None else keep, mine, sems)

    chunk = up_keep.shape[-1] // 4
    up_p = (slice(None),) * 4 + (pl.ds(0, chunk),)
    up_c = (slice(None),) * 4 + (pl.ds(chunk, 3 * chunk),)
    sums = [
        take("plane", down_give),
        take("plane", out_give),
        take("plane", up_give.at[up_p]),
        take("column", up_give.at[up_c]),
    ]
    loads = [
        pltpu.make_async_copy(source, total.whole, load_sem.at[i])
        for i, (source, total) in enumerate(
            zip((down_keep, out_keep, up_keep.at[up_p], up_keep.at[up_c]), sums)
        )
    ]
    give_a, give_b, *refs = refs
    more = [take("plane", give_a), take("plane", give_b)]
    heads = H // BATCH

    @pl.when(step == 0)
    def _():
        greet(here.partners())
        for load, total in zip(loads, sums):
            load.start()
            total.start(0)

    def far_copy(h):
        return remote(far_out.at[h % BATCH], far_in.at[h], far_sems, h, here.other_core())

    @pl.when((step % BATCH == 0) & (step > 0))
    def _():
        base = step - BATCH
        for i in range(BATCH):
            far_copy(base + i).wait()
        for i in range(0, BATCH, 2):
            two = pl.ds(base + i, 2)
            some = slice(i, i + 2)
            d_k = kept[some, 1] + far_in[two, 0].astype(F32)
            d_v = kept[some, 2] + far_in[two, 1].astype(F32)
            d, sum_q, sum_k = head_backs(
                kept[some, 0],
                d_k,
                d_v,
                attn[5][two],
                attn[6][two],
                *[ref[some] for ref in gain_refs],
                scale_ref[0, some],
                scale_ref[1, some],
            )
            d_ref[:, some] = d
            sum_q_ref[some] = sum_q
            sum_k_ref[some] = sum_k
        grad = mul(h_ref[...], d_ref[...].reshape(-1, d_ref.shape[-1]), NT)
        for i, (keep, give) in enumerate(
            ((more[0].keep, give_a), (more[1].keep, give_b), (keep_c, give_c))
        ):

            @pl.when(step == BATCH * (i + 1))
            def _():
                spread(grad, here.core, keep, give, 8)
                if i < 2:
                    more[i].start(0)

    @pl.when(step < H)
    def _():
        head_back(here, step, attn, far_out, far_in, far_sems, kept)

    @pl.when(step == 2)
    def _():
        for load, total in zip(loads, sums):
            load.wait()
            total.add_first()

    @pl.when(step == 5)
    def _():
        more[0].add_first()

    @pl.when(step == 8)
    def _():
        for total in sums:
            total.add_second()

    @pl.when(step == 9)
    def _():
        more[0].add_second()
        more[1].add_first()

    @pl.when(step == 11)
    def _():
        more[1].add_second()

    @pl.when(step == H)
    def _():
        down_out[...] = sums[0].add_third()
        unfold(out_out, sums[1].add_third())
        unfold(up_out, sums[2].add_third())
        rest = sums[3].add_third()
        for i in range(3):
            unfold(up_out, rest[:, i * chunk : (i + 1) * chunk], (i + 1) * chunk * 2 // 3)
        unfold(qkv_a, more[0].add_third())
        unfold(qkv_b, more[1].add_third())


def once(shape):
    return pl.BlockSpec(shape, lambda *_: (0,) * len(shape), pipeline_mode=pl.Buffered(1))


ANYWHERE = pl.BlockSpec(memory_space=pl.ANY)


def backward_all(
    e_far, e_near, d_o, o, linv, q, k, k_far, v_far, v, ones, gains, scales, h_t, up, down, out
):
    _, keys, rows = e_far.shape
    width = h_t.shape[0]
    inner = up[0].shape[-1] * 2 // 3

    def head(*tail):
        return pl.BlockSpec((1,) + tail, lambda s: (jnp.minimum(s, H - 1),) + (0,) * len(tail))

    def batch(s):
        return jnp.maximum(s // BATCH - 1, 0)

    gain = pl.BlockSpec((BATCH, HD, 1), lambda s: (batch(s), 0, 0))
    specs = [head(keys, rows), head(keys, rows), head(HD, rows), head(HD, rows), head(8, rows)]
    specs += [once(q.shape), once(k.shape), head(HD, keys), head(HD, keys), head(HD, keys)]
    specs += [once(ones.shape)] + [gain] * 4
    specs.append(pl.BlockSpec((2, BATCH, 1, rows), lambda s: (0, batch(s), 0, 0)))
    specs.append(once(h_t.shape))
    specs += [ANYWHERE] * 6
    part = (16, 3 * BATCH * HD * 3 // 2)
    third = jax.ShapeDtypeStruct((4, 2, 2) + part, BF16)
    shard = width // 32
    outs = [
        jax.ShapeDtypeStruct((3, H, HD, rows), BF16),
        jax.ShapeDtypeStruct((H, HD, 1), F32),
        jax.ShapeDtypeStruct((H, HD, 1), F32),
        third,
        third,
        jax.ShapeDtypeStruct((shard, inner), F32),
        jax.ShapeDtypeStruct((inner // 32, width), F32),
        jax.ShapeDtypeStruct((shard, width), F32),
        jax.ShapeDtypeStruct((shard, 3 * BATCH * HD), F32),
        jax.ShapeDtypeStruct((shard, 3 * BATCH * HD), F32),
    ]
    out_specs = [pl.BlockSpec((3, BATCH, HD, rows), lambda s: (0, batch(s), 0, 0)), gain, gain]
    out_specs += [once(a.shape) for a in outs[3:]]
    chunk = inner * 3 // 8
    scratch = [
        pltpu.VMEM((BATCH, 2, HD, keys), BF16),
        pltpu.VMEM((H, 2, HD, keys), BF16),
        pltpu.SemaphoreType.DMA((H,)),
        pltpu.SemaphoreType.DMA((H,)),
        pltpu.VMEM((BATCH, 3, HD, rows), F32),
        pltpu.SemaphoreType.DMA((4,)),
        *sum_scratch("plane", (inner // 32, width)),
        *sum_scratch("plane", (16, width * 3 // 2)),
        *sum_scratch("plane", (16, chunk)),
        *sum_scratch("column", (16, 3 * chunk)),
        pltpu.VMEM((4, 2, 2) + part, BF16),
        pltpu.VMEM((4, 2, 2) + part, BF16),
        *sum_scratch("plane", part),
        *sum_scratch("plane", part),
    ]
    return pl.pallas_call(
        backward_all_kernel,
        grid=(H + 1,),
        in_specs=specs,
        out_specs=out_specs,
        out_shape=outs,
        scratch_shapes=scratch,
        compiler_params=pltpu.CompilerParams(
            vmem_limit_bytes=61 * 2**20, collective_id=0, has_side_effects=True
        ),
        name="backward_all",
    )(
        e_far, e_near, d_o, o, linv, q, k, k_far, v_far, v, ones, *gains, scales, h_t,
        *up, *down, *out,
    )


def tail_kernel(*refs):
    d_ref, w_ref, x_ref, dx1_ref, gain_ref, *refs = refs
    sum_q_ref, sum_k_ref, dgain2_ref, dbias2_ref, keep_ref, give_ref, *refs = refs
    out_ref, qkv_ref, table_ref, *refs = refs
    made, vectors, keep_t, give_t, stay_sem, swap_send, swap_recv, *refs = refs
    here = Here()
    step = pl.program_id(0)
    steps = pl.num_programs(0)
    block = x_ref.shape[0]
    swapped = here.core != here.y
    opposite = here.device(core=here.y, y=here.core)
    rest = Sum(here, "column", give_ref, keep_ref, refs[:5], refs[5:7])
    table = Sum(here, "plane", give_t, keep_t, refs[7:12], refs[12:14])

    @pl.when(step == 0)
    def _():
        greet(here.partners() + [here.device(core=1 - here.core, y=1 - here.y)])
        rest.start(0)

    def stay(i):
        cut = pl.ds(i * block, block)
        return pltpu.make_async_copy(made.at[cut], out_ref.at[cut], stay_sem.at[i])

    def move(i):
        cut = pl.ds(i * block, block)
        return remote(made.at[cut], out_ref.at[cut], (swap_send, swap_recv), i, opposite)

    new, dgain, dbias = token_grads(
        d_ref[...], w_ref[...], x_ref[...], dx1_ref[...], gain_ref[...]
    )
    made[pl.ds(pl.multiple_of(step * block, block), block), :] = new
    first = step == 0
    vectors[0:1, :] = jnp.where(first, dgain, vectors[0:1, :] + dgain)
    vectors[1:2, :] = jnp.where(first, dbias, vectors[1:2, :] + dbias)

    @pl.when(swapped)
    def _():
        move(step).start()

    @pl.when(jnp.logical_not(swapped))
    def _():
        stay(step).start()

    @pl.when(step == 0)
    def _():
        rest.add_first()

    @pl.when(step == steps - 1)
    def _():
        width = x_ref.shape[1]
        rows = [vectors[0:1, :], vectors[1:2, :], dgain2_ref[...], dbias2_ref[...]]
        rows.append(jnp.zeros((124, width), F32))
        columns = jnp.concatenate(rows, axis=0).T
        lane = lax.broadcasted_iota(jnp.int32, columns.shape, 1)
        columns = jnp.where(lane == 4, sum_q_ref[...].reshape(width, 1), columns)
        columns = jnp.where(lane == 5, sum_k_ref[...].reshape(width, 1), columns)
        columns = columns.reshape(8, 2, 2, width // 32, 128)
        mine = here.core == 0
        keep_t[...] = jnp.where(mine, columns[:, 0], columns[:, 1]).reshape(keep_t.shape)
        give_t[...] = jnp.where(mine, columns[:, 1], columns[:, 0]).reshape(keep_t.shape)
        table.start(0)
        table.add_first()
        table.add_second()
        rest.add_second()
        table_ref[...] = table.add_third()
        unfold(qkv_ref, rest.add_third())

        @pl.when(swapped)
        def _():
            for i in range(steps):
                move(i).wait()

        @pl.when(jnp.logical_not(swapped))
        def _():
            for i in range(steps):
                stay(i).wait()


def tail(d, w, x, dx1, gain, sum_q, sum_k, dgain2, dbias2, keep, give):
    rows, width = x.shape
    block = math.gcd(rows, 256)
    steps = rows // block
    row = pl.BlockSpec((block, width), lambda i: (i, 0))
    shard = width // 32
    part = keep.shape[-2:]
    return pl.pallas_call(
        tail_kernel,
        grid=(steps,),
        in_specs=[
            pl.BlockSpec(d.shape[:3] + (block,), lambda i: (0, 0, 0, i)),
            once(w.shape),
            row,
            row,
            once(gain.shape),
            once(sum_q.shape),
            once(sum_k.shape),
            once(dgain2.shape),
            once(dbias2.shape),
            once(keep.shape),
            ANYWHERE,
        ],
        out_specs=[ANYWHERE, once((shard, 3 * BATCH * HD)), once((shard, 128))],
        out_shape=[
            jax.ShapeDtypeStruct((rows, width), BF16),
            jax.ShapeDtypeStruct((shard, 3 * BATCH * HD), F32),
            jax.ShapeDtypeStruct((shard, 128), F32),
        ],
        scratch_shapes=[
            pltpu.VMEM((rows, width), BF16),
            pltpu.VMEM((8, width), F32),
            pltpu.VMEM((4, 2, 2, shard, 128), F32),
            pltpu.VMEM((4, 2, 2, shard, 128), F32),
            pltpu.SemaphoreType.DMA((steps,)),
            pltpu.SemaphoreType.DMA((steps,)),
            pltpu.SemaphoreType.DMA((steps,)),
            *sum_scratch("column", part),
            *sum_scratch("plane", (shard, 128), F32),
        ],
        compiler_params=pltpu.CompilerParams(
            vmem_limit_bytes=VMEM_LIMIT, collective_id=1, has_side_effects=True
        ),
        name="tail",
    )(d, w, x, dx1, gain, sum_q, sum_k, dgain2, dbias2, keep, give)


def place(index):
    return index // 8, index // 4 % 2, index // 2 % 2, index % 2


def device(z, x, core, y):
    return ((z * 2 + x) * 2 + core) * 2 + y


def pairs(other):
    every = [(i, device(*other(*place(i)))) for i in range(32)]
    return [(i, j) for i, j in every if i != j]


SWAP = pairs(lambda z, x, c, y: (z, x, y, c))
CORE = pairs(lambda z, x, c, y: (z, x, 1 - c, y))


def send(value, where):
    return lax.ppermute(value, AXES, where)


def after(values, *done):
    return lax.optimization_barrier((values, done))[0]


def segments(lengths, group, mine, rows):
    count = lengths.shape[1]
    at = jnp.arange(count)
    ends = jnp.sum(jnp.where(at[:, None] <= at[None, :], lengths[0][:, None], 0), axis=0)
    spots = jnp.arange(group, dtype=jnp.int32)
    segment = jnp.sum((spots[None, :] >= ends[:, None]).astype(jnp.int32), axis=0)
    is_in = jnp.arange(AUG)[:, None] == segment[None, :]
    mask_k = is_in.astype(BF16)
    mask_q = jnp.where(is_in, 0.0, BLOCKED).astype(BF16)
    mask_q = lax.dynamic_slice_in_dim(mask_q, mine * rows, rows, axis=1)
    ones = jnp.broadcast_to((jnp.arange(AUG) < 2)[:, None], (AUG, group)).astype(BF16)
    return mask_q, mask_k, ones


def ungroup(grads):
    parts = [g.reshape(-1, 3, BATCH * HD) for g in grads]
    return jnp.concatenate(parts, axis=2).reshape(parts[0].shape[0], -1)


def on_chips(tokens, lengths, gains, w_t, w_qkv, w_out, w_up, w_down, cotangent):
    ln1_gain, ln1_bias, ln2_gain, ln2_bias, fold_q, fold_k, inv_q, inv_k, gain_q, gain_k = gains
    rows, width = tokens.shape
    wide, y = lax.axis_index("wide"), lax.axis_index("blk")
    core = wide % 2
    swapped = core != y
    flag = swapped.astype(jnp.int32).reshape(1)
    core_at = core.astype(jnp.int32).reshape(1)

    def swap(value):
        return jnp.where(swapped, send(value, SWAP), value)

    lengths = swap(lengths)
    came = send(tokens, SWAP)
    cotangent_came = send(after(cotangent, came), SWAP)
    mask_q, mask_k, ones = segments(lengths, 2 * rows, core, rows)
    mask_near = lax.dynamic_slice_in_dim(mask_k, core * rows, rows, axis=1)
    mask_far = lax.dynamic_slice_in_dim(mask_k, (1 - core) * rows, rows, axis=1)
    ones = ones[:, :rows]

    h_t, q, k, v, scales, tokens = project(
        tokens, ln1_gain, ln1_bias, w_t, fold_q, fold_k, flag, came
    )
    k_far, v_far = send(k, CORE), send(v, CORE)
    had, e_near = attend(q, k, v, mask_q, mask_near, ones)
    e_far, o, linv = attend(q, k_far, v_far, mask_q, mask_far, ones, had)
    cotangent = jnp.where(swapped, cotangent_came, cotangent)
    output, dx1, d_o, dgain2, dbias2, *grads = middle(
        tokens, o.reshape(width, rows), cotangent, w_out, ln2_gain, ln2_bias, w_up, w_down, core_at
    )
    d_o = d_o.reshape(H, HD, rows)
    output = swap(output)
    gains = [inv_q, inv_k, gain_q, gain_k]
    d, sum_q, sum_k, keep, give, up, down, out, qkv_a, qkv_b = backward_all(
        e_far, e_near, d_o, o, linv, q, k, k_far, v_far, v, ones, gains, scales, h_t,
        grads[0:2], grads[2:4], grads[4:6],
    )
    grad_tokens, qkv_c, table = tail(
        d, w_qkv, tokens, dx1, ln1_gain, sum_q, sum_k, dgain2, dbias2, keep, give
    )
    sums = [table[:, i] for i in (0, 1, 4, 5, 2, 3)]
    return output, grad_tokens, sums, ungroup([qkv_a, qkv_b, qkv_c]), out, up, down


def anywhere(tokens, lengths, gains, w_t, w_qkv, w_out, w_up, w_down, cotangent):
    ln1_gain, ln1_bias, ln2_gain, ln2_bias, fold_q, fold_k, inv_q, inv_k, gain_q, gain_k = gains
    rows, width = tokens.shape
    parts = lax.axis_size("blk")
    mask_q, mask_k, ones = segments(lengths, rows * parts, lax.axis_index("blk"), rows)
    h_t, q, k, v, scales = project(tokens, ln1_gain, ln1_bias, w_t, fold_q, fold_k)
    k_all = lax.all_gather(k, "blk", axis=2, tiled=True)
    v_all = lax.all_gather(v, "blk", axis=2, tiled=True)
    had, e_all = attend(q, k_all, v_all, mask_q, mask_k, ones)
    linv = jnp.broadcast_to(1.0 / had[:, HD : HD + 1], (H, 8, rows))
    o = (had[:, :HD] * linv[:, :1]).astype(BF16)
    output, dx1, d_o, dgain2, dbias2, up, down, out = middle(
        tokens, o.reshape(width, rows), cotangent, w_out, ln2_gain, ln2_bias, w_up, w_down
    )
    d_o = d_o.reshape(H, HD, rows)
    d_q, d_k, d_v = attend_back(e_all, d_o, o, linv, q, k_all, v_all, ones, 0, H, F32)
    pair = jnp.stack([d_k, d_v]).reshape(2, H, HD, parts, rows)
    pair = jnp.transpose(pair, (3, 0, 1, 2, 4)).astype(BF16)
    pair = lax.psum_scatter(pair, "blk", scatter_dimension=0, tiled=False).astype(F32)
    d, sum_q, sum_k, grad = post(
        d_q, pair[0], pair[1], q, k, inv_q, inv_k, gain_q, gain_k, scales, h_t
    )
    grad_tokens, dgain1, dbias1 = last(d, w_qkv, tokens, dx1, ln1_gain)
    scatter = functools.partial(lax.psum_scatter, axis_name=AXES, scatter_dimension=0, tiled=True)
    sums = [
        scatter(g.reshape(width)) for g in (dgain1, dbias1, sum_q, sum_k, dgain2, dbias2)
    ]
    grad = ungroup(jnp.split(grad, H // BATCH, axis=1))
    return output, grad_tokens, sums, scatter(grad), scatter(out), scatter(up), scatter(down)


def shards(
    tokens,
    lengths,
    ln1_gain,
    ln1_bias,
    w_qkv,
    q_gain,
    k_gain,
    w_out,
    ln2_gain,
    ln2_bias,
    w_up,
    w_down,
    cotangent,
):
    width = tokens.shape[1]
    fold_q, fold_k = LOG2E / math.sqrt(HD), 1.0
    gains = [g.reshape(1, width) for g in (ln1_gain, ln1_bias, ln2_gain, ln2_bias)]
    gains += [
        g.reshape(H, HD, 1)
        for g in (
            q_gain * fold_q,
            k_gain * fold_k,
            1.0 / (q_gain * fold_q),
            1.0 / (k_gain * fold_k),
            q_gain,
            k_gain,
        )
    ]
    known = lax.axis_size("blk") == 2 and lax.axis_size("wide") == 16
    run = on_chips if known else anywhere
    output, grad_tokens, sums, s_qkv, s_out, s_up, s_down = run(
        tokens, lengths, gains, w_qkv.T, w_qkv, w_out, w_up, w_down, cotangent
    )
    return (
        output,
        grad_tokens,
        sums[0],
        sums[1],
        s_qkv,
        sums[2],
        sums[3],
        s_out,
        sums[4],
        sums[5],
        s_up,
        s_down,
    )


def solution(mesh):
    split = P(AXES, None)
    in_specs = (split, P("wide", None)) + (P(),) * 10 + (split,)
    vector = P(AXES)
    out_specs = (
        split,
        split,
        vector,
        vector,
        split,
        vector,
        vector,
        split,
        vector,
        vector,
        split,
        split,
    )
    return jax.shard_map(shards, mesh=mesh, in_specs=in_specs, out_specs=out_specs, check_vma=False)
```

```python
import functools
import math

import jax
import jax.numpy as jnp
from jax import lax
from jax.experimental import pallas as pl
from jax.experimental.pallas import tpu as pltpu
from jax.sharding import PartitionSpec as P

H = 12
HD = 64
EPS = 1e-06
AXES = ("wide", "blk")
AUG = 16
BLOCKED = -512.0
LOG2E = math.log2(math.e)
NN = (((1,), (0,)), ((), ()))
NT = (((1,), (1,)), ((), ()))
TN = (((0,), (0,)), ((), ()))
TT = (((0,), (1,)), ((), ()))
BF16 = jnp.bfloat16
MESH = pl.DeviceIdType.MESH
F32 = jnp.float32
VMEM_LIMIT = 56 * 2**20


def mul(left, right, dims, kind=F32):
    return lax.dot_general(left, right, dims, preferred_element_type=F32).astype(kind)


def ones_rows(columns):
    return (lax.broadcasted_iota(jnp.int32, (AUG, columns), 0) < 2).astype(BF16)


def key_block(keys):
    return math.gcd(keys, 512)


def forward_kernel(count, *refs):
    q_ref, mq_ref, *refs = refs
    parts, (o_ref, linv_ref, *e_refs) = refs[: 3 * count], refs[3 * count :]
    keys = parts[0].shape[2]
    bk = key_block(keys)
    ones = ones_rows(bk)
    for h in range(q_ref.shape[0]):
        q = jnp.concatenate([q_ref[h], mq_ref[...]], axis=0)
        acc = None
        for p in range(count):
            k_ref, v_ref, mk_ref = parts[3 * p : 3 * p + 3]
            for i in range(keys // bk):
                cut = slice(i * bk, (i + 1) * bk)
                k = jnp.concatenate([k_ref[h, :, cut], mk_ref[:, cut]], axis=0)
                v = jnp.concatenate([v_ref[h, :, cut], ones], axis=0)
                e = jnp.exp2(mul(k, q, TN)).astype(BF16)
                e_refs[p][h, cut, :] = e
                part = mul(v, e, NN)
                acc = part if acc is None else acc + part
        linv = 1.0 / acc[HD : HD + 1]
        o_ref[h] = (acc[:HD] * linv).astype(BF16)
        linv_ref[h] = jnp.broadcast_to(linv, linv_ref.shape[1:])


def attend(q, mask_q, parts):
    heads, _, rows = q.shape
    keys = parts[0][0].shape[2]
    some = 2 if len(parts) * keys * rows <= 1 << 21 else 1

    def head(*tail):
        return pl.BlockSpec((some,) + tail, lambda h: (h,) + (0,) * len(tail))

    specs = [head(HD, rows), fixed(mask_q.shape)]
    for part in parts:
        specs += [head(HD, keys), head(HD, keys), fixed(part[2].shape)]
    return pl.pallas_call(
        functools.partial(forward_kernel, len(parts)),
        grid=(heads // some,),
        in_specs=specs,
        out_specs=[head(HD, rows), head(8, rows)] + [head(keys, rows)] * len(parts),
        out_shape=[
            jax.ShapeDtypeStruct((heads, HD, rows), BF16),
            jax.ShapeDtypeStruct((heads, 8, rows), F32),
        ]
        + [jax.ShapeDtypeStruct((heads, keys, rows), BF16)] * len(parts),
        compiler_params=params(),
        cost_estimate=pl.CostEstimate(
            flops=heads * rows * keys * len(parts) * 1024,
            bytes_accessed=heads * rows * keys * len(parts) * 2,
            transcendentals=heads * rows * keys * len(parts),
        ),
        name="attend",
    )(q, mask_q, *[a for part in parts for a in part])


def scaled_gradient(do_ref, o_ref, linv_ref, h):
    low = (do_ref[h] * linv_ref[h, :1]).astype(BF16)
    delta = -jnp.sum(low.astype(F32) * o_ref[h].astype(F32), axis=0, keepdims=True)
    top = delta.astype(BF16).astype(F32)
    row = lax.broadcasted_iota(jnp.int32, (AUG, delta.shape[1]), 0)
    extra = jnp.where(row == 0, top, jnp.where(row == 1, delta - top, 0.0)).astype(BF16)
    return low, jnp.concatenate([low, extra], axis=0)


def block_back(e, low, do, q, k, v):
    v = jnp.concatenate([v, ones_rows(v.shape[1])], axis=0)
    ds = (e.astype(F32) * mul(v, do, TN)).astype(BF16)
    return mul(k, ds, NN), mul(q, ds, NT), mul(low, e, NT)


def backward_kernel(e_ref, do_ref, o_ref, linv_ref, q_ref, k_ref, v_ref, dq_ref, dk_ref, dv_ref):
    keys = k_ref.shape[2]
    bk = key_block(keys)
    low, do = scaled_gradient(do_ref, o_ref, linv_ref, 0)
    acc = None
    for i in range(keys // bk):
        cut = slice(i * bk, (i + 1) * bk)
        part, dk_ref[0, :, cut], dv_ref[0, :, cut] = block_back(
            e_ref[0, cut, :], low, do, q_ref[0], k_ref[0, :, cut], v_ref[0, :, cut]
        )
        acc = part if acc is None else acc + part
    dq_ref[0] = acc


def attend_back(e, do, o, linv, q, k, v):
    heads, keys, rows = e.shape

    def head(*tail):
        return pl.BlockSpec((1,) + tail, lambda h: (h,) + (0,) * len(tail))

    specs = [head(keys, rows), head(HD, rows), head(HD, rows), head(8, rows), head(HD, rows)]
    return pl.pallas_call(
        backward_kernel,
        grid=(heads,),
        in_specs=specs + [head(HD, keys)] * 2,
        out_specs=[head(HD, rows), head(HD, keys), head(HD, keys)],
        out_shape=[
            jax.ShapeDtypeStruct((heads, HD, rows), F32),
            jax.ShapeDtypeStruct((heads, HD, keys), F32),
            jax.ShapeDtypeStruct((heads, HD, keys), F32),
        ],
        compiler_params=params(),
        name="attend_back",
    )(e, do, o, linv, q, k, v)


def norm(value, axis):
    mean = jnp.mean(value, axis=axis, keepdims=True)
    centred = value - mean
    scale = lax.rsqrt(jnp.mean(centred * centred, axis=axis, keepdims=True) + EPS)
    return centred * scale, scale


def norm_back(grad, unit, scale, axis):
    mean = jnp.mean(grad, axis=axis, keepdims=True)
    along = jnp.mean(grad * unit, axis=axis, keepdims=True)
    return scale * (grad - mean - unit * along)


def gelu_parts(u):
    root = math.sqrt(2.0 / math.pi)
    square = u * u
    t = jnp.tanh(u * (root + (root * 0.044715) * square))
    half = 0.5 + 0.5 * t
    slope = half + (u * (0.5 - 0.5 * t * t)) * (root + (3 * root * 0.044715) * square)
    return u * half, slope


def params(**more):
    return pltpu.CompilerParams(vmem_limit_bytes=VMEM_LIMIT, **more)


def fixed(shape):
    return pl.BlockSpec(shape, lambda *_: (0,) * len(shape))


SCALAR = pl.BlockSpec(memory_space=pltpu.SMEM)
ANYWHERE = pl.BlockSpec(memory_space=pl.ANY)


def normed(x, gain, bias):
    return (norm(x.astype(F32), -1)[0] * gain + bias).astype(BF16)


def heads_of(h, w_ref, gains_ref):
    width = h.shape[1]

    def part(i):
        value = mul(w_ref[i * width : (i + 1) * width, :], h, NT)
        return value.reshape(width // HD, HD, h.shape[0])

    unit_k, scale_k = norm(part(1), 1)
    k = (unit_k * gains_ref[:, :, 1:2]).astype(BF16)
    v = part(2).astype(BF16)
    unit_q, scale_q = norm(part(0), 1)
    q = (unit_q * gains_ref[:, :, 0:1]).astype(BF16)
    return q, k, v, scale_q, scale_k


def project_kernel(x_ref, vec_ref, w_ref, gains_ref, h_ref, q_ref, k_ref, v_ref, scale_ref):
    h = normed(x_ref[...], vec_ref[0:1, :], vec_ref[1:2, :])
    h_ref[...] = h.T
    q_ref[...], k_ref[...], v_ref[...], scale_ref[0], scale_ref[1] = heads_of(h, w_ref, gains_ref)


def project(tokens, vectors, w_t, gains):
    rows, width = tokens.shape
    block = math.gcd(rows, 256)
    head = pl.BlockSpec((H, HD, block), lambda i: (0, 0, i))
    head_shape = jax.ShapeDtypeStruct((H, HD, rows), BF16)
    return pl.pallas_call(
        project_kernel,
        grid=(rows // block,),
        in_specs=[pl.BlockSpec((block, width), lambda i: (i, 0))]
        + [fixed(a.shape) for a in (vectors, w_t, gains)],
        out_specs=[
            pl.BlockSpec((width, block), lambda i: (0, i)),
            head,
            head,
            head,
            pl.BlockSpec((2, H, 1, block), lambda i: (0, 0, 0, i)),
        ],
        out_shape=[
            jax.ShapeDtypeStruct((width, rows), BF16),
            head_shape,
            head_shape,
            head_shape,
            jax.ShapeDtypeStruct((2, H, 1, rows), F32),
        ],
        compiler_params=params(),
        name="project",
    )(tokens, vectors, w_t, gains)


def fold(value):
    if value.shape[-2] % 16 == 0:
        return value
    half = value.shape[-1] // 2
    low = value[..., 16:, :]
    low = jnp.concatenate([low[..., :half], low[..., half:]], axis=-2)
    return jnp.concatenate([value[..., :16, :], low], axis=-1)


def unfold(out_ref, value, start=0):
    count = value.shape[-1] * 2 // 3
    half = count // 2
    out_ref[:16, start : start + count] = value[:, :count]
    out_ref[16:, start : start + half] = value[:8, count:]
    out_ref[16:, start + half : start + count] = value[8:, count:]


def spread(value, core, keep_ref, give_ref, lead):
    rows, columns = value.shape
    value = value.reshape((lead, 2, 2, rows // (4 * lead), columns))
    mine = core == 0
    keep = jnp.where(mine, value[:, 0], value[:, 1])
    give = jnp.where(mine, value[:, 1], value[:, 0])
    keep_ref[...] = fold(keep).astype(BF16).reshape(keep_ref.shape)
    give_ref[...] = fold(give).astype(BF16).reshape(give_ref.shape)


def middle_kernel(split, *refs):
    x_ref, o_ref, dy_ref, w_out_ref, vec_ref, w_up_ref, w_down_ref, *refs = refs
    if split:
        dy_here, (dy_came, *refs) = dy_ref, refs
    out_ref, dx1_ref, do_ref, dgain_ref, dbias_ref, *refs = refs
    grads, refs = (refs[:6], refs[6:]) if split else (refs[:3], refs[3:])
    x1_ref, h2_ref, h2t_ref, acc_ref, dh2_ref, g_ref, du_ref, da_ref, *refs = refs
    step = pl.program_id(0)
    rows = x_ref.shape[0]
    block = math.gcd(rows, 256)
    cuts = [slice(i, i + block) for i in range(0, rows, block)]
    if split:
        here = Here()
        keep_up, keep_down, keep_out, give_out, came_up, came_down = grads
        give_up, give_down, up_send, up_recv, down_send, down_recv, dy_ref, dy_sem = refs
        swapped = here.core != here.y

        def copies(f):
            to = here.other_core()
            return [
                remote(give_up.at[f % 2], came_up.at[f], (up_send, up_recv), f, to),
                remote(give_down.at[f % 2], came_down.at[f], (down_send, down_recv), f, to),
            ]

    @pl.when(step == 0)
    def _():
        if split:
            greet([here.other_core()])

            @pl.when(swapped)
            def _():
                pltpu.make_async_copy(dy_came, dy_ref, dy_sem.at[0]).start()

            @pl.when(jnp.logical_not(swapped))
            def _():
                pltpu.make_async_copy(dy_here, dy_ref, dy_sem.at[0]).start()

        for cut in cuts:
            x1 = x_ref[cut, :].astype(F32) + mul(o_ref[:, cut], w_out_ref[...], TN)
            x1_ref[cut, :] = x1
            acc_ref[cut, :] = x1
            h2 = normed(x1, vec_ref[2:3, :], vec_ref[3:4, :])
            h2_ref[cut, :] = h2
            h2t_ref[:, cut] = h2.T
        if split:
            pltpu.make_async_copy(dy_here, dy_ref, dy_sem.at[0]).wait()

    for cut in cuts:
        dy = dy_ref[cut, :]
        value, slope = gelu_parts(mul(h2_ref[cut, :], w_up_ref[...], NN))
        g = value.astype(BF16)
        g_ref[cut, :] = g
        acc_ref[cut, :] += mul(g, w_down_ref[...], NN)
        du = (mul(dy, w_down_ref[...], NT) * slope).astype(BF16)
        du_ref[cut, :] = du
        part = mul(du, w_up_ref[...], NT)
        dh2_ref[cut, :] = jnp.where(step == 0, part, dh2_ref[cut, :] + part)
    grad_up = mul(h2t_ref[...], du_ref[...], NN)
    grad_down = mul(g_ref[...], dy_ref[...], TN)
    if split:

        @pl.when(step >= 2)
        def _():
            for copy in copies(step - 2):
                copy.wait_send()

        spread(grad_up, here.core, keep_up, give_up.at[step % 2], 8)
        spread(grad_down, here.core, keep_down, give_down.at[step % 2], 2)
        for copy in copies(step):
            copy.start()
    else:
        grads[0][...] = grad_up
        grads[1][...] = grad_down

    @pl.when(step == pl.num_programs(0) - 1)
    def _():
        dgain, dbias = 0.0, 0.0
        for cut in cuts:
            out_ref[cut, :] = acc_ref[cut, :].astype(BF16)
            unit, scale = norm(x1_ref[cut, :], -1)
            dh2 = dh2_ref[cut, :]
            dgain += jnp.sum(dh2 * unit, axis=0, keepdims=True)
            dbias += jnp.sum(dh2, axis=0, keepdims=True)
            dx1 = dy_ref[cut, :].astype(F32) + norm_back(dh2 * vec_ref[2:3, :], unit, scale, -1)
            dx1_ref[cut, :] = dx1
            da = dx1.astype(BF16)
            da_ref[cut, :] = da
            do_ref[:, cut] = mul(w_out_ref[...], da, NT)
        dgain_ref[...] = dgain
        dbias_ref[...] = dbias
        grad_out = mul(o_ref[...], da_ref[...], NN)
        if split:
            spread(grad_out, here.core, keep_out, give_out, 8)
            for f in range(FF_STEPS):
                for copy in copies(f):
                    copy.wait_recv()
                    if f >= FF_STEPS - 2:
                        copy.wait_send()
        else:
            grads[2][...] = grad_out


FF_STEPS = 4


def middle(x, o, dy, w_out, vectors, w_up, w_down, came=None):
    rows, width = x.shape
    inner = w_up.shape[1]
    chunk = inner // FF_STEPS
    split = came is not None
    ins = [x, o, dy, w_out, vectors, w_up, w_down]
    specs = [fixed(a.shape) for a in ins[:5]]
    specs += [pl.BlockSpec((width, chunk), lambda f: (0, f)), pl.BlockSpec((chunk, width), lambda f: (f, 0))]
    weights = specs[-2:]
    if split:
        ins.append(came)
        specs[2] = ANYWHERE
        specs.append(ANYWHERE)
    outs = [
        jax.ShapeDtypeStruct((rows, width), BF16),
        jax.ShapeDtypeStruct((rows, width), F32),
        jax.ShapeDtypeStruct((width, rows), F32),
        jax.ShapeDtypeStruct((1, width), F32),
        jax.ShapeDtypeStruct((1, width), F32),
    ]
    out_specs = [fixed(a.shape) for a in outs]
    scratch = [
        pltpu.VMEM((rows, width), F32),
        pltpu.VMEM((rows, width), BF16),
        pltpu.VMEM((width, rows), BF16),
        pltpu.VMEM((rows, width), F32),
        pltpu.VMEM((rows, width), F32),
        pltpu.VMEM((rows, chunk), BF16),
        pltpu.VMEM((rows, chunk), BF16),
        pltpu.VMEM((rows, width), BF16),
    ]
    more = {}
    if split:
        up = (4, 2, 2, 16, chunk * 3 // 2)
        down = (2, 2, inner // 32, width)
        out = jax.ShapeDtypeStruct((4, 2, 2, 16, width * 3 // 2), BF16)
        ups = jax.ShapeDtypeStruct((FF_STEPS,) + up, BF16)
        downs = jax.ShapeDtypeStruct((FF_STEPS,) + down, BF16)
        outs += [ups, downs, out, out, ups, downs]
        out_specs += [pl.BlockSpec((1,) + up, lambda f: (f,) + (0,) * len(up))]
        out_specs += [pl.BlockSpec((1,) + down, lambda f: (f,) + (0,) * len(down))]
        out_specs += [fixed(out.shape), fixed(out.shape), ANYWHERE, ANYWHERE]
        scratch += [pltpu.VMEM((2,) + up, BF16), pltpu.VMEM((2,) + down, BF16)]
        scratch += [pltpu.SemaphoreType.DMA((FF_STEPS,))] * 4
        scratch += [pltpu.VMEM((rows, width), BF16), pltpu.SemaphoreType.DMA((1,))]
        more = {"collective_id": 2, "has_side_effects": True}
    else:
        outs += [jax.ShapeDtypeStruct(a.shape, F32) for a in (w_up, w_down, w_out)]
        out_specs += [*weights, fixed(w_out.shape)]
    return pl.pallas_call(
        functools.partial(middle_kernel, split),
        grid=(FF_STEPS,),
        in_specs=specs,
        out_specs=out_specs,
        out_shape=outs,
        scratch_shapes=scratch,
        compiler_params=params(**more),
        cost_estimate=pl.CostEstimate(
            flops=6 * rows * (2 * w_up.size + w_out.size),
            bytes_accessed=40 * rows * width,
            transcendentals=rows * inner,
        ),
        name="middle",
    )(*ins)


def head_backs(d_q, d_k, d_v, q, k, gains, scale_q, scale_k):
    d_q = d_q * (1.0 / math.sqrt(HD))
    d_k = d_k * (1.0 / LOG2E)
    inv_q, inv_k, gain_q, gain_k = [gains[:, :, i : i + 1] for i in range(2, 6)]
    unit_q = q.astype(F32) * inv_q
    unit_k = k.astype(F32) * inv_k
    sum_q = jnp.sum(d_q * unit_q, axis=2, keepdims=True)
    sum_k = jnp.sum(d_k * unit_k, axis=2, keepdims=True)
    d_q = norm_back(d_q * gain_q, unit_q, scale_q, 1).astype(BF16)
    d_k = norm_back(d_k * gain_k, unit_k, scale_k, 1).astype(BF16)
    return jnp.stack([d_q, d_k, d_v.astype(BF16)]), sum_q, sum_k


def post_kernel(*refs):
    *ins, scale_ref, h_ref, d_ref, sum_q_ref, sum_k_ref, grad_ref = refs
    values = [ref[...] for ref in ins]
    d, sum_q_ref[...], sum_k_ref[...] = head_backs(*values, scale_ref[0], scale_ref[1])
    d_ref[...] = d
    grad_ref[...] = mul(h_ref[...], d.reshape(-1, d.shape[-1]), NT)


def post(d_q, d_k, d_v, q, k, gains, scales, h_t):
    heads, _, rows = d_q.shape
    width = h_t.shape[0]
    some = 4
    here = pl.BlockSpec((some, HD, rows), lambda i: (i, 0, 0))
    gain = pl.BlockSpec((some, HD, 1), lambda i: (i, 0, 0))
    columns = 3 * some * HD
    return pl.pallas_call(
        post_kernel,
        grid=(heads // some,),
        in_specs=[here] * 5
        + [pl.BlockSpec((some, HD, 8), lambda i: (i, 0, 0))]
        + [pl.BlockSpec((2, some, 1, rows), lambda i: (0, i, 0, 0)), fixed(h_t.shape)],
        out_specs=[
            pl.BlockSpec((3, some, HD, rows), lambda i: (0, i, 0, 0)),
            gain,
            gain,
            pl.BlockSpec((width, columns), lambda i: (0, i)),
        ],
        out_shape=[
            jax.ShapeDtypeStruct((3, heads, HD, rows), BF16),
            jax.ShapeDtypeStruct((heads, HD, 1), F32),
            jax.ShapeDtypeStruct((heads, HD, 1), F32),
            jax.ShapeDtypeStruct((width, 3 * heads * HD), F32),
        ],
        compiler_params=params(),
        cost_estimate=pl.CostEstimate(
            flops=6 * rows * width * heads * HD,
            bytes_accessed=30 * rows * heads * HD,
            transcendentals=0,
        ),
        name="post",
    )(d_q, d_k, d_v, q, k, gains, scales, h_t)


def token_grads(d, w, x, dx1, gain):
    d_h = mul(w, d.reshape(-1, d.shape[-1]), NN).T
    unit, scale = norm(x.astype(F32), -1)
    d_x = dx1 + norm_back(d_h * gain, unit, scale, -1)
    dgain = jnp.sum(d_h * unit, axis=0, keepdims=True)
    dbias = jnp.sum(d_h, axis=0, keepdims=True)
    return d_x.astype(BF16), dgain, dbias


def last_kernel(d_ref, w_ref, x_ref, dx1_ref, vec_ref, out_ref, dgain_ref, dbias_ref):
    out_ref[...], dgain, dbias = token_grads(
        d_ref[...], w_ref[...], x_ref[...], dx1_ref[...], vec_ref[0:1, :]
    )
    first = pl.program_id(0) == 0
    dgain_ref[...] = jnp.where(first, dgain, dgain_ref[...] + dgain)
    dbias_ref[...] = jnp.where(first, dbias, dbias_ref[...] + dbias)


def last(d, w, x, dx1, vectors):
    rows, width = x.shape
    block = math.gcd(rows, 256)
    row = pl.BlockSpec((block, width), lambda i: (i, 0))
    return pl.pallas_call(
        last_kernel,
        grid=(rows // block,),
        in_specs=[
            pl.BlockSpec(d.shape[:3] + (block,), lambda i: (0, 0, 0, i)),
            fixed(w.shape),
            row,
            row,
            fixed(vectors.shape),
        ],
        out_specs=[row, fixed((1, width)), fixed((1, width))],
        out_shape=[
            jax.ShapeDtypeStruct((rows, width), BF16),
            jax.ShapeDtypeStruct((1, width), F32),
            jax.ShapeDtypeStruct((1, width), F32),
        ],
        compiler_params=params(),
        name="last",
    )(d, w, x, dx1, vectors)


class Here:
    def __init__(self):
        wide, self.y = lax.axis_index("wide"), lax.axis_index("blk")
        self.core, self.x, self.z = wide % 2, wide // 2 % 2, wide // 4

    def device(self, z=None, x=None, core=None, y=None):
        z = self.z if z is None else z
        x = self.x if x is None else x
        core = self.core if core is None else core
        return (z * 4 + x * 2 + core, self.y if y is None else y)

    def other_core(self):
        return self.device(core=1 - self.core)

    def at(self, kind, k):
        z = self.z
        if kind == "column":
            return {"z": (z, z + 1 - 2 * (z % 2), (z + 2) % 4, 3 - z)[k]}
        x = 1 - self.x if k % 2 else self.x
        y = 1 - self.y if k // 2 else self.y
        return {"plane": {"x": x, "y": y}, "x": {"x": x}, "y": {"y": 1 - self.y if k else self.y}}[kind]

    def partner(self, kind, k):
        return self.device(**self.at(kind, k))

    def partners(self):
        every = [self.partner(kind, k) for kind in ("plane", "column") for k in (1, 2, 3)]
        return [self.other_core()] + every

    def part(self, ref, axes, kind, k):
        where = self.at(kind, k)
        return ref.at[tuple(where.get(axis, slice(None)) for axis in axes)]


def greet(others):
    barrier = pltpu.get_barrier_semaphore()
    for other in others:
        pl.semaphore_signal(barrier, inc=1, device_id=other, device_id_type=MESH)
    pl.semaphore_wait(barrier, len(others))


def remote(source, target, sems, at, to):
    return pltpu.make_async_remote_copy(
        src_ref=source,
        dst_ref=target,
        send_sem=sems[0].at[at],
        recv_sem=sems[1].at[at],
        device_id=to,
        device_id_type=MESH,
    )


class Sum:
    def __init__(self, here, stages, give, keep, refs):
        self.here, self.stages, self.give = here, stages, give
        count = len(stages)
        self.held, self.came = list(refs[: count + 1]), refs[count + 1 : 2 * count + 2]
        self.sems = refs[2 * count + 2 : 2 * count + 4]
        self.keep = self.held[0] if keep is None else keep
        self.axes = ["zxy"]
        for stage in stages:
            gone = {"plane": "xy", "column": "z"}.get(stage, stage)
            self.axes.append("".join(axis for axis in self.axes[-1] if axis not in gone))

    def copies(self, stage):
        here = self.here
        if stage == 0:
            return [remote(self.give, self.came[0], self.sems, 0, here.other_core())]
        kind = self.stages[stage - 1]
        return [
            remote(
                here.part(self.held[stage - 1], self.axes[stage - 1], kind, k),
                self.came[stage].at[k - 1],
                self.sems,
                3 * stage - 3 + k,
                here.partner(kind, k),
            )
            for k in range(1, self.came[stage].shape[0] + 1)
        ]

    def start(self, stage):
        for copy in self.copies(stage):
            copy.start()

    def wait(self, stage):
        for copy in self.copies(stage):
            copy.wait()

    def add(self, stage, landed=False):
        if not landed:
            self.wait(stage)
        if stage == 0:
            terms = [self.keep, self.came[0]]
        else:
            kind = self.stages[stage - 1]
            terms = [self.here.part(self.held[stage - 1], self.axes[stage - 1], kind, 0)]
            terms += [self.came[stage].at[k] for k in range(self.came[stage].shape[0])]
        if stage == len(self.stages):
            return sum(term[...].astype(F32) for term in terms)
        target = self.held[stage]

        def body(i, _):
            target[i] = sum(term[i].astype(F32) for term in terms).astype(target.dtype)
            return 0

        lax.fori_loop(0, target.shape[0], body, 0)

    def go(self, stage):
        self.add(stage)
        self.start(stage + 1)


def sum_scratch(stages, tail, kind=BF16):
    left = {"z": 4, "x": 2, "y": 2}
    held, came = [tuple(left.values())], [tuple(left.values())]
    for stage in stages:
        partners = {"plane": 3, "column": 3}.get(stage, 1)
        for axis in {"plane": "xy", "column": "z"}.get(stage, stage):
            left.pop(axis)
        held.append(tuple(left.values()))
        came.append((partners,) + held[-1])
    held[-1] = (1,)
    shapes = [pltpu.VMEM(shape + tail, kind) for shape in held[:-1] + [(1,)] + came]
    shapes[len(stages)] = pltpu.VMEM((8, 128), kind)
    return shapes + [pltpu.SemaphoreType.DMA((3 * len(stages) + 1,))] * 2


BATCH = 4


def head_back(here, h, ins, far_out, far_in, far_sems, kept):
    e_far, e_near, do_ref, o_ref, linv_ref, q_ref, k_ref, k_far, v_far, v_near = ins
    low, do = scaled_gradient(do_ref, o_ref, linv_ref, 0)
    q = q_ref[h]
    slot = h % BATCH
    keys = k_far.shape[2]
    bk = key_block(keys)
    acc = None
    for i in range(keys // bk):
        cut = slice(i * bk, (i + 1) * bk)
        part, d_k, d_v = block_back(
            e_far[0, cut, :], low, do, q, k_far[0, :, cut], v_far[0, :, cut]
        )
        acc = part if acc is None else acc + part
        far_out[slot, 0, :, cut] = d_k.astype(BF16)
        far_out[slot, 1, :, cut] = d_v.astype(BF16)
    remote(far_out.at[slot], far_in.at[h], far_sems, h, here.other_core()).start()
    for i in range(keys // bk):
        cut = slice(i * bk, (i + 1) * bk)
        part, kept[slot, 1, :, cut], kept[slot, 2, :, cut] = block_back(
            e_near[0, cut, :], low, do, q, k_ref[h, :, cut], v_near[0, :, cut]
        )
        acc = acc + part
    kept[slot, 0] = acc


DOWN_STAGES = [("plane", "column"), ("x", "column", "y")]
UP_STAGES = [("column", "plane"), ("column", "plane"), ("plane", "column"), ("x", "column", "y")]
TWO = ("plane", "column")


def backward_all_kernel(*refs):
    attn, refs = refs[:10], refs[10:]
    gains_ref, scale_ref, h_ref, *refs = refs
    keep_up, keep_down, keep_out, give_out, came_up, came_down, *refs = refs
    d_ref, sum_q_ref, sum_k_ref, keep_c, give_c, *refs = refs
    up_out, down_out, out_out, qkv_a, some_b, *refs = refs
    far_out, far_in, far_send, far_recv, kept, load_sem, *refs = refs
    here = Here()
    step = pl.program_id(0)
    far_sems = (far_send, far_recv)

    def take(stages, give=None):
        nonlocal refs
        count = 2 * len(stages) + 4
        mine, refs = refs[:count], refs[count:]
        return Sum(here, stages, give, None, mine)

    half = keep_down.shape[-1] // 2
    downs, ups, loads = [], [], []
    for i, stages in enumerate(DOWN_STAGES):
        cut = (slice(None),) * 4 + (pl.ds(i * half, half),)
        downs.append(take(stages))
        loads += [(keep_down.at[cut], downs[-1].held[0]), (came_down.at[cut], downs[-1].came[0])]
    for i, stages in enumerate(UP_STAGES):
        ups.append(take(stages))
        loads += [(keep_up.at[i], ups[-1].held[0]), (came_up.at[i], ups[-1].came[0])]
    out = take(TWO, give_out)
    loads.append((keep_out, out.held[0]))
    loads = [pltpu.make_async_copy(*load, load_sem.at[i]) for i, load in enumerate(loads)]
    give_a, give_b, *refs = refs
    a, b = take(TWO, give_a), take(("x",), give_b)

    @pl.when(step == 0)
    def _():
        greet(here.partners())
        out.start(0)
        for load in loads:
            load.start()

    def far_copy(h):
        return remote(far_out.at[h % BATCH], far_in.at[h], far_sems, h, here.other_core())

    @pl.when((step % BATCH == 0) & (step > 0))
    def _():
        base = step - BATCH
        for i in range(BATCH):
            far_copy(base + i).wait()
        for i in range(0, BATCH, 2):
            two = pl.ds(base + i, 2)
            some = slice(i, i + 2)
            d_k = kept[some, 1] + far_in[two, 0].astype(F32)
            d_v = kept[some, 2] + far_in[two, 1].astype(F32)
            d, sum_q, sum_k = head_backs(
                kept[some, 0],
                d_k,
                d_v,
                attn[5][two],
                attn[6][two],
                gains_ref[some],
                scale_ref[0, some],
                scale_ref[1, some],
            )
            d_ref[:, some] = d
            sum_q_ref[some] = sum_q
            sum_k_ref[some] = sum_k
        grad = mul(h_ref[...], d_ref[...].reshape(-1, d_ref.shape[-1]), NT)
        for i, (keep, give) in enumerate(
            ((a.held[0], give_a), (b.held[0], give_b), (keep_c, give_c))
        ):

            @pl.when(step == BATCH * (i + 1))
            def _():
                spread(grad, here.core, keep, give, 8)
                if i < 2:
                    (a, b)[i].start(0)

    @pl.when(step < H)
    def _():
        head_back(here, step, attn, far_out, far_in, far_sems, kept)

    def enter(total, first):
        for load in loads[first : first + 2]:
            load.wait()
        total.add(0, landed=True)

    @pl.when(step == 0)
    def _():
        enter(downs[1], 2)
        downs[1].start(1)
        enter(ups[3], 10)
        ups[3].start(1)
        enter(ups[0], 4)
        ups[0].start(1)
        enter(ups[1], 6)
        ups[1].start(1)

    @pl.when(step == 1)
    def _():
        enter(downs[0], 0)
        enter(ups[2], 8)
        loads[12].wait()
        out.add(0)

    @pl.when(step == 3)
    def _():
        for total in (downs[0], ups[2], out):
            total.start(1)

    @pl.when(step == 4)
    def _():
        downs[1].go(1)
        ups[3].go(1)

    @pl.when(step == 5)
    def _():
        ups[0].go(1)
        ups[1].go(1)
        a.add(0)

    @pl.when(step == 8)
    def _():
        for total in (downs[0], ups[2], out):
            total.go(1)
        a.start(1)

    @pl.when(step == 9)
    def _():
        downs[1].go(2)
        ups[3].go(2)
        b.go(0)

    @pl.when(step == 10)
    def _():
        a.go(1)

    @pl.when(step == H)
    def _():
        wide = up_out.shape[1] // len(ups)
        for i, total in enumerate(ups):
            unfold(up_out, total.add(len(total.stages)), i * wide)
        for i, total in enumerate(downs):
            down_out[:, i * half : (i + 1) * half] = total.add(len(total.stages))
        unfold(out_out, out.add(2))
        unfold(qkv_a, a.add(2))
        some_b[...] = b.add(1).astype(BF16)


def once(shape):
    return pl.BlockSpec(shape, lambda *_: (0,) * len(shape), pipeline_mode=pl.Buffered(1))


def backward_all(e_far, e_near, d_o, o, linv, q, k, k_far, v_far, v, gains, scales, h_t, grads):
    _, keys, rows = e_far.shape
    width = h_t.shape[0]

    def head(*tail):
        return pl.BlockSpec((1,) + tail, lambda s: (jnp.minimum(s, H - 1),) + (0,) * len(tail))

    def batch(s):
        return jnp.maximum(s // BATCH - 1, 0)

    gain = pl.BlockSpec((BATCH, HD, 1), lambda s: (batch(s), 0, 0))
    specs = [head(keys, rows), head(keys, rows), head(HD, rows), head(HD, rows), head(8, rows)]
    specs += [once(q.shape), once(k.shape), head(HD, keys), head(HD, keys), head(HD, keys)]
    specs.append(pl.BlockSpec((BATCH, HD, 8), lambda s: (batch(s), 0, 0)))
    specs.append(pl.BlockSpec((2, BATCH, 1, rows), lambda s: (0, batch(s), 0, 0)))
    specs.append(once(h_t.shape))
    specs += [ANYWHERE] * 6
    shard, chunk = width // 32, grads[0].shape[-1]
    down_rows, half = grads[1].shape[-2], width // 2
    part = (16, 3 * BATCH * HD * 3 // 2)
    third = jax.ShapeDtypeStruct((4, 2, 2) + part, BF16)
    outs = [
        jax.ShapeDtypeStruct((3, H, HD, rows), BF16),
        jax.ShapeDtypeStruct((H, HD, 1), F32),
        jax.ShapeDtypeStruct((H, HD, 1), F32),
        third,
        third,
        jax.ShapeDtypeStruct((shard, len(UP_STAGES) * chunk * 2 // 3), F32),
        jax.ShapeDtypeStruct((down_rows, width), F32),
        jax.ShapeDtypeStruct((shard, width), F32),
        jax.ShapeDtypeStruct((shard, 3 * BATCH * HD), F32),
        jax.ShapeDtypeStruct((4, 2) + part, BF16),
    ]
    out_specs = [pl.BlockSpec((3, BATCH, HD, rows), lambda s: (0, batch(s), 0, 0)), gain, gain]
    out_specs += [once(a.shape) for a in outs[3:]]
    scratch = [
        pltpu.VMEM((BATCH, 2, HD, keys), BF16),
        pltpu.VMEM((H, 2, HD, keys), BF16),
        pltpu.SemaphoreType.DMA((H,)),
        pltpu.SemaphoreType.DMA((H,)),
        pltpu.VMEM((BATCH, 3, HD, rows), F32),
        pltpu.SemaphoreType.DMA((13,)),
    ]
    for stages in DOWN_STAGES:
        scratch += sum_scratch(stages, (down_rows, half))
    for stages in UP_STAGES:
        scratch += sum_scratch(stages, (16, chunk))
    scratch += sum_scratch(TWO, (16, width * 3 // 2))
    scratch += [pltpu.VMEM((4, 2, 2) + part, BF16)] * 2
    scratch += sum_scratch(TWO, part) + sum_scratch(("x",), part)
    return pl.pallas_call(
        backward_all_kernel,
        grid=(H + 1,),
        in_specs=specs,
        out_specs=out_specs,
        out_shape=outs,
        scratch_shapes=scratch,
        compiler_params=pltpu.CompilerParams(
            vmem_limit_bytes=61 * 2**20, collective_id=0, has_side_effects=True
        ),
        name="backward_all",
    )(e_far, e_near, d_o, o, linv, q, k, k_far, v_far, v, gains, scales, h_t, *grads)


def front_kernel(*refs):
    all_ref, vec_ref, here_ref, w_ref, *refs = refs
    h_ref, q_ref, k_ref, v_ref, scale_ref, x_ref, mq_ref, near_ref, far_ref, gains_ref, *refs = refs
    k_far, v_far, *refs = refs
    w_t, came, len_came, len_send, len_recv, row_send, row_recv, k_send, k_recv, v_send, v_recv = refs
    here = Here()
    step = pl.program_id(0)
    steps = pl.num_programs(0)
    block, width = here_ref.shape
    rows = all_ref.shape[0]
    swapped = here.core != here.y
    opposite = here.device(core=here.y, y=here.core)

    def move(i):
        cut = pl.ds(i * block, block)
        return remote(all_ref.at[cut], came.at[cut], (row_send, row_recv), i, opposite)

    move_lengths = remote(vec_ref, len_came, (len_send, len_recv), 0, opposite)

    def give(i):
        cut = (slice(None), slice(None), pl.ds(pl.multiple_of(i * block, block), block))
        to = here.other_core()
        return [
            remote(k_ref.at[cut], k_far.at[cut], (k_send, k_recv), i, to),
            remote(v_ref.at[cut], v_far.at[cut], (v_send, v_recv), i, to),
        ]

    @pl.when(step == 0)
    def _():
        greet([here.other_core(), here.device(core=1 - here.core, y=1 - here.y)])

        @pl.when(swapped)
        def _():
            move_lengths.start()
            for i in range(rows // block):
                move(i).start()

        for i in range(0, w_ref.shape[1], width // 3):
            w_t[i : i + width // 3, :] = w_ref[:, i : i + width // 3].T

        @pl.when(swapped)
        def _():
            move_lengths.wait()

        @pl.when(jnp.logical_not(swapped))
        def _():
            len_came[...] = vec_ref[...]

        gains_ref[...] = gains_table(vec_ref[...])
        lengths = len_came[LENGTHS : LENGTHS + 1, :]
        row = lax.broadcasted_iota(jnp.int32, (AUG, rows), 0)
        spot = lax.broadcasted_iota(jnp.int32, (AUG, rows), 1).astype(F32)

        def inside(first):
            found = jnp.zeros((AUG, rows), jnp.int32)
            begin = jnp.zeros((1, 1), F32)
            where = spot + (first * 1).astype(F32)
            for c in range(SEQS):
                end = begin + lengths[:, c : c + 1]
                hit = (row == c) & (where >= begin) & (where < end)
                found = jnp.where(hit, 1, found)
                begin = end
            return found

        near = inside(here.core * rows)
        near_ref[...] = near.astype(F32).astype(BF16)
        mq_ref[...] = jnp.where(near == 1, 0.0, BLOCKED).astype(BF16)
        far_ref[...] = inside((1 - here.core) * rows).astype(F32).astype(BF16)

    @pl.when(swapped)
    def _():
        move(step).wait()
        x_ref[...] = came[pl.ds(pl.multiple_of(step * block, block), block), :]

    @pl.when(jnp.logical_not(swapped))
    def _():
        x_ref[...] = here_ref[...]

    h = normed(x_ref[...], vec_ref[0:1, :], vec_ref[1:2, :])
    h_ref[...] = h.T
    q, k, v, scale_q, scale_k = heads_of(h, w_t, gains_ref)
    at = pl.ds(pl.multiple_of(step * block, block), block)
    k_ref[:, :, at] = k
    v_ref[:, :, at] = v
    for copy in give(step):
        copy.start()
    q_ref[...] = q
    scale_ref[0] = scale_q
    scale_ref[1] = scale_k

    @pl.when(step == steps - 1)
    def _():
        for i in range(rows // block):
            for copy in give(i):
                copy.wait()


SEQS = 6
LENGTHS = 6


def gains_table(vectors):
    width = vectors.shape[1]
    gain_q, gain_k = vectors[4:5, :], vectors[5:6, :]
    folded = gain_q * (LOG2E / math.sqrt(HD))
    table = [folded, gain_k, 1.0 / folded, 1.0 / gain_k, gain_q, gain_k]
    table.append(jnp.zeros((122, width), F32))
    return jnp.concatenate(table, axis=0).T[:, :8].reshape(H, HD, 8)


def front(tokens, vectors, w):
    rows, width = tokens.shape
    block = math.gcd(rows, 256)
    steps = rows // block
    row = pl.BlockSpec((block, width), lambda i: (i, 0))
    head = pl.BlockSpec((H, HD, block), lambda i: (0, 0, i))
    heads = jax.ShapeDtypeStruct((H, HD, rows), BF16)
    mask = jax.ShapeDtypeStruct((AUG, rows), BF16)
    return pl.pallas_call(
        front_kernel,
        grid=(steps,),
        in_specs=[ANYWHERE, once(vectors.shape), row, once(w.shape)],
        out_specs=[
            pl.BlockSpec((width, block), lambda i: (0, i)),
            head,
            once(heads.shape),
            once(heads.shape),
            pl.BlockSpec((2, H, 1, block), lambda i: (0, 0, 0, i)),
            row,
            once(mask.shape),
            once(mask.shape),
            once(mask.shape),
            once((H, HD, 8)),
            ANYWHERE,
            ANYWHERE,
        ],
        out_shape=[
            jax.ShapeDtypeStruct((width, rows), BF16),
            heads,
            heads,
            heads,
            jax.ShapeDtypeStruct((2, H, 1, rows), F32),
            jax.ShapeDtypeStruct((rows, width), BF16),
            mask,
            mask,
            mask,
            jax.ShapeDtypeStruct((H, HD, 8), F32),
            heads,
            heads,
        ],
        scratch_shapes=[
            pltpu.VMEM((w.shape[1], width), BF16),
            pltpu.VMEM((rows, width), BF16),
            pltpu.VMEM(vectors.shape, F32),
            pltpu.SemaphoreType.DMA((1,)),
            pltpu.SemaphoreType.DMA((1,)),
        ]
        + [pltpu.SemaphoreType.DMA((steps,))] * 6,
        compiler_params=params(collective_id=3, has_side_effects=True),
        cost_estimate=pl.CostEstimate(
            flops=2 * rows * w.size, bytes_accessed=12 * rows * width, transcendentals=0
        ),
        name="front",
    )(tokens, vectors, tokens, w)


REST_STAGES = [("column", "plane"), ("x", "column", "y")]
TABLE_STAGES = ("column", "plane")


def tail_kernel(*refs):
    d_ref, w_ref, x_ref, dx1_ref, vec_ref, *refs = refs
    sum_q_ref, sum_k_ref, dgain2_ref, dbias2_ref, keep_ref, some_ref, give_ref, *refs = refs
    out_ref, qkv_b, qkv_c, table_ref, *refs = refs
    made, vectors, keep_t, give_t, stay_sem, swap_send, swap_recv, *refs = refs
    here = Here()
    step = pl.program_id(0)
    steps = pl.num_programs(0)
    block = x_ref.shape[0]
    swapped = here.core != here.y
    opposite = here.device(core=here.y, y=here.core)
    parts, start = [], 0
    for stages in REST_STAGES:
        count = 2 * len(stages) + 4
        size = refs[0].shape[-1]
        cut = (slice(None),) * 4 + (pl.ds(start, size),)
        parts.append(Sum(here, stages, give_ref.at[cut], keep_ref.at[cut], refs[:count]))
        refs, start = refs[count:], start + size
    table = Sum(here, TABLE_STAGES, give_t, keep_t, refs[:8])
    other = Sum(here, REST_STAGES[1], None, None, refs[8:])
    other.held[1] = some_ref

    @pl.when(step == 0)
    def _():
        greet(here.partners() + [here.device(core=1 - here.core, y=1 - here.y)])
        other.start(2)
        for part in parts:
            part.start(0)

    def stay(i):
        cut = pl.ds(i * block, block)
        return pltpu.make_async_copy(made.at[cut], out_ref.at[cut], stay_sem.at[i])

    def move(i):
        cut = pl.ds(i * block, block)
        return remote(made.at[cut], out_ref.at[cut], (swap_send, swap_recv), i, opposite)

    new, dgain, dbias = token_grads(
        d_ref[...], w_ref[...], x_ref[...], dx1_ref[...], vec_ref[0:1, :]
    )
    made[pl.ds(pl.multiple_of(step * block, block), block), :] = new
    first = step == 0
    vectors[0:1, :] = jnp.where(first, dgain, vectors[0:1, :] + dgain)
    vectors[1:2, :] = jnp.where(first, dbias, vectors[1:2, :] + dbias)

    @pl.when(swapped)
    def _():
        move(step).start()

    @pl.when(jnp.logical_not(swapped))
    def _():
        stay(step).start()

    @pl.when(step == 0)
    def _():
        for part in parts:
            part.go(0)

    @pl.when(step == 2)
    def _():
        parts[1].go(1)

    @pl.when(step == steps - 1)
    def _():
        width = x_ref.shape[1]
        rows = [vectors[0:1, :], vectors[1:2, :], dgain2_ref[...], dbias2_ref[...]]
        rows.append(jnp.zeros((124, width), F32))
        columns = jnp.concatenate(rows, axis=0).T
        lane = lax.broadcasted_iota(jnp.int32, columns.shape, 1)
        columns = jnp.where(lane == 4, sum_q_ref[...].reshape(width, 1), columns)
        columns = jnp.where(lane == 5, sum_k_ref[...].reshape(width, 1), columns)
        columns = columns.reshape(8, 2, 2, width // 32, 128)
        mine = here.core == 0
        keep_t[...] = jnp.where(mine, columns[:, 0], columns[:, 1]).reshape(keep_t.shape)
        give_t[...] = jnp.where(mine, columns[:, 1], columns[:, 0]).reshape(keep_t.shape)
        table.start(0)
        parts[0].go(1)
        table.go(0)
        other.go(2)
        table.go(1)
        parts[1].go(2)
        unfold(qkv_b, other.add(3))
        table_ref[...] = table.add(2)
        unfold(qkv_c, jnp.concatenate([part.add(len(part.stages)) for part in parts], axis=-1))

        @pl.when(swapped)
        def _():
            for i in range(steps):
                move(i).wait()

        @pl.when(jnp.logical_not(swapped))
        def _():
            for i in range(steps):
                stay(i).wait()


def tail(d, w, x, dx1, vectors, sum_q, sum_k, dgain2, dbias2, keep, some, give):
    rows, width = x.shape
    block = math.gcd(rows, 256)
    steps = rows // block
    row = pl.BlockSpec((block, width), lambda i: (i, 0))
    shard = width // 32
    part = keep.shape[-2:]
    return pl.pallas_call(
        tail_kernel,
        grid=(steps,),
        in_specs=[
            pl.BlockSpec(d.shape[:3] + (block,), lambda i: (0, 0, 0, i)),
            once(w.shape),
            row,
            row,
            once(vectors.shape),
            once(sum_q.shape),
            once(sum_k.shape),
            once(dgain2.shape),
            once(dbias2.shape),
            once(keep.shape),
            once(some.shape),
            ANYWHERE,
        ],
        out_specs=[ANYWHERE] + [once((shard, 3 * BATCH * HD))] * 2 + [once((shard, 128))],
        out_shape=[
            jax.ShapeDtypeStruct((rows, width), BF16),
            jax.ShapeDtypeStruct((shard, 3 * BATCH * HD), F32),
            jax.ShapeDtypeStruct((shard, 3 * BATCH * HD), F32),
            jax.ShapeDtypeStruct((shard, 128), F32),
        ],
        scratch_shapes=[
            pltpu.VMEM((rows, width), BF16),
            pltpu.VMEM((8, width), F32),
            pltpu.VMEM((4, 2, 2, shard, 128), F32),
            pltpu.VMEM((4, 2, 2, shard, 128), F32),
            pltpu.SemaphoreType.DMA((steps,)),
            pltpu.SemaphoreType.DMA((steps,)),
            pltpu.SemaphoreType.DMA((steps,)),
            *sum_scratch(REST_STAGES[0], (part[0], part[1] // 3)),
            *sum_scratch(REST_STAGES[1], (part[0], part[1] * 2 // 3)),
            *sum_scratch(TABLE_STAGES, (shard, 128), F32),
            *sum_scratch(REST_STAGES[1], part),
        ],
        compiler_params=pltpu.CompilerParams(
            vmem_limit_bytes=VMEM_LIMIT, collective_id=1, has_side_effects=True
        ),
        name="tail",
    )(d, w, x, dx1, vectors, sum_q, sum_k, dgain2, dbias2, keep, some, give)


def finish_kernel(here_ref, came_ref, tokens_ref, *refs):
    qkvs, ins, outs = refs[:3], refs[3:6], refs[6:]
    here = Here()
    swapped = here.core != here.y

    @pl.when(swapped)
    def _():
        outs[0][...] = came_ref[...]

    @pl.when(jnp.logical_not(swapped))
    def _():
        outs[0][...] = here_ref[...]

    outs[1][...] = tokens_ref[...]
    some = BATCH * HD

    @pl.when(pl.program_id(0) == 0)
    def _():
        for g in range(3):
            for part in range(3):
                at = (part * 3 + g) * some
                outs[2][:, at : at + some] = qkvs[g][:, part * some : (part + 1) * some]
        for source, target in zip(ins, outs[3:]):
            target[...] = source[...]


def finish(output, came, grad_tokens, qkvs, out, up, down):
    rows, width = output.shape
    steps = 4
    small = [jax.ShapeDtypeStruct((out.shape[0], 9 * BATCH * HD), F32), out, up, down]
    row = pl.BlockSpec((rows // steps, width), lambda i: (i, 0))
    return pl.pallas_call(
        finish_kernel,
        grid=(steps,),
        in_specs=[row] * 3 + [once(a.shape) for a in (*qkvs, out, up, down)],
        out_specs=[row] * 2 + [once(a.shape) for a in small],
        out_shape=[
            jax.ShapeDtypeStruct(a.shape, a.dtype) for a in (output, grad_tokens, *small)
        ],
        compiler_params=params(),
        name="finish",
    )(output, came, grad_tokens, *qkvs, out, up, down)


def place(index):
    return index // 8, index // 4 % 2, index // 2 % 2, index % 2


def device(z, x, core, y):
    return ((z * 2 + x) * 2 + core) * 2 + y


def pairs(other):
    every = [(i, device(*other(*place(i)))) for i in range(32)]
    return [(i, j) for i, j in every if i != j]


SWAP = pairs(lambda z, x, c, y: (z, x, y, c))


def send(value, where):
    return lax.ppermute(value, AXES, where)


def after(values, *done):
    return lax.optimization_barrier((values, done))[0]


def segments(lengths, group, mine, rows):
    count = lengths.shape[1]
    at = jnp.arange(count)
    ends = jnp.sum(jnp.where(at[:, None] <= at[None, :], lengths[0][:, None], 0), axis=0)
    spots = jnp.arange(group, dtype=jnp.int32)
    segment = jnp.sum((spots[None, :] >= ends[:, None]).astype(jnp.int32), axis=0)
    is_in = jnp.arange(AUG)[:, None] == segment[None, :]
    mask_k = is_in.astype(BF16)
    mask_q = jnp.where(is_in, 0.0, BLOCKED).astype(BF16)
    mask_q = lax.dynamic_slice_in_dim(mask_q, mine * rows, rows, axis=1)
    return mask_q, mask_k


def ungroup(grads):
    parts = [g.reshape(-1, 3, BATCH * HD) for g in grads]
    return jnp.concatenate(parts, axis=2).reshape(parts[0].shape[0], -1)


def on_chips(tokens, vectors, lengths, w_qkv, w_out, w_up, w_down, cotangent):
    rows, width = tokens.shape
    h_t, q, k, v, scales, tokens, mask_q, mask_near, mask_far, gains, k_far, v_far = front(
        tokens, vectors, w_qkv
    )
    came = send(after(cotangent, tokens), SWAP)
    o, linv, e_near, e_far = attend(q, mask_q, [(k, v, mask_near), (k_far, v_far, mask_far)])
    output, dx1, d_o, dgain2, dbias2, *grads = middle(
        tokens, o.reshape(width, rows), cotangent, w_out, vectors, w_up, w_down, came
    )
    d_o = d_o.reshape(H, HD, rows)
    output_came = send(output, SWAP)
    d, sum_q, sum_k, keep, give, up, down, out, qkv_a, some = backward_all(
        e_far, e_near, d_o, o, linv, q, k, k_far, v_far, v, gains, scales, h_t, grads
    )
    grad_tokens, qkv_b, qkv_c, table = tail(
        d, w_qkv, tokens, dx1, vectors, sum_q, sum_k, dgain2, dbias2, keep, some, give
    )
    sums = [table[:, i] for i in (0, 1, 4, 5, 2, 3)]
    output, grad_tokens, sum_w_qkv, out, up, down = finish(
        output, output_came, grad_tokens, [qkv_a, qkv_b, qkv_c], out, up, down
    )
    return output, grad_tokens, sums, sum_w_qkv, out, up, down


def anywhere(tokens, vectors, lengths, w_qkv, w_out, w_up, w_down, cotangent):
    rows, width = tokens.shape
    parts = lax.axis_size("blk")
    mask_q, mask_k = segments(lengths, rows * parts, lax.axis_index("blk"), rows)
    h_t, q, k, v, scales = project(tokens, vectors, w_qkv.T, gains_table(vectors))
    k_all = lax.all_gather(k, "blk", axis=2, tiled=True)
    v_all = lax.all_gather(v, "blk", axis=2, tiled=True)
    o, linv, e_all = attend(q, mask_q, [(k_all, v_all, mask_k)])
    output, dx1, d_o, dgain2, dbias2, up, down, out = middle(
        tokens, o.reshape(width, rows), cotangent, w_out, vectors, w_up, w_down
    )
    d_o = d_o.reshape(H, HD, rows)
    d_q, d_k, d_v = attend_back(e_all, d_o, o, linv, q, k_all, v_all)
    pair = jnp.stack([d_k, d_v]).reshape(2, H, HD, parts, rows)
    pair = jnp.transpose(pair, (3, 0, 1, 2, 4)).astype(BF16)
    pair = lax.psum_scatter(pair, "blk", scatter_dimension=0, tiled=False).astype(F32)
    d, sum_q, sum_k, grad = post(
        d_q, pair[0], pair[1], q, k, gains_table(vectors), scales, h_t
    )
    grad_tokens, dgain1, dbias1 = last(d, w_qkv, tokens, dx1, vectors)
    scatter = functools.partial(lax.psum_scatter, axis_name=AXES, scatter_dimension=0, tiled=True)
    sums = [
        scatter(g.reshape(width)) for g in (dgain1, dbias1, sum_q, sum_k, dgain2, dbias2)
    ]
    grad = ungroup(jnp.split(grad, H // BATCH, axis=1))
    return output, grad_tokens, sums, scatter(grad), scatter(out), scatter(up), scatter(down)


def shards(
    tokens,
    lengths,
    ln1_gain,
    ln1_bias,
    w_qkv,
    q_gain,
    k_gain,
    w_out,
    ln2_gain,
    ln2_bias,
    w_up,
    w_down,
    cotangent,
):
    width = tokens.shape[1]
    lengths_row = jnp.pad(lengths[0].astype(F32), (0, width - lengths.shape[1]))
    rows = [ln1_gain, ln1_bias, ln2_gain, ln2_bias, q_gain, k_gain, lengths_row, lengths_row]
    vectors = jnp.stack(rows)
    known = lax.axis_size("blk") == 2 and lax.axis_size("wide") == 16
    run = on_chips if known else anywhere
    output, grad_tokens, sums, s_qkv, s_out, s_up, s_down = run(
        tokens, vectors, lengths, w_qkv, w_out, w_up, w_down, cotangent
    )
    return (
        output,
        grad_tokens,
        sums[0],
        sums[1],
        s_qkv,
        sums[2],
        sums[3],
        s_out,
        sums[4],
        sums[5],
        s_up,
        s_down,
    )


def solution(mesh):
    split = P(AXES, None)
    in_specs = (split, P("wide", None)) + (P(),) * 10 + (split,)
    vector = P(AXES)
    out_specs = (
        split,
        split,
        vector,
        vector,
        split,
        vector,
        vector,
        split,
        vector,
        vector,
        split,
        split,
    )
    return jax.shard_map(shards, mesh=mesh, in_specs=in_specs, out_specs=out_specs, check_vma=False)
```

```python
import functools
import math

import jax
import jax.numpy as jnp
from jax import lax
from jax.experimental import pallas as pl
from jax.experimental.pallas import tpu as pltpu
from jax.sharding import PartitionSpec as P

H = 12
HD = 64
EPS = 1e-06
AXES = ("wide", "blk")
AUG = 16
BLOCKED = -512.0
LOG2E = math.log2(math.e)
NN = (((1,), (0,)), ((), ()))
NT = (((1,), (1,)), ((), ()))
TN = (((0,), (0,)), ((), ()))
TT = (((0,), (1,)), ((), ()))
BF16 = jnp.bfloat16
MESH = pl.DeviceIdType.MESH
F32 = jnp.float32
VMEM_LIMIT = 56 * 2**20


def mul(left, right, dims, kind=F32):
    return lax.dot_general(left, right, dims, preferred_element_type=F32).astype(kind)


def ones_rows(columns):
    return (lax.broadcasted_iota(jnp.int32, (AUG, columns), 0) < 2).astype(BF16)


def key_block(keys):
    return math.gcd(keys, 512)


def forward_kernel(count, *refs):
    q_ref, mq_ref, *refs = refs
    parts, refs = refs[: 3 * count], refs[3 * count :]
    if count == 2:
        own_ref, o_ref, linv_ref, *e_refs, came_ref, send_sem, recv_sem = refs
        here = Here()
        swapped = here.core != here.y
        swap = remote(own_ref, came_ref, (send_sem, recv_sem), 0, here.opposite())

        @pl.when(pl.program_id(0) == 0)
        def _():
            greet([here.opposite()])

            @pl.when(swapped)
            def _():
                swap.start()
    else:
        o_ref, linv_ref, *e_refs = refs
    keys = parts[0].shape[2]
    bk = key_block(keys)
    ones = ones_rows(bk)
    for h in range(q_ref.shape[0]):
        q = jnp.concatenate([q_ref[h], mq_ref[...]], axis=0)
        acc = None
        for p in range(count):
            k_ref, v_ref, mk_ref = parts[3 * p : 3 * p + 3]
            for i in range(keys // bk):
                cut = slice(i * bk, (i + 1) * bk)
                k = jnp.concatenate([k_ref[h, :, cut], mk_ref[:, cut]], axis=0)
                v = jnp.concatenate([v_ref[h, :, cut], ones], axis=0)
                e = jnp.exp2(mul(k, q, TN)).astype(BF16)
                e_refs[p][h, cut, :] = e
                part = mul(v, e, NN)
                acc = part if acc is None else acc + part
        linv = 1.0 / acc[HD : HD + 1]
        o_ref[h] = (acc[:HD] * linv).astype(BF16)
        linv_ref[h] = jnp.broadcast_to(linv, linv_ref.shape[1:])
    if count == 2:

        @pl.when(swapped & (pl.program_id(0) == pl.num_programs(0) - 1))
        def _():
            swap.wait()


def attend(q, mask_q, parts, cotangent=None):
    heads, _, rows = q.shape
    keys = parts[0][0].shape[2]
    some = 2 if len(parts) * keys * rows <= 1 << 21 else 1

    def head(*tail):
        return pl.BlockSpec((some,) + tail, lambda h: (h,) + (0,) * len(tail))

    specs = [head(HD, rows), fixed(mask_q.shape)]
    for part in parts:
        specs += [head(HD, keys), head(HD, keys), fixed(part[2].shape)]
    ins, more_out, more_specs, scratch, more = [], [], [], [], {}
    if cotangent is not None:
        ins = [cotangent]
        specs.append(ANYWHERE)
        more_out, more_specs = [jax.ShapeDtypeStruct(cotangent.shape, BF16)], [ANYWHERE]
        scratch = [pltpu.SemaphoreType.DMA((1,))] * 2
        more = {"collective_id": 4, "has_side_effects": True}
    return pl.pallas_call(
        functools.partial(forward_kernel, len(parts)),
        grid=(heads // some,),
        in_specs=specs,
        out_specs=[head(HD, rows), head(8, rows)] + [head(keys, rows)] * len(parts) + more_specs,
        out_shape=[
            jax.ShapeDtypeStruct((heads, HD, rows), BF16),
            jax.ShapeDtypeStruct((heads, 8, rows), F32),
        ]
        + [jax.ShapeDtypeStruct((heads, keys, rows), BF16)] * len(parts)
        + more_out,
        scratch_shapes=scratch,
        compiler_params=params(**more),
        cost_estimate=pl.CostEstimate(
            flops=heads * rows * keys * len(parts) * 1024,
            bytes_accessed=heads * rows * keys * len(parts) * 2,
            transcendentals=heads * rows * keys * len(parts),
        ),
        name="attend",
    )(q, mask_q, *[a for part in parts for a in part], *ins)


def scaled_gradient(do_ref, o_ref, linv_ref, h):
    low = (do_ref[h] * linv_ref[h, :1]).astype(BF16)
    delta = -jnp.sum(low.astype(F32) * o_ref[h].astype(F32), axis=0, keepdims=True)
    top = delta.astype(BF16).astype(F32)
    row = lax.broadcasted_iota(jnp.int32, (AUG, delta.shape[1]), 0)
    extra = jnp.where(row == 0, top, jnp.where(row == 1, delta - top, 0.0)).astype(BF16)
    return low, jnp.concatenate([low, extra], axis=0)


def block_back(e, low, do, q, k, v):
    v = jnp.concatenate([v, ones_rows(v.shape[1])], axis=0)
    ds = (e.astype(F32) * mul(v, do, TN)).astype(BF16)
    return mul(k, ds, NN), mul(q, ds, NT), mul(low, e, NT)


def backward_kernel(e_ref, do_ref, o_ref, linv_ref, q_ref, k_ref, v_ref, dq_ref, dk_ref, dv_ref):
    keys = k_ref.shape[2]
    bk = key_block(keys)
    low, do = scaled_gradient(do_ref, o_ref, linv_ref, 0)
    acc = None
    for i in range(keys // bk):
        cut = slice(i * bk, (i + 1) * bk)
        part, dk_ref[0, :, cut], dv_ref[0, :, cut] = block_back(
            e_ref[0, cut, :], low, do, q_ref[0], k_ref[0, :, cut], v_ref[0, :, cut]
        )
        acc = part if acc is None else acc + part
    dq_ref[0] = acc


def attend_back(e, do, o, linv, q, k, v):
    heads, keys, rows = e.shape

    def head(*tail):
        return pl.BlockSpec((1,) + tail, lambda h: (h,) + (0,) * len(tail))

    specs = [head(keys, rows), head(HD, rows), head(HD, rows), head(8, rows), head(HD, rows)]
    return pl.pallas_call(
        backward_kernel,
        grid=(heads,),
        in_specs=specs + [head(HD, keys)] * 2,
        out_specs=[head(HD, rows), head(HD, keys), head(HD, keys)],
        out_shape=[
            jax.ShapeDtypeStruct((heads, HD, rows), F32),
            jax.ShapeDtypeStruct((heads, HD, keys), F32),
            jax.ShapeDtypeStruct((heads, HD, keys), F32),
        ],
        compiler_params=params(),
        name="attend_back",
    )(e, do, o, linv, q, k, v)


def norm(value, axis):
    mean = jnp.mean(value, axis=axis, keepdims=True)
    centred = value - mean
    scale = lax.rsqrt(jnp.mean(centred * centred, axis=axis, keepdims=True) + EPS)
    return centred * scale, scale


def norm_back(grad, unit, scale, axis):
    mean = jnp.mean(grad, axis=axis, keepdims=True)
    along = jnp.mean(grad * unit, axis=axis, keepdims=True)
    return scale * (grad - mean - unit * along)


def gelu_parts(u):
    root = math.sqrt(2.0 / math.pi)
    square = u * u
    t = jnp.tanh(u * (root + (root * 0.044715) * square))
    half = 0.5 + 0.5 * t
    slope = half + (u * (0.5 - 0.5 * t * t)) * (root + (3 * root * 0.044715) * square)
    return u * half, slope


def params(**more):
    return pltpu.CompilerParams(vmem_limit_bytes=VMEM_LIMIT, **more)


def fixed(shape):
    return pl.BlockSpec(shape, lambda *_: (0,) * len(shape))


SCALAR = pl.BlockSpec(memory_space=pltpu.SMEM)
ANYWHERE = pl.BlockSpec(memory_space=pl.ANY)


def normed(x, gain, bias):
    return (norm(x.astype(F32), -1)[0] * gain + bias).astype(BF16)


def heads_of(h, w_ref, gains_ref):
    width = h.shape[1]

    def part(i):
        value = mul(w_ref[i * width : (i + 1) * width, :], h, NT)
        return value.reshape(width // HD, HD, h.shape[0])

    unit_k, scale_k = norm(part(1), 1)
    k = (unit_k * gains_ref[:, :, 1:2]).astype(BF16)
    v = part(2).astype(BF16)
    unit_q, scale_q = norm(part(0), 1)
    q = (unit_q * gains_ref[:, :, 0:1]).astype(BF16)
    return q, k, v, scale_q, scale_k


def project_kernel(x_ref, vec_ref, w_ref, gains_ref, h_ref, q_ref, k_ref, v_ref, scale_ref):
    h = normed(x_ref[...], vec_ref[0:1, :], vec_ref[1:2, :])
    h_ref[...] = h.T
    q_ref[...], k_ref[...], v_ref[...], scale_ref[0], scale_ref[1] = heads_of(h, w_ref, gains_ref)


def project(tokens, vectors, w_t, gains):
    rows, width = tokens.shape
    block = math.gcd(rows, 256)
    head = pl.BlockSpec((H, HD, block), lambda i: (0, 0, i))
    head_shape = jax.ShapeDtypeStruct((H, HD, rows), BF16)
    return pl.pallas_call(
        project_kernel,
        grid=(rows // block,),
        in_specs=[pl.BlockSpec((block, width), lambda i: (i, 0))]
        + [fixed(a.shape) for a in (vectors, w_t, gains)],
        out_specs=[
            pl.BlockSpec((width, block), lambda i: (0, i)),
            head,
            head,
            head,
            pl.BlockSpec((2, H, 1, block), lambda i: (0, 0, 0, i)),
        ],
        out_shape=[
            jax.ShapeDtypeStruct((width, rows), BF16),
            head_shape,
            head_shape,
            head_shape,
            jax.ShapeDtypeStruct((2, H, 1, rows), F32),
        ],
        compiler_params=params(),
        name="project",
    )(tokens, vectors, w_t, gains)


def fold(value):
    if value.shape[-2] % 16 == 0:
        return value
    half = value.shape[-1] // 2
    low = value[..., 16:, :]
    low = jnp.concatenate([low[..., :half], low[..., half:]], axis=-2)
    return jnp.concatenate([value[..., :16, :], low], axis=-1)


def unfold(out_ref, value, start=0):
    count = value.shape[-1] * 2 // 3
    half = count // 2
    out_ref[:16, start : start + count] = value[:, :count]
    out_ref[16:, start : start + half] = value[:8, count:]
    out_ref[16:, start + half : start + count] = value[8:, count:]


def spread(value, core, keep_ref, give_ref, lead):
    rows, columns = value.shape
    value = value.reshape((lead, 2, 2, rows // (4 * lead), columns))
    mine = core == 0
    keep = jnp.where(mine, value[:, 0], value[:, 1])
    give = jnp.where(mine, value[:, 1], value[:, 0])
    keep_ref[...] = fold(keep).astype(BF16).reshape(keep_ref.shape)
    give_ref[...] = fold(give).astype(BF16).reshape(give_ref.shape)


def middle_kernel(split, *refs):
    x_ref, o_ref, dy_ref, w_out_ref, vec_ref, w_up_ref, w_down_ref, *refs = refs
    if split:
        dy_here, (dy_came, *refs) = dy_ref, refs
    out_ref, dx1_ref, do_ref, dgain_ref, dbias_ref, *refs = refs
    grads, refs = (refs[:6], refs[6:]) if split else (refs[:3], refs[3:])
    x1_ref, h2_ref, h2t_ref, acc_ref, dh2_ref, g_ref, du_ref, da_ref, *refs = refs
    step = pl.program_id(0)
    rows = x_ref.shape[0]
    block = math.gcd(rows, 256)
    cuts = [slice(i, i + block) for i in range(0, rows, block)]
    if split:
        here = Here()
        keep_up, keep_down, keep_out, give_out, came_up, came_down = grads
        give_up, give_down, up_send, up_recv, down_send, down_recv, dy_ref, dy_sem = refs
        swapped = here.core != here.y

        def copies(f):
            to = here.other_core()
            return [
                remote(give_up.at[f % 2], came_up.at[f], (up_send, up_recv), f, to),
                remote(give_down.at[f % 2], came_down.at[f], (down_send, down_recv), f, to),
            ]

    @pl.when(step == 0)
    def _():
        if split:
            greet([here.other_core()])

            @pl.when(swapped)
            def _():
                pltpu.make_async_copy(dy_came, dy_ref, dy_sem.at[0]).start()

            @pl.when(jnp.logical_not(swapped))
            def _():
                pltpu.make_async_copy(dy_here, dy_ref, dy_sem.at[0]).start()

        for cut in cuts:
            x1 = x_ref[cut, :].astype(F32) + mul(o_ref[:, cut], w_out_ref[...], TN)
            x1_ref[cut, :] = x1
            acc_ref[cut, :] = x1
            h2 = normed(x1, vec_ref[2:3, :], vec_ref[3:4, :])
            h2_ref[cut, :] = h2
            h2t_ref[:, cut] = h2.T
        if split:
            pltpu.make_async_copy(dy_here, dy_ref, dy_sem.at[0]).wait()

    for cut in cuts:
        dy = dy_ref[cut, :]
        value, slope = gelu_parts(mul(h2_ref[cut, :], w_up_ref[...], NN))
        g = value.astype(BF16)
        g_ref[cut, :] = g
        acc_ref[cut, :] += mul(g, w_down_ref[...], NN)
        du = (mul(dy, w_down_ref[...], NT) * slope).astype(BF16)
        du_ref[cut, :] = du
        part = mul(du, w_up_ref[...], NT)
        dh2_ref[cut, :] = jnp.where(step == 0, part, dh2_ref[cut, :] + part)
    grad_up = mul(h2t_ref[...], du_ref[...], NN)
    grad_down = mul(g_ref[...], dy_ref[...], TN)
    if split:

        @pl.when(step >= 2)
        def _():
            for copy in copies(step - 2):
                copy.wait_send()

        spread(grad_up, here.core, keep_up, give_up.at[step % 2], 8)
        spread(grad_down, here.core, keep_down, give_down.at[step % 2], 2)
        for copy in copies(step):
            copy.start()
    else:
        grads[0][...] = grad_up
        grads[1][...] = grad_down

    @pl.when(step == pl.num_programs(0) - 1)
    def _():
        dgain, dbias = 0.0, 0.0
        for cut in cuts:
            out_ref[cut, :] = acc_ref[cut, :].astype(BF16)
            unit, scale = norm(x1_ref[cut, :], -1)
            dh2 = dh2_ref[cut, :]
            dgain += jnp.sum(dh2 * unit, axis=0, keepdims=True)
            dbias += jnp.sum(dh2, axis=0, keepdims=True)
            dx1 = dy_ref[cut, :].astype(F32) + norm_back(dh2 * vec_ref[2:3, :], unit, scale, -1)
            dx1_ref[cut, :] = dx1
            da = dx1.astype(BF16)
            da_ref[cut, :] = da
            do_ref[:, cut] = mul(w_out_ref[...], da, NT)
        dgain_ref[...] = dgain
        dbias_ref[...] = dbias
        grad_out = mul(o_ref[...], da_ref[...], NN)
        if split:
            spread(grad_out, here.core, keep_out, give_out, 8)
            for f in range(FF_STEPS):
                for copy in copies(f):
                    copy.wait_recv()
                    if f >= FF_STEPS - 2:
                        copy.wait_send()
        else:
            grads[2][...] = grad_out


FF_STEPS = 4


def middle(x, o, dy, w_out, vectors, w_up, w_down, came=None):
    rows, width = x.shape
    inner = w_up.shape[1]
    chunk = inner // FF_STEPS
    split = came is not None
    ins = [x, o, dy, w_out, vectors, w_up, w_down]
    specs = [fixed(a.shape) for a in ins[:5]]
    specs += [pl.BlockSpec((width, chunk), lambda f: (0, f)), pl.BlockSpec((chunk, width), lambda f: (f, 0))]
    weights = specs[-2:]
    if split:
        ins.append(came)
        specs[2] = ANYWHERE
        specs.append(ANYWHERE)
    outs = [
        jax.ShapeDtypeStruct((rows, width), BF16),
        jax.ShapeDtypeStruct((rows, width), F32),
        jax.ShapeDtypeStruct((width, rows), F32),
        jax.ShapeDtypeStruct((1, width), F32),
        jax.ShapeDtypeStruct((1, width), F32),
    ]
    out_specs = [fixed(a.shape) for a in outs]
    scratch = [
        pltpu.VMEM((rows, width), F32),
        pltpu.VMEM((rows, width), BF16),
        pltpu.VMEM((width, rows), BF16),
        pltpu.VMEM((rows, width), F32),
        pltpu.VMEM((rows, width), F32),
        pltpu.VMEM((rows, chunk), BF16),
        pltpu.VMEM((rows, chunk), BF16),
        pltpu.VMEM((rows, width), BF16),
    ]
    more = {}
    if split:
        up = (4, 2, 2, 16, chunk * 3 // 2)
        down = (2, 2, inner // 32, width)
        out = jax.ShapeDtypeStruct((4, 2, 2, 16, width * 3 // 2), BF16)
        ups = jax.ShapeDtypeStruct((FF_STEPS,) + up, BF16)
        downs = jax.ShapeDtypeStruct((FF_STEPS,) + down, BF16)
        outs += [ups, downs, out, out, ups, downs]
        out_specs += [pl.BlockSpec((1,) + up, lambda f: (f,) + (0,) * len(up))]
        out_specs += [pl.BlockSpec((1,) + down, lambda f: (f,) + (0,) * len(down))]
        out_specs += [fixed(out.shape), fixed(out.shape), ANYWHERE, ANYWHERE]
        scratch += [pltpu.VMEM((2,) + up, BF16), pltpu.VMEM((2,) + down, BF16)]
        scratch += [pltpu.SemaphoreType.DMA((FF_STEPS,))] * 4
        scratch += [pltpu.VMEM((rows, width), BF16), pltpu.SemaphoreType.DMA((1,))]
        more = {"collective_id": 2, "has_side_effects": True}
    else:
        outs += [jax.ShapeDtypeStruct(a.shape, F32) for a in (w_up, w_down, w_out)]
        out_specs += [*weights, fixed(w_out.shape)]
    return pl.pallas_call(
        functools.partial(middle_kernel, split),
        grid=(FF_STEPS,),
        in_specs=specs,
        out_specs=out_specs,
        out_shape=outs,
        scratch_shapes=scratch,
        compiler_params=params(**more),
        cost_estimate=pl.CostEstimate(
            flops=6 * rows * (2 * w_up.size + w_out.size),
            bytes_accessed=40 * rows * width,
            transcendentals=rows * inner,
        ),
        name="middle",
    )(*ins)


def head_backs(d_q, d_k, d_v, q, k, gains, scale_q, scale_k):
    d_q = d_q * (1.0 / math.sqrt(HD))
    d_k = d_k * (1.0 / LOG2E)
    inv_q, inv_k, gain_q, gain_k = [gains[:, :, i : i + 1] for i in range(2, 6)]
    unit_q = q.astype(F32) * inv_q
    unit_k = k.astype(F32) * inv_k
    sum_q = jnp.sum(d_q * unit_q, axis=2, keepdims=True)
    sum_k = jnp.sum(d_k * unit_k, axis=2, keepdims=True)
    d_q = norm_back(d_q * gain_q, unit_q, scale_q, 1).astype(BF16)
    d_k = norm_back(d_k * gain_k, unit_k, scale_k, 1).astype(BF16)
    return jnp.stack([d_q, d_k, d_v.astype(BF16)]), sum_q, sum_k


def post_kernel(*refs):
    *ins, scale_ref, h_ref, d_ref, sum_q_ref, sum_k_ref, grad_ref = refs
    values = [ref[...] for ref in ins]
    d, sum_q_ref[...], sum_k_ref[...] = head_backs(*values, scale_ref[0], scale_ref[1])
    d_ref[...] = d
    grad_ref[...] = mul(h_ref[...], d.reshape(-1, d.shape[-1]), NT)


def post(d_q, d_k, d_v, q, k, gains, scales, h_t):
    heads, _, rows = d_q.shape
    width = h_t.shape[0]
    some = 4
    here = pl.BlockSpec((some, HD, rows), lambda i: (i, 0, 0))
    gain = pl.BlockSpec((some, HD, 1), lambda i: (i, 0, 0))
    columns = 3 * some * HD
    return pl.pallas_call(
        post_kernel,
        grid=(heads // some,),
        in_specs=[here] * 5
        + [pl.BlockSpec((some, HD, 8), lambda i: (i, 0, 0))]
        + [pl.BlockSpec((2, some, 1, rows), lambda i: (0, i, 0, 0)), fixed(h_t.shape)],
        out_specs=[
            pl.BlockSpec((3, some, HD, rows), lambda i: (0, i, 0, 0)),
            gain,
            gain,
            pl.BlockSpec((width, columns), lambda i: (0, i)),
        ],
        out_shape=[
            jax.ShapeDtypeStruct((3, heads, HD, rows), BF16),
            jax.ShapeDtypeStruct((heads, HD, 1), F32),
            jax.ShapeDtypeStruct((heads, HD, 1), F32),
            jax.ShapeDtypeStruct((width, 3 * heads * HD), F32),
        ],
        compiler_params=params(),
        cost_estimate=pl.CostEstimate(
            flops=6 * rows * width * heads * HD,
            bytes_accessed=30 * rows * heads * HD,
            transcendentals=0,
        ),
        name="post",
    )(d_q, d_k, d_v, q, k, gains, scales, h_t)


def token_grads(d, w, x, dx1, gain):
    d_h = mul(w, d.reshape(-1, d.shape[-1]), NN).T
    unit, scale = norm(x.astype(F32), -1)
    d_x = dx1 + norm_back(d_h * gain, unit, scale, -1)
    dgain = jnp.sum(d_h * unit, axis=0, keepdims=True)
    dbias = jnp.sum(d_h, axis=0, keepdims=True)
    return d_x.astype(BF16), dgain, dbias


def last_kernel(d_ref, w_ref, x_ref, dx1_ref, vec_ref, out_ref, dgain_ref, dbias_ref):
    out_ref[...], dgain, dbias = token_grads(
        d_ref[...], w_ref[...], x_ref[...], dx1_ref[...], vec_ref[0:1, :]
    )
    first = pl.program_id(0) == 0
    dgain_ref[...] = jnp.where(first, dgain, dgain_ref[...] + dgain)
    dbias_ref[...] = jnp.where(first, dbias, dbias_ref[...] + dbias)


def last(d, w, x, dx1, vectors):
    rows, width = x.shape
    block = math.gcd(rows, 256)
    row = pl.BlockSpec((block, width), lambda i: (i, 0))
    return pl.pallas_call(
        last_kernel,
        grid=(rows // block,),
        in_specs=[
            pl.BlockSpec(d.shape[:3] + (block,), lambda i: (0, 0, 0, i)),
            fixed(w.shape),
            row,
            row,
            fixed(vectors.shape),
        ],
        out_specs=[row, fixed((1, width)), fixed((1, width))],
        out_shape=[
            jax.ShapeDtypeStruct((rows, width), BF16),
            jax.ShapeDtypeStruct((1, width), F32),
            jax.ShapeDtypeStruct((1, width), F32),
        ],
        compiler_params=params(),
        name="last",
    )(d, w, x, dx1, vectors)


class Here:
    def __init__(self):
        wide, self.y = lax.axis_index("wide"), lax.axis_index("blk")
        self.core, self.x, self.z = wide % 2, wide // 2 % 2, wide // 4

    def device(self, z=None, x=None, core=None, y=None):
        z = self.z if z is None else z
        x = self.x if x is None else x
        core = self.core if core is None else core
        return (z * 4 + x * 2 + core, self.y if y is None else y)

    def other_core(self):
        return self.device(core=1 - self.core)

    def opposite(self):
        return self.device(core=1 - self.core, y=1 - self.y)

    def at(self, kind, k):
        z = self.z
        if kind == "column":
            return {"z": (z, z + 1 - 2 * (z % 2), (z + 2) % 4, 3 - z)[k]}
        x = 1 - self.x if k % 2 else self.x
        y = 1 - self.y if k // 2 else self.y
        return {"plane": {"x": x, "y": y}, "x": {"x": x}, "y": {"y": 1 - self.y if k else self.y}}[kind]

    def partner(self, kind, k):
        return self.device(**self.at(kind, k))

    def partners(self):
        every = [self.partner(kind, k) for kind in ("plane", "column") for k in (1, 2, 3)]
        return [self.other_core()] + every

    def part(self, ref, axes, kind, k):
        where = self.at(kind, k)
        return ref.at[tuple(where.get(axis, slice(None)) for axis in axes)]


def greet(others):
    barrier = pltpu.get_barrier_semaphore()
    for other in others:
        pl.semaphore_signal(barrier, inc=1, device_id=other, device_id_type=MESH)
    pl.semaphore_wait(barrier, len(others))


def remote(source, target, sems, at, to):
    return pltpu.make_async_remote_copy(
        src_ref=source,
        dst_ref=target,
        send_sem=sems[0].at[at],
        recv_sem=sems[1].at[at],
        device_id=to,
        device_id_type=MESH,
    )


class Sum:
    def __init__(self, here, stages, give, keep, refs):
        self.here, self.stages, self.give = here, stages, give
        count = len(stages)
        self.held, self.came = list(refs[: count + 1]), refs[count + 1 : 2 * count + 2]
        self.sems = refs[2 * count + 2 : 2 * count + 4]
        self.keep = self.held[0] if keep is None else keep
        self.axes = ["zxy"]
        for stage in stages:
            gone = {"plane": "xy", "column": "z"}.get(stage, stage)
            self.axes.append("".join(axis for axis in self.axes[-1] if axis not in gone))

    def copies(self, stage):
        here = self.here
        if stage == 0:
            return [remote(self.give, self.came[0], self.sems, 0, here.other_core())]
        kind = self.stages[stage - 1]
        return [
            remote(
                here.part(self.held[stage - 1], self.axes[stage - 1], kind, k),
                self.came[stage].at[k - 1],
                self.sems,
                3 * stage - 3 + k,
                here.partner(kind, k),
            )
            for k in range(1, self.came[stage].shape[0] + 1)
        ]

    def start(self, stage):
        for copy in self.copies(stage):
            copy.start()

    def wait(self, stage):
        for copy in self.copies(stage):
            copy.wait()

    def add(self, stage, landed=False):
        if not landed:
            self.wait(stage)
        if stage == 0:
            terms = [self.keep, self.came[0]]
        else:
            kind = self.stages[stage - 1]
            terms = [self.here.part(self.held[stage - 1], self.axes[stage - 1], kind, 0)]
            terms += [self.came[stage].at[k] for k in range(self.came[stage].shape[0])]
        if stage == len(self.stages):
            return sum(term[...].astype(F32) for term in terms)
        target = self.held[stage]

        def body(i, _):
            target[i] = sum(term[i].astype(F32) for term in terms).astype(target.dtype)
            return 0

        lax.fori_loop(0, target.shape[0], body, 0)

    def go(self, stage):
        self.add(stage)
        self.start(stage + 1)


def sum_scratch(stages, tail, kind=BF16):
    left = {"z": 4, "x": 2, "y": 2}
    held, came = [tuple(left.values())], [tuple(left.values())]
    for stage in stages:
        partners = {"plane": 3, "column": 3}.get(stage, 1)
        for axis in {"plane": "xy", "column": "z"}.get(stage, stage):
            left.pop(axis)
        held.append(tuple(left.values()))
        came.append((partners,) + held[-1])
    held[-1] = (1,)
    shapes = [pltpu.VMEM(shape + tail, kind) for shape in held[:-1] + [(1,)] + came]
    shapes[len(stages)] = pltpu.VMEM((8, 128), kind)
    return shapes + [pltpu.SemaphoreType.DMA((3 * len(stages) + 1,))] * 2


BATCH = 4


def head_back(here, h, ins, far_out, far_in, far_sems, kept):
    e_far, e_near, do_ref, o_ref, linv_ref, q_ref, k_ref, k_far, v_far, v_near = ins
    low, do = scaled_gradient(do_ref, o_ref, linv_ref, 0)
    q = q_ref[h]
    slot = h % BATCH
    keys = k_far.shape[2]
    bk = key_block(keys)
    acc = None
    for i in range(keys // bk):
        cut = slice(i * bk, (i + 1) * bk)
        part, d_k, d_v = block_back(
            e_far[0, cut, :], low, do, q, k_far[0, :, cut], v_far[0, :, cut]
        )
        acc = part if acc is None else acc + part
        far_out[slot, 0, :, cut] = d_k.astype(BF16)
        far_out[slot, 1, :, cut] = d_v.astype(BF16)
    remote(far_out.at[slot], far_in.at[h], far_sems, h, here.other_core()).start()
    for i in range(keys // bk):
        cut = slice(i * bk, (i + 1) * bk)
        part, kept[slot, 1, :, cut], kept[slot, 2, :, cut] = block_back(
            e_near[0, cut, :], low, do, q, k_ref[h, :, cut], v_near[0, :, cut]
        )
        acc = acc + part
    kept[slot, 0] = acc


DOWN_STAGES = [("plane", "column"), ("x", "column", "y")]
UP_STAGES = [("column", "plane"), ("column", "plane"), ("plane", "column"), ("x", "column", "y")]
TWO = ("plane", "column")


def backward_all_kernel(*refs):
    attn, refs = refs[:10], refs[10:]
    gains_ref, scale_ref, h_ref, *refs = refs
    keep_up, keep_down, keep_out, give_out, came_up, came_down, own_ref, *refs = refs
    d_ref, sum_q_ref, sum_k_ref, keep_c, give_c, *refs = refs
    up_out, down_out, out_out, qkv_a, some_b, swap_ref, *refs = refs
    far_out, far_in, far_send, far_recv, kept, load_sem, swap_send, swap_recv, *refs = refs
    here = Here()
    swap = remote(own_ref, swap_ref, (swap_send, swap_recv), 0, here.opposite())
    step = pl.program_id(0)
    far_sems = (far_send, far_recv)

    def take(stages, give=None):
        nonlocal refs
        count = 2 * len(stages) + 4
        mine, refs = refs[:count], refs[count:]
        return Sum(here, stages, give, None, mine)

    half = keep_down.shape[-1] // 2
    downs, ups, loads = [], [], []
    for i, stages in enumerate(DOWN_STAGES):
        cut = (slice(None),) * 4 + (pl.ds(i * half, half),)
        downs.append(take(stages))
        loads += [(keep_down.at[cut], downs[-1].held[0]), (came_down.at[cut], downs[-1].came[0])]
    for i, stages in enumerate(UP_STAGES):
        ups.append(take(stages))
        loads += [(keep_up.at[i], ups[-1].held[0]), (came_up.at[i], ups[-1].came[0])]
    out = take(TWO, give_out)
    loads.append((keep_out, out.held[0]))
    loads = [pltpu.make_async_copy(*load, load_sem.at[i]) for i, load in enumerate(loads)]
    give_a, give_b, *refs = refs
    a, b = take(TWO, give_a), take(("x",), give_b)

    @pl.when(step == 0)
    def _():
        greet(here.partners() + [here.opposite()])
        out.start(0)

        @pl.when(here.core != here.y)
        def _():
            swap.start()

        for load in loads:
            load.start()

    def far_copy(h):
        return remote(far_out.at[h % BATCH], far_in.at[h], far_sems, h, here.other_core())

    @pl.when((step % BATCH == 0) & (step > 0))
    def _():
        base = step - BATCH
        for i in range(BATCH):
            far_copy(base + i).wait()
        for i in range(0, BATCH, 2):
            two = pl.ds(base + i, 2)
            some = slice(i, i + 2)
            d_k = kept[some, 1] + far_in[two, 0].astype(F32)
            d_v = kept[some, 2] + far_in[two, 1].astype(F32)
            d, sum_q, sum_k = head_backs(
                kept[some, 0],
                d_k,
                d_v,
                attn[5][two],
                attn[6][two],
                gains_ref[some],
                scale_ref[0, some],
                scale_ref[1, some],
            )
            d_ref[:, some] = d
            sum_q_ref[some] = sum_q
            sum_k_ref[some] = sum_k
        grad = mul(h_ref[...], d_ref[...].reshape(-1, d_ref.shape[-1]), NT)
        for i, (keep, give) in enumerate(
            ((a.held[0], give_a), (b.held[0], give_b), (keep_c, give_c))
        ):

            @pl.when(step == BATCH * (i + 1))
            def _():
                spread(grad, here.core, keep, give, 8)
                if i < 2:
                    (a, b)[i].start(0)

    @pl.when(step < H)
    def _():
        head_back(here, step, attn, far_out, far_in, far_sems, kept)

    def enter(total, first):
        for load in loads[first : first + 2]:
            load.wait()
        total.add(0, landed=True)

    @pl.when(step == 0)
    def _():
        enter(downs[1], 2)
        downs[1].start(1)
        enter(ups[3], 10)
        ups[3].start(1)
        enter(ups[0], 4)
        ups[0].start(1)
        enter(ups[1], 6)
        ups[1].start(1)

    @pl.when(step == 1)
    def _():
        enter(downs[0], 0)
        enter(ups[2], 8)
        loads[12].wait()
        out.add(0)

    @pl.when(step == 3)
    def _():
        for total in (downs[0], ups[2], out):
            total.start(1)

    @pl.when(step == 5)
    def _():
        downs[1].go(1)
        ups[3].go(1)

    @pl.when(step == 6)
    def _():
        ups[0].go(1)
        ups[1].go(1)
        a.add(0)

    @pl.when(step == 8)
    def _():
        for total in (downs[0], ups[2], out):
            total.go(1)
        a.start(1)

    @pl.when(step == 9)
    def _():
        downs[1].go(2)
        ups[3].go(2)
        b.go(0)

    @pl.when(step == 10)
    def _():
        a.go(1)

    @pl.when(step == H)
    def _():
        wide = up_out.shape[1] // len(ups)
        for i, total in enumerate(ups):
            unfold(up_out, total.add(len(total.stages)), i * wide)
        for i, total in enumerate(downs):
            down_out[:, i * half : (i + 1) * half] = total.add(len(total.stages))
        unfold(out_out, out.add(2))
        unfold(qkv_a, a.add(2))
        some_b[...] = b.add(1).astype(BF16)

        @pl.when(here.core != here.y)
        def _():
            swap.wait()


def once(shape):
    return pl.BlockSpec(shape, lambda *_: (0,) * len(shape), pipeline_mode=pl.Buffered(1))


def backward_all(
    e_far, e_near, d_o, o, linv, q, k, k_far, v_far, v, gains, scales, h_t, grads, output
):
    _, keys, rows = e_far.shape
    width = h_t.shape[0]

    def head(*tail):
        return pl.BlockSpec((1,) + tail, lambda s: (jnp.minimum(s, H - 1),) + (0,) * len(tail))

    def batch(s):
        return jnp.maximum(s // BATCH - 1, 0)

    gain = pl.BlockSpec((BATCH, HD, 1), lambda s: (batch(s), 0, 0))
    specs = [head(keys, rows), head(keys, rows), head(HD, rows), head(HD, rows), head(8, rows)]
    specs += [once(q.shape), once(k.shape), head(HD, keys), head(HD, keys), head(HD, keys)]
    specs.append(pl.BlockSpec((BATCH, HD, 8), lambda s: (batch(s), 0, 0)))
    specs.append(pl.BlockSpec((2, BATCH, 1, rows), lambda s: (0, batch(s), 0, 0)))
    specs.append(once(h_t.shape))
    specs += [ANYWHERE] * 7
    shard, chunk = width // 32, grads[0].shape[-1]
    down_rows, half = grads[1].shape[-2], width // 2
    part = (16, 3 * BATCH * HD * 3 // 2)
    third = jax.ShapeDtypeStruct((4, 2, 2) + part, BF16)
    outs = [
        jax.ShapeDtypeStruct((3, H, HD, rows), BF16),
        jax.ShapeDtypeStruct((H, HD, 1), F32),
        jax.ShapeDtypeStruct((H, HD, 1), F32),
        third,
        third,
        jax.ShapeDtypeStruct((shard, len(UP_STAGES) * chunk * 2 // 3), F32),
        jax.ShapeDtypeStruct((down_rows, width), F32),
        jax.ShapeDtypeStruct((shard, width), F32),
        jax.ShapeDtypeStruct((shard, 3 * BATCH * HD), F32),
        jax.ShapeDtypeStruct((4, 2) + part, BF16),
    ]
    out_specs = [pl.BlockSpec((3, BATCH, HD, rows), lambda s: (0, batch(s), 0, 0)), gain, gain]
    out_specs += [once(a.shape) for a in outs[3:]] + [ANYWHERE]
    outs.append(jax.ShapeDtypeStruct(output.shape, BF16))
    scratch = [
        pltpu.VMEM((BATCH, 2, HD, keys), BF16),
        pltpu.VMEM((H, 2, HD, keys), BF16),
        pltpu.SemaphoreType.DMA((H,)),
        pltpu.SemaphoreType.DMA((H,)),
        pltpu.VMEM((BATCH, 3, HD, rows), F32),
        pltpu.SemaphoreType.DMA((13,)),
        pltpu.SemaphoreType.DMA((1,)),
        pltpu.SemaphoreType.DMA((1,)),
    ]
    for stages in DOWN_STAGES:
        scratch += sum_scratch(stages, (down_rows, half))
    for stages in UP_STAGES:
        scratch += sum_scratch(stages, (16, chunk))
    scratch += sum_scratch(TWO, (16, width * 3 // 2))
    scratch += [pltpu.VMEM((4, 2, 2) + part, BF16)] * 2
    scratch += sum_scratch(TWO, part) + sum_scratch(("x",), part)
    return pl.pallas_call(
        backward_all_kernel,
        grid=(H + 1,),
        in_specs=specs,
        out_specs=out_specs,
        out_shape=outs,
        scratch_shapes=scratch,
        compiler_params=pltpu.CompilerParams(
            vmem_limit_bytes=61 * 2**20, collective_id=0, has_side_effects=True
        ),
        name="backward_all",
    )(e_far, e_near, d_o, o, linv, q, k, k_far, v_far, v, gains, scales, h_t, *grads, output)


def front_kernel(*refs):
    all_ref, vec_ref, here_ref, w_ref, *refs = refs
    h_ref, q_ref, k_ref, v_ref, scale_ref, x_ref, mq_ref, near_ref, far_ref, gains_ref, *refs = refs
    k_far, v_far, *refs = refs
    w_t, came, len_came, len_send, len_recv, row_send, row_recv, k_send, k_recv, v_send, v_recv = refs
    here = Here()
    step = pl.program_id(0)
    steps = pl.num_programs(0)
    block, width = here_ref.shape
    rows = all_ref.shape[0]
    swapped = here.core != here.y
    opposite = here.device(core=here.y, y=here.core)

    def move(i):
        cut = pl.ds(i * block, block)
        return remote(all_ref.at[cut], came.at[cut], (row_send, row_recv), i, opposite)

    move_lengths = remote(vec_ref, len_came, (len_send, len_recv), 0, opposite)

    def give(i):
        cut = (slice(None), slice(None), pl.ds(pl.multiple_of(i * block, block), block))
        to = here.other_core()
        return [
            remote(k_ref.at[cut], k_far.at[cut], (k_send, k_recv), i, to),
            remote(v_ref.at[cut], v_far.at[cut], (v_send, v_recv), i, to),
        ]

    @pl.when(step == 0)
    def _():
        greet([here.other_core(), here.device(core=1 - here.core, y=1 - here.y)])

        @pl.when(swapped)
        def _():
            move_lengths.start()
            for i in range(rows // block):
                move(i).start()

        for i in range(0, w_ref.shape[1], width // 3):
            w_t[i : i + width // 3, :] = w_ref[:, i : i + width // 3].T

        @pl.when(swapped)
        def _():
            move_lengths.wait()

        @pl.when(jnp.logical_not(swapped))
        def _():
            len_came[...] = vec_ref[...]

        gains_ref[...] = gains_table(vec_ref[...])
        lengths = len_came[LENGTHS : LENGTHS + 1, :]
        row = lax.broadcasted_iota(jnp.int32, (AUG, rows), 0)
        spot = lax.broadcasted_iota(jnp.int32, (AUG, rows), 1).astype(F32)

        def inside(first):
            found = jnp.zeros((AUG, rows), jnp.int32)
            begin = jnp.zeros((1, 1), F32)
            where = spot + (first * 1).astype(F32)
            for c in range(SEQS):
                end = begin + lengths[:, c : c + 1]
                hit = (row == c) & (where >= begin) & (where < end)
                found = jnp.where(hit, 1, found)
                begin = end
            return found

        near = inside(here.core * rows)
        near_ref[...] = near.astype(F32).astype(BF16)
        mq_ref[...] = jnp.where(near == 1, 0.0, BLOCKED).astype(BF16)
        far_ref[...] = inside((1 - here.core) * rows).astype(F32).astype(BF16)

    @pl.when(swapped)
    def _():
        move(step).wait()
        x_ref[...] = came[pl.ds(pl.multiple_of(step * block, block), block), :]

    @pl.when(jnp.logical_not(swapped))
    def _():
        x_ref[...] = here_ref[...]

    h = normed(x_ref[...], vec_ref[0:1, :], vec_ref[1:2, :])
    h_ref[...] = h.T
    q, k, v, scale_q, scale_k = heads_of(h, w_t, gains_ref)
    at = pl.ds(pl.multiple_of(step * block, block), block)
    k_ref[:, :, at] = k
    v_ref[:, :, at] = v
    for copy in give(step):
        copy.start()
    q_ref[...] = q
    scale_ref[0] = scale_q
    scale_ref[1] = scale_k

    @pl.when(step == steps - 1)
    def _():
        for i in range(rows // block):
            for copy in give(i):
                copy.wait()


SEQS = 6
LENGTHS = 6


def gains_table(vectors):
    width = vectors.shape[1]
    gain_q, gain_k = vectors[4:5, :], vectors[5:6, :]
    folded = gain_q * (LOG2E / math.sqrt(HD))
    table = [folded, gain_k, 1.0 / folded, 1.0 / gain_k, gain_q, gain_k]
    table.append(jnp.zeros((122, width), F32))
    return jnp.concatenate(table, axis=0).T[:, :8].reshape(H, HD, 8)


def front(tokens, vectors, w):
    rows, width = tokens.shape
    block = math.gcd(rows, 128)
    steps = rows // block
    row = pl.BlockSpec((block, width), lambda i: (i, 0))
    head = pl.BlockSpec((H, HD, block), lambda i: (0, 0, i))
    heads = jax.ShapeDtypeStruct((H, HD, rows), BF16)
    mask = jax.ShapeDtypeStruct((AUG, rows), BF16)
    return pl.pallas_call(
        front_kernel,
        grid=(steps,),
        in_specs=[ANYWHERE, once(vectors.shape), row, once(w.shape)],
        out_specs=[
            pl.BlockSpec((width, block), lambda i: (0, i)),
            head,
            once(heads.shape),
            once(heads.shape),
            pl.BlockSpec((2, H, 1, block), lambda i: (0, 0, 0, i)),
            row,
            once(mask.shape),
            once(mask.shape),
            once(mask.shape),
            once((H, HD, 8)),
            ANYWHERE,
            ANYWHERE,
        ],
        out_shape=[
            jax.ShapeDtypeStruct((width, rows), BF16),
            heads,
            heads,
            heads,
            jax.ShapeDtypeStruct((2, H, 1, rows), F32),
            jax.ShapeDtypeStruct((rows, width), BF16),
            mask,
            mask,
            mask,
            jax.ShapeDtypeStruct((H, HD, 8), F32),
            heads,
            heads,
        ],
        scratch_shapes=[
            pltpu.VMEM((w.shape[1], width), BF16),
            pltpu.VMEM((rows, width), BF16),
            pltpu.VMEM(vectors.shape, F32),
            pltpu.SemaphoreType.DMA((1,)),
            pltpu.SemaphoreType.DMA((1,)),
        ]
        + [pltpu.SemaphoreType.DMA((steps,))] * 6,
        compiler_params=params(collective_id=3, has_side_effects=True),
        cost_estimate=pl.CostEstimate(
            flops=2 * rows * w.size, bytes_accessed=12 * rows * width, transcendentals=0
        ),
        name="front",
    )(tokens, vectors, tokens, w)


REST_STAGES = [("column", "plane"), ("x", "column", "y")]
TABLE_STAGES = ("column", "plane")


def tail_kernel(*refs):
    d_ref, w_ref, x_ref, dx1_ref, vec_ref, *refs = refs
    sum_q_ref, sum_k_ref, dgain2_ref, dbias2_ref, keep_ref, some_ref, give_ref, *refs = refs
    out_ref, qkv_b, qkv_c, table_ref, *refs = refs
    made, vectors, keep_t, give_t, stay_sem, swap_send, swap_recv, *refs = refs
    here = Here()
    step = pl.program_id(0)
    steps = pl.num_programs(0)
    block = x_ref.shape[0]
    swapped = here.core != here.y
    opposite = here.device(core=here.y, y=here.core)
    parts, start = [], 0
    for stages in REST_STAGES:
        count = 2 * len(stages) + 4
        size = refs[0].shape[-1]
        cut = (slice(None),) * 4 + (pl.ds(start, size),)
        parts.append(Sum(here, stages, give_ref.at[cut], keep_ref.at[cut], refs[:count]))
        refs, start = refs[count:], start + size
    table = Sum(here, TABLE_STAGES, give_t, keep_t, refs[:8])
    other = Sum(here, REST_STAGES[1], None, None, refs[8:])
    other.held[1] = some_ref

    @pl.when(step == 0)
    def _():
        greet(here.partners() + [here.device(core=1 - here.core, y=1 - here.y)])
        other.start(2)
        for part in parts:
            part.start(0)

    def stay(i):
        cut = pl.ds(i * block, block)
        return pltpu.make_async_copy(made.at[cut], out_ref.at[cut], stay_sem.at[i])

    def move(i):
        cut = pl.ds(i * block, block)
        return remote(made.at[cut], out_ref.at[cut], (swap_send, swap_recv), i, opposite)

    new, dgain, dbias = token_grads(
        d_ref[...], w_ref[...], x_ref[...], dx1_ref[...], vec_ref[0:1, :]
    )
    made[pl.ds(pl.multiple_of(step * block, block), block), :] = new
    first = step == 0
    vectors[0:1, :] = jnp.where(first, dgain, vectors[0:1, :] + dgain)
    vectors[1:2, :] = jnp.where(first, dbias, vectors[1:2, :] + dbias)

    @pl.when(swapped)
    def _():
        move(step).start()

    @pl.when(jnp.logical_not(swapped))
    def _():
        stay(step).start()

    @pl.when(step == 0)
    def _():
        for part in parts:
            part.go(0)

    @pl.when(step == 2)
    def _():
        parts[1].go(1)

    @pl.when(step == steps - 1)
    def _():
        width = x_ref.shape[1]
        rows = [vectors[0:1, :], vectors[1:2, :], dgain2_ref[...], dbias2_ref[...]]
        rows.append(jnp.zeros((124, width), F32))
        columns = jnp.concatenate(rows, axis=0).T
        lane = lax.broadcasted_iota(jnp.int32, columns.shape, 1)
        columns = jnp.where(lane == 4, sum_q_ref[...].reshape(width, 1), columns)
        columns = jnp.where(lane == 5, sum_k_ref[...].reshape(width, 1), columns)
        columns = columns.reshape(8, 2, 2, width // 32, 128)
        mine = here.core == 0
        keep_t[...] = jnp.where(mine, columns[:, 0], columns[:, 1]).reshape(keep_t.shape)
        give_t[...] = jnp.where(mine, columns[:, 1], columns[:, 0]).reshape(keep_t.shape)
        table.start(0)
        parts[0].go(1)
        table.go(0)
        other.go(2)
        table.go(1)
        parts[1].go(2)
        unfold(qkv_b, other.add(3))
        table_ref[...] = table.add(2)
        unfold(qkv_c, jnp.concatenate([part.add(len(part.stages)) for part in parts], axis=-1))

        @pl.when(swapped)
        def _():
            for i in range(steps):
                move(i).wait()

        @pl.when(jnp.logical_not(swapped))
        def _():
            for i in range(steps):
                stay(i).wait()


def tail(d, w, x, dx1, vectors, sum_q, sum_k, dgain2, dbias2, keep, some, give):
    rows, width = x.shape
    block = math.gcd(rows, 256)
    steps = rows // block
    row = pl.BlockSpec((block, width), lambda i: (i, 0))
    shard = width // 32
    part = keep.shape[-2:]
    return pl.pallas_call(
        tail_kernel,
        grid=(steps,),
        in_specs=[
            pl.BlockSpec(d.shape[:3] + (block,), lambda i: (0, 0, 0, i)),
            once(w.shape),
            row,
            row,
            once(vectors.shape),
            once(sum_q.shape),
            once(sum_k.shape),
            once(dgain2.shape),
            once(dbias2.shape),
            once(keep.shape),
            once(some.shape),
            ANYWHERE,
        ],
        out_specs=[ANYWHERE] + [once((shard, 3 * BATCH * HD))] * 2 + [once((shard, 128))],
        out_shape=[
            jax.ShapeDtypeStruct((rows, width), BF16),
            jax.ShapeDtypeStruct((shard, 3 * BATCH * HD), F32),
            jax.ShapeDtypeStruct((shard, 3 * BATCH * HD), F32),
            jax.ShapeDtypeStruct((shard, 128), F32),
        ],
        scratch_shapes=[
            pltpu.VMEM((rows, width), BF16),
            pltpu.VMEM((8, width), F32),
            pltpu.VMEM((4, 2, 2, shard, 128), F32),
            pltpu.VMEM((4, 2, 2, shard, 128), F32),
            pltpu.SemaphoreType.DMA((steps,)),
            pltpu.SemaphoreType.DMA((steps,)),
            pltpu.SemaphoreType.DMA((steps,)),
            *sum_scratch(REST_STAGES[0], (part[0], part[1] // 3)),
            *sum_scratch(REST_STAGES[1], (part[0], part[1] * 2 // 3)),
            *sum_scratch(TABLE_STAGES, (shard, 128), F32),
            *sum_scratch(REST_STAGES[1], part),
        ],
        compiler_params=pltpu.CompilerParams(
            vmem_limit_bytes=VMEM_LIMIT, collective_id=1, has_side_effects=True
        ),
        name="tail",
    )(d, w, x, dx1, vectors, sum_q, sum_k, dgain2, dbias2, keep, some, give)


def finish_kernel(here_ref, came_ref, tokens_ref, *refs):
    qkvs, ins, outs = refs[:3], refs[3:6], refs[6:]
    here = Here()
    swapped = here.core != here.y

    @pl.when(swapped)
    def _():
        outs[0][...] = came_ref[...]

    @pl.when(jnp.logical_not(swapped))
    def _():
        outs[0][...] = here_ref[...]

    outs[1][...] = tokens_ref[...]
    some = BATCH * HD

    @pl.when(pl.program_id(0) == 0)
    def _():
        for g in range(3):
            for part in range(3):
                at = (part * 3 + g) * some
                outs[2][:, at : at + some] = qkvs[g][:, part * some : (part + 1) * some]
        for source, target in zip(ins, outs[3:]):
            target[...] = source[...]


def finish(output, came, grad_tokens, qkvs, out, up, down):
    rows, width = output.shape
    steps = 4
    small = [jax.ShapeDtypeStruct((out.shape[0], 9 * BATCH * HD), F32), out, up, down]
    row = pl.BlockSpec((rows // steps, width), lambda i: (i, 0))
    return pl.pallas_call(
        finish_kernel,
        grid=(steps,),
        in_specs=[row] * 3 + [once(a.shape) for a in (*qkvs, out, up, down)],
        out_specs=[row] * 2 + [once(a.shape) for a in small],
        out_shape=[
            jax.ShapeDtypeStruct(a.shape, a.dtype) for a in (output, grad_tokens, *small)
        ],
        compiler_params=params(),
        name="finish",
    )(output, came, grad_tokens, *qkvs, out, up, down)


def segments(lengths, group, mine, rows):
    count = lengths.shape[1]
    at = jnp.arange(count)
    ends = jnp.sum(jnp.where(at[:, None] <= at[None, :], lengths[0][:, None], 0), axis=0)
    spots = jnp.arange(group, dtype=jnp.int32)
    segment = jnp.sum((spots[None, :] >= ends[:, None]).astype(jnp.int32), axis=0)
    is_in = jnp.arange(AUG)[:, None] == segment[None, :]
    mask_k = is_in.astype(BF16)
    mask_q = jnp.where(is_in, 0.0, BLOCKED).astype(BF16)
    mask_q = lax.dynamic_slice_in_dim(mask_q, mine * rows, rows, axis=1)
    return mask_q, mask_k


def ungroup(grads):
    parts = [g.reshape(-1, 3, BATCH * HD) for g in grads]
    return jnp.concatenate(parts, axis=2).reshape(parts[0].shape[0], -1)


def on_chips(tokens, vectors, lengths, w_qkv, w_out, w_up, w_down, cotangent):
    rows, width = tokens.shape
    h_t, q, k, v, scales, tokens, mask_q, mask_near, mask_far, gains, k_far, v_far = front(
        tokens, vectors, w_qkv
    )
    parts = [(k, v, mask_near), (k_far, v_far, mask_far)]
    o, linv, e_near, e_far, came = attend(q, mask_q, parts, cotangent)
    output, dx1, d_o, dgain2, dbias2, *grads = middle(
        tokens, o.reshape(width, rows), cotangent, w_out, vectors, w_up, w_down, came
    )
    d_o = d_o.reshape(H, HD, rows)
    d, sum_q, sum_k, keep, give, up, down, out, qkv_a, some, output_came = backward_all(
        e_far, e_near, d_o, o, linv, q, k, k_far, v_far, v, gains, scales, h_t, grads, output
    )
    grad_tokens, qkv_b, qkv_c, table = tail(
        d, w_qkv, tokens, dx1, vectors, sum_q, sum_k, dgain2, dbias2, keep, some, give
    )
    sums = [table[:, i] for i in (0, 1, 4, 5, 2, 3)]
    output, grad_tokens, sum_w_qkv, out, up, down = finish(
        output, output_came, grad_tokens, [qkv_a, qkv_b, qkv_c], out, up, down
    )
    return output, grad_tokens, sums, sum_w_qkv, out, up, down


def anywhere(tokens, vectors, lengths, w_qkv, w_out, w_up, w_down, cotangent):
    rows, width = tokens.shape
    parts = lax.axis_size("blk")
    mask_q, mask_k = segments(lengths, rows * parts, lax.axis_index("blk"), rows)
    h_t, q, k, v, scales = project(tokens, vectors, w_qkv.T, gains_table(vectors))
    k_all = lax.all_gather(k, "blk", axis=2, tiled=True)
    v_all = lax.all_gather(v, "blk", axis=2, tiled=True)
    o, linv, e_all = attend(q, mask_q, [(k_all, v_all, mask_k)])
    output, dx1, d_o, dgain2, dbias2, up, down, out = middle(
        tokens, o.reshape(width, rows), cotangent, w_out, vectors, w_up, w_down
    )
    d_o = d_o.reshape(H, HD, rows)
    d_q, d_k, d_v = attend_back(e_all, d_o, o, linv, q, k_all, v_all)
    pair = jnp.stack([d_k, d_v]).reshape(2, H, HD, parts, rows)
    pair = jnp.transpose(pair, (3, 0, 1, 2, 4)).astype(BF16)
    pair = lax.psum_scatter(pair, "blk", scatter_dimension=0, tiled=False).astype(F32)
    d, sum_q, sum_k, grad = post(
        d_q, pair[0], pair[1], q, k, gains_table(vectors), scales, h_t
    )
    grad_tokens, dgain1, dbias1 = last(d, w_qkv, tokens, dx1, vectors)
    scatter = functools.partial(lax.psum_scatter, axis_name=AXES, scatter_dimension=0, tiled=True)
    sums = [
        scatter(g.reshape(width)) for g in (dgain1, dbias1, sum_q, sum_k, dgain2, dbias2)
    ]
    grad = ungroup(jnp.split(grad, H // BATCH, axis=1))
    return output, grad_tokens, sums, scatter(grad), scatter(out), scatter(up), scatter(down)


def shards(
    tokens,
    lengths,
    ln1_gain,
    ln1_bias,
    w_qkv,
    q_gain,
    k_gain,
    w_out,
    ln2_gain,
    ln2_bias,
    w_up,
    w_down,
    cotangent,
):
    width = tokens.shape[1]
    lengths_row = jnp.pad(lengths[0].astype(F32), (0, width - lengths.shape[1]))
    rows = [ln1_gain, ln1_bias, ln2_gain, ln2_bias, q_gain, k_gain, lengths_row]
    at = lax.broadcasted_iota(jnp.int32, (8, width), 0)
    vectors = jnp.zeros((8, width), F32)
    for i, row in enumerate(rows):
        vectors = jnp.where(at == i, row[None, :], vectors)
    known = lax.axis_size("blk") == 2 and lax.axis_size("wide") == 16
    run = on_chips if known else anywhere
    output, grad_tokens, sums, s_qkv, s_out, s_up, s_down = run(
        tokens, vectors, lengths, w_qkv, w_out, w_up, w_down, cotangent
    )
    return (
        output,
        grad_tokens,
        sums[0],
        sums[1],
        s_qkv,
        sums[2],
        sums[3],
        s_out,
        sums[4],
        sums[5],
        s_up,
        s_down,
    )


def solution(mesh):
    split = P(AXES, None)
    in_specs = (split, P("wide", None)) + (P(),) * 10 + (split,)
    vector = P(AXES)
    out_specs = (
        split,
        split,
        vector,
        vector,
        split,
        vector,
        vector,
        split,
        vector,
        vector,
        split,
        split,
    )
    return jax.shard_map(shards, mesh=mesh, in_specs=in_specs, out_specs=out_specs, check_vma=False)
```

```python
import functools
import math

import jax
import jax.numpy as jnp
from jax import lax
from jax.experimental import pallas as pl
from jax.experimental.pallas import tpu as pltpu
from jax.sharding import PartitionSpec as P

H = 12
HD = 64
EPS = 1e-06
AXES = ("wide", "blk")
AUG = 16
BLOCKED = -512.0
LOG2E = math.log2(math.e)
NN = (((1,), (0,)), ((), ()))
NT = (((1,), (1,)), ((), ()))
TN = (((0,), (0,)), ((), ()))
TT = (((0,), (1,)), ((), ()))
BF16 = jnp.bfloat16
MESH = pl.DeviceIdType.MESH
F32 = jnp.float32
VMEM_LIMIT = 56 * 2**20


def mul(left, right, dims, kind=F32):
    return lax.dot_general(left, right, dims, preferred_element_type=F32).astype(kind)


def ones_rows(columns):
    return (lax.broadcasted_iota(jnp.int32, (AUG, columns), 0) < 2).astype(BF16)


def key_block(keys):
    return math.gcd(keys, 512)


def forward_kernel(count, *refs):
    q_ref, mq_ref, *refs = refs
    parts, refs = refs[: 3 * count], refs[3 * count :]
    if count == 2:
        own_ref, o_ref, linv_ref, *e_refs, came_ref, send_sem, recv_sem = refs
        here = Here()
        swapped = here.core != here.y
        swap = remote(own_ref, came_ref, (send_sem, recv_sem), 0, here.opposite())

        @pl.when(pl.program_id(0) == 0)
        def _():
            greet([here.opposite()])

            @pl.when(swapped)
            def _():
                swap.start()
    else:
        o_ref, linv_ref, *e_refs = refs
    keys = parts[0].shape[2]
    bk = key_block(keys)
    ones = ones_rows(bk)
    for h in range(q_ref.shape[0]):
        q = jnp.concatenate([q_ref[h], mq_ref[...]], axis=0)
        acc = None
        for p in range(count):
            k_ref, v_ref, mk_ref = parts[3 * p : 3 * p + 3]
            for i in range(keys // bk):
                cut = slice(i * bk, (i + 1) * bk)
                k = jnp.concatenate([k_ref[h, :, cut], mk_ref[:, cut]], axis=0)
                v = jnp.concatenate([v_ref[h, :, cut], ones], axis=0)
                e = jnp.exp2(mul(k, q, TN)).astype(BF16)
                e_refs[p][h, cut, :] = e
                part = mul(v, e, NN)
                acc = part if acc is None else acc + part
        linv = 1.0 / acc[HD : HD + 1]
        o_ref[h] = (acc[:HD] * linv).astype(BF16)
        linv_ref[h] = jnp.broadcast_to(linv, linv_ref.shape[1:])
    if count == 2:

        @pl.when(swapped & (pl.program_id(0) == pl.num_programs(0) - 1))
        def _():
            swap.wait()


def attend(q, mask_q, parts, cotangent=None):
    heads, _, rows = q.shape
    keys = parts[0][0].shape[2]
    some = 2 if len(parts) * keys * rows <= 1 << 21 else 1

    def head(*tail):
        return pl.BlockSpec((some,) + tail, lambda h: (h,) + (0,) * len(tail))

    specs = [head(HD, rows), fixed(mask_q.shape)]
    for part in parts:
        specs += [head(HD, keys), head(HD, keys), fixed(part[2].shape)]
    ins, more_out, more_specs, scratch, more = [], [], [], [], {}
    if cotangent is not None:
        ins = [cotangent]
        specs.append(ANYWHERE)
        more_out, more_specs = [jax.ShapeDtypeStruct(cotangent.shape, BF16)], [ANYWHERE]
        scratch = [pltpu.SemaphoreType.DMA((1,))] * 2
        more = {"collective_id": 4, "has_side_effects": True}
    return pl.pallas_call(
        functools.partial(forward_kernel, len(parts)),
        grid=(heads // some,),
        in_specs=specs,
        out_specs=[head(HD, rows), head(8, rows)] + [head(keys, rows)] * len(parts) + more_specs,
        out_shape=[
            jax.ShapeDtypeStruct((heads, HD, rows), BF16),
            jax.ShapeDtypeStruct((heads, 8, rows), F32),
        ]
        + [jax.ShapeDtypeStruct((heads, keys, rows), BF16)] * len(parts)
        + more_out,
        scratch_shapes=scratch,
        compiler_params=params(**more),
        cost_estimate=pl.CostEstimate(
            flops=heads * rows * keys * len(parts) * 1024,
            bytes_accessed=heads * rows * keys * len(parts) * 2,
            transcendentals=heads * rows * keys * len(parts),
        ),
        name="attend",
    )(q, mask_q, *[a for part in parts for a in part], *ins)


def scaled_gradient(do_ref, o_ref, linv_ref, h):
    low = (do_ref[h] * linv_ref[h, :1]).astype(BF16)
    delta = -jnp.sum(low.astype(F32) * o_ref[h].astype(F32), axis=0, keepdims=True)
    top = delta.astype(BF16).astype(F32)
    row = lax.broadcasted_iota(jnp.int32, (AUG, delta.shape[1]), 0)
    extra = jnp.where(row == 0, top, jnp.where(row == 1, delta - top, 0.0)).astype(BF16)
    return low, jnp.concatenate([low, extra], axis=0)


def block_back(e, low, do, q, k, v):
    v = jnp.concatenate([v, ones_rows(v.shape[1])], axis=0)
    ds = (e.astype(F32) * mul(v, do, TN)).astype(BF16)
    return mul(k, ds, NN), mul(q, ds, NT), mul(low, e, NT)


def backward_kernel(e_ref, do_ref, o_ref, linv_ref, q_ref, k_ref, v_ref, dq_ref, dk_ref, dv_ref):
    keys = k_ref.shape[2]
    bk = key_block(keys)
    low, do = scaled_gradient(do_ref, o_ref, linv_ref, 0)
    acc = None
    for i in range(keys // bk):
        cut = slice(i * bk, (i + 1) * bk)
        part, dk_ref[0, :, cut], dv_ref[0, :, cut] = block_back(
            e_ref[0, cut, :], low, do, q_ref[0], k_ref[0, :, cut], v_ref[0, :, cut]
        )
        acc = part if acc is None else acc + part
    dq_ref[0] = acc


def attend_back(e, do, o, linv, q, k, v):
    heads, keys, rows = e.shape

    def head(*tail):
        return pl.BlockSpec((1,) + tail, lambda h: (h,) + (0,) * len(tail))

    specs = [head(keys, rows), head(HD, rows), head(HD, rows), head(8, rows), head(HD, rows)]
    return pl.pallas_call(
        backward_kernel,
        grid=(heads,),
        in_specs=specs + [head(HD, keys)] * 2,
        out_specs=[head(HD, rows), head(HD, keys), head(HD, keys)],
        out_shape=[
            jax.ShapeDtypeStruct((heads, HD, rows), F32),
            jax.ShapeDtypeStruct((heads, HD, keys), F32),
            jax.ShapeDtypeStruct((heads, HD, keys), F32),
        ],
        compiler_params=params(),
        name="attend_back",
    )(e, do, o, linv, q, k, v)


def norm(value, axis):
    mean = jnp.mean(value, axis=axis, keepdims=True)
    centred = value - mean
    scale = lax.rsqrt(jnp.mean(centred * centred, axis=axis, keepdims=True) + EPS)
    return centred * scale, scale


def norm_back(grad, unit, scale, axis):
    mean = jnp.mean(grad, axis=axis, keepdims=True)
    along = jnp.mean(grad * unit, axis=axis, keepdims=True)
    return scale * (grad - mean - unit * along)


def gelu_parts(u):
    root = math.sqrt(2.0 / math.pi)
    square = u * u
    t = jnp.tanh(u * (root + (root * 0.044715) * square))
    half = 0.5 + 0.5 * t
    slope = half + (u * (0.5 - 0.5 * t * t)) * (root + (3 * root * 0.044715) * square)
    return u * half, slope


def params(**more):
    return pltpu.CompilerParams(vmem_limit_bytes=VMEM_LIMIT, **more)


def fixed(shape):
    return pl.BlockSpec(shape, lambda *_: (0,) * len(shape))


SCALAR = pl.BlockSpec(memory_space=pltpu.SMEM)
ANYWHERE = pl.BlockSpec(memory_space=pl.ANY)


def normed(x, gain, bias):
    return (norm(x.astype(F32), -1)[0] * gain + bias).astype(BF16)


def heads_of(h, w_ref, gains_ref):
    width = h.shape[1]

    def part(i):
        value = mul(w_ref[i * width : (i + 1) * width, :], h, NT)
        return value.reshape(width // HD, HD, h.shape[0])

    unit_k, scale_k = norm(part(1), 1)
    k = (unit_k * gains_ref[:, :, 1:2]).astype(BF16)
    v = part(2).astype(BF16)
    unit_q, scale_q = norm(part(0), 1)
    q = (unit_q * gains_ref[:, :, 0:1]).astype(BF16)
    return q, k, v, scale_q, scale_k


def project_kernel(x_ref, vec_ref, w_ref, gains_ref, h_ref, q_ref, k_ref, v_ref, scale_ref):
    h = normed(x_ref[...], vec_ref[0:1, :], vec_ref[1:2, :])
    h_ref[...] = h.T
    q_ref[...], k_ref[...], v_ref[...], scale_ref[0], scale_ref[1] = heads_of(h, w_ref, gains_ref)


def project(tokens, vectors, w_t, gains):
    rows, width = tokens.shape
    block = math.gcd(rows, 256)
    head = pl.BlockSpec((H, HD, block), lambda i: (0, 0, i))
    head_shape = jax.ShapeDtypeStruct((H, HD, rows), BF16)
    return pl.pallas_call(
        project_kernel,
        grid=(rows // block,),
        in_specs=[pl.BlockSpec((block, width), lambda i: (i, 0))]
        + [fixed(a.shape) for a in (vectors, w_t, gains)],
        out_specs=[
            pl.BlockSpec((width, block), lambda i: (0, i)),
            head,
            head,
            head,
            pl.BlockSpec((2, H, 1, block), lambda i: (0, 0, 0, i)),
        ],
        out_shape=[
            jax.ShapeDtypeStruct((width, rows), BF16),
            head_shape,
            head_shape,
            head_shape,
            jax.ShapeDtypeStruct((2, H, 1, rows), F32),
        ],
        compiler_params=params(),
        name="project",
    )(tokens, vectors, w_t, gains)


def fold(value):
    if value.shape[-2] % 16 == 0:
        return value
    half = value.shape[-1] // 2
    low = value[..., 16:, :]
    low = jnp.concatenate([low[..., :half], low[..., half:]], axis=-2)
    return jnp.concatenate([value[..., :16, :], low], axis=-1)


def unfold(out_ref, value, start=0):
    count = value.shape[-1] * 2 // 3
    half = count // 2
    out_ref[:16, start : start + count] = value[:, :count]
    out_ref[16:, start : start + half] = value[:8, count:]
    out_ref[16:, start + half : start + count] = value[8:, count:]


def spread(value, core, keep_ref, give_ref, lead):
    rows, columns = value.shape
    value = value.reshape((lead, 2, 2, rows // (4 * lead), columns))
    mine = core == 0
    keep = jnp.where(mine, value[:, 0], value[:, 1])
    give = jnp.where(mine, value[:, 1], value[:, 0])
    keep_ref[...] = fold(keep).astype(BF16).reshape(keep_ref.shape)
    give_ref[...] = fold(give).astype(BF16).reshape(give_ref.shape)


def middle_kernel(split, *refs):
    x_ref, o_ref, dy_ref, w_out_ref, vec_ref, w_up_ref, w_down_ref, *refs = refs
    if split:
        dy_here, (dy_came, *refs) = dy_ref, refs
    out_ref, dx1_ref, do_ref, dgain_ref, dbias_ref, *refs = refs
    grads, refs = (refs[:6], refs[6:]) if split else (refs[:3], refs[3:])
    x1_ref, h2_ref, h2t_ref, acc_ref, dh2_ref, g_ref, du_ref, da_ref, *refs = refs
    step = pl.program_id(0)
    rows = x_ref.shape[0]
    block = math.gcd(rows, 256)
    cuts = [slice(i, i + block) for i in range(0, rows, block)]
    if split:
        here = Here()
        keep_up, keep_down, keep_out, give_out, came_up, came_down = grads
        give_up, give_down, up_send, up_recv, down_send, down_recv, dy_ref, dy_sem = refs
        swapped = here.core != here.y

        def copies(f):
            to = here.other_core()
            return [
                remote(give_up.at[f % 2], came_up.at[f], (up_send, up_recv), f, to),
                remote(give_down.at[f % 2], came_down.at[f], (down_send, down_recv), f, to),
            ]

    @pl.when(step == 0)
    def _():
        if split:
            greet([here.other_core()])

            @pl.when(swapped)
            def _():
                pltpu.make_async_copy(dy_came, dy_ref, dy_sem.at[0]).start()

            @pl.when(jnp.logical_not(swapped))
            def _():
                pltpu.make_async_copy(dy_here, dy_ref, dy_sem.at[0]).start()

        for cut in cuts:
            x1 = x_ref[cut, :].astype(F32) + mul(o_ref[:, cut], w_out_ref[...], TN)
            x1_ref[cut, :] = x1
            acc_ref[cut, :] = x1
            h2 = normed(x1, vec_ref[2:3, :], vec_ref[3:4, :])
            h2_ref[cut, :] = h2
            h2t_ref[:, cut] = h2.T
        if split:
            pltpu.make_async_copy(dy_here, dy_ref, dy_sem.at[0]).wait()

    for cut in cuts:
        dy = dy_ref[cut, :]
        value, slope = gelu_parts(mul(h2_ref[cut, :], w_up_ref[...], NN))
        g = value.astype(BF16)
        g_ref[cut, :] = g
        acc_ref[cut, :] += mul(g, w_down_ref[...], NN)
        du = (mul(dy, w_down_ref[...], NT) * slope).astype(BF16)
        du_ref[cut, :] = du
        part = mul(du, w_up_ref[...], NT)
        dh2_ref[cut, :] = jnp.where(step == 0, part, dh2_ref[cut, :] + part)
    grad_up = mul(h2t_ref[...], du_ref[...], NN)
    grad_down = mul(g_ref[...], dy_ref[...], TN)
    if split:

        @pl.when(step >= 2)
        def _():
            for copy in copies(step - 2):
                copy.wait_send()

        spread(grad_up, here.core, keep_up, give_up.at[step % 2], 8)
        spread(grad_down, here.core, keep_down, give_down.at[step % 2], 2)
        for copy in copies(step):
            copy.start()
    else:
        grads[0][...] = grad_up
        grads[1][...] = grad_down

    @pl.when(step == pl.num_programs(0) - 1)
    def _():
        dgain, dbias = 0.0, 0.0
        for cut in cuts:
            out_ref[cut, :] = acc_ref[cut, :].astype(BF16)
            unit, scale = norm(x1_ref[cut, :], -1)
            dh2 = dh2_ref[cut, :]
            dgain += jnp.sum(dh2 * unit, axis=0, keepdims=True)
            dbias += jnp.sum(dh2, axis=0, keepdims=True)
            dx1 = dy_ref[cut, :].astype(F32) + norm_back(dh2 * vec_ref[2:3, :], unit, scale, -1)
            dx1_ref[cut, :] = dx1
            da = dx1.astype(BF16)
            da_ref[cut, :] = da
            do_ref[:, cut] = mul(w_out_ref[...], da, NT)
        dgain_ref[...] = dgain
        dbias_ref[...] = dbias
        grad_out = mul(o_ref[...], da_ref[...], NN)
        if split:
            spread(grad_out, here.core, keep_out, give_out, 8)
            for f in range(FF_STEPS):
                for copy in copies(f):
                    copy.wait_recv()
                    if f >= FF_STEPS - 2:
                        copy.wait_send()
        else:
            grads[2][...] = grad_out


FF_STEPS = 4


def middle(x, o, dy, w_out, vectors, w_up, w_down, came=None):
    rows, width = x.shape
    inner = w_up.shape[1]
    chunk = inner // FF_STEPS
    split = came is not None
    ins = [x, o, dy, w_out, vectors, w_up, w_down]
    specs = [fixed(a.shape) for a in ins[:5]]
    specs += [pl.BlockSpec((width, chunk), lambda f: (0, f)), pl.BlockSpec((chunk, width), lambda f: (f, 0))]
    weights = specs[-2:]
    if split:
        ins.append(came)
        specs[2] = ANYWHERE
        specs.append(ANYWHERE)
    outs = [
        jax.ShapeDtypeStruct((rows, width), BF16),
        jax.ShapeDtypeStruct((rows, width), F32),
        jax.ShapeDtypeStruct((width, rows), F32),
        jax.ShapeDtypeStruct((1, width), F32),
        jax.ShapeDtypeStruct((1, width), F32),
    ]
    out_specs = [fixed(a.shape) for a in outs]
    scratch = [
        pltpu.VMEM((rows, width), F32),
        pltpu.VMEM((rows, width), BF16),
        pltpu.VMEM((width, rows), BF16),
        pltpu.VMEM((rows, width), F32),
        pltpu.VMEM((rows, width), F32),
        pltpu.VMEM((rows, chunk), BF16),
        pltpu.VMEM((rows, chunk), BF16),
        pltpu.VMEM((rows, width), BF16),
    ]
    more = {}
    if split:
        up = (4, 2, 2, 16, chunk * 3 // 2)
        down = (2, 2, inner // 32, width)
        out = jax.ShapeDtypeStruct((4, 2, 2, 16, width * 3 // 2), BF16)
        ups = jax.ShapeDtypeStruct((FF_STEPS,) + up, BF16)
        downs = jax.ShapeDtypeStruct((FF_STEPS,) + down, BF16)
        outs += [ups, downs, out, out, ups, downs]
        out_specs += [pl.BlockSpec((1,) + up, lambda f: (f,) + (0,) * len(up))]
        out_specs += [pl.BlockSpec((1,) + down, lambda f: (f,) + (0,) * len(down))]
        out_specs += [fixed(out.shape), fixed(out.shape), ANYWHERE, ANYWHERE]
        scratch += [pltpu.VMEM((2,) + up, BF16), pltpu.VMEM((2,) + down, BF16)]
        scratch += [pltpu.SemaphoreType.DMA((FF_STEPS,))] * 4
        scratch += [pltpu.VMEM((rows, width), BF16), pltpu.SemaphoreType.DMA((1,))]
        more = {"collective_id": 2, "has_side_effects": True}
    else:
        outs += [jax.ShapeDtypeStruct(a.shape, F32) for a in (w_up, w_down, w_out)]
        out_specs += [*weights, fixed(w_out.shape)]
    return pl.pallas_call(
        functools.partial(middle_kernel, split),
        grid=(FF_STEPS,),
        in_specs=specs,
        out_specs=out_specs,
        out_shape=outs,
        scratch_shapes=scratch,
        compiler_params=params(**more),
        cost_estimate=pl.CostEstimate(
            flops=6 * rows * (2 * w_up.size + w_out.size),
            bytes_accessed=40 * rows * width,
            transcendentals=rows * inner,
        ),
        name="middle",
    )(*ins)


def head_backs(d_q, d_k, d_v, q, k, gains, scale_q, scale_k):
    d_q = d_q * (1.0 / math.sqrt(HD))
    d_k = d_k * (1.0 / LOG2E)
    inv_q, inv_k, gain_q, gain_k = [gains[:, :, i : i + 1] for i in range(2, 6)]
    unit_q = q.astype(F32) * inv_q
    unit_k = k.astype(F32) * inv_k
    sum_q = jnp.sum(d_q * unit_q, axis=2, keepdims=True)
    sum_k = jnp.sum(d_k * unit_k, axis=2, keepdims=True)
    d_q = norm_back(d_q * gain_q, unit_q, scale_q, 1).astype(BF16)
    d_k = norm_back(d_k * gain_k, unit_k, scale_k, 1).astype(BF16)
    return jnp.stack([d_q, d_k, d_v.astype(BF16)]), sum_q, sum_k


def post_kernel(*refs):
    *ins, scale_ref, h_ref, d_ref, sum_q_ref, sum_k_ref, grad_ref = refs
    values = [ref[...] for ref in ins]
    d, sum_q_ref[...], sum_k_ref[...] = head_backs(*values, scale_ref[0], scale_ref[1])
    d_ref[...] = d
    grad_ref[...] = mul(h_ref[...], d.reshape(-1, d.shape[-1]), NT)


def post(d_q, d_k, d_v, q, k, gains, scales, h_t):
    heads, _, rows = d_q.shape
    width = h_t.shape[0]
    some = 4
    here = pl.BlockSpec((some, HD, rows), lambda i: (i, 0, 0))
    gain = pl.BlockSpec((some, HD, 1), lambda i: (i, 0, 0))
    columns = 3 * some * HD
    return pl.pallas_call(
        post_kernel,
        grid=(heads // some,),
        in_specs=[here] * 5
        + [pl.BlockSpec((some, HD, 8), lambda i: (i, 0, 0))]
        + [pl.BlockSpec((2, some, 1, rows), lambda i: (0, i, 0, 0)), fixed(h_t.shape)],
        out_specs=[
            pl.BlockSpec((3, some, HD, rows), lambda i: (0, i, 0, 0)),
            gain,
            gain,
            pl.BlockSpec((width, columns), lambda i: (0, i)),
        ],
        out_shape=[
            jax.ShapeDtypeStruct((3, heads, HD, rows), BF16),
            jax.ShapeDtypeStruct((heads, HD, 1), F32),
            jax.ShapeDtypeStruct((heads, HD, 1), F32),
            jax.ShapeDtypeStruct((width, 3 * heads * HD), F32),
        ],
        compiler_params=params(),
        cost_estimate=pl.CostEstimate(
            flops=6 * rows * width * heads * HD,
            bytes_accessed=30 * rows * heads * HD,
            transcendentals=0,
        ),
        name="post",
    )(d_q, d_k, d_v, q, k, gains, scales, h_t)


def token_grads(d, w, x, dx1, gain):
    d_h = mul(w, d.reshape(-1, d.shape[-1]), NN).T
    unit, scale = norm(x.astype(F32), -1)
    d_x = dx1 + norm_back(d_h * gain, unit, scale, -1)
    dgain = jnp.sum(d_h * unit, axis=0, keepdims=True)
    dbias = jnp.sum(d_h, axis=0, keepdims=True)
    return d_x.astype(BF16), dgain, dbias


def last_kernel(d_ref, w_ref, x_ref, dx1_ref, vec_ref, out_ref, dgain_ref, dbias_ref):
    out_ref[...], dgain, dbias = token_grads(
        d_ref[...], w_ref[...], x_ref[...], dx1_ref[...], vec_ref[0:1, :]
    )
    first = pl.program_id(0) == 0
    dgain_ref[...] = jnp.where(first, dgain, dgain_ref[...] + dgain)
    dbias_ref[...] = jnp.where(first, dbias, dbias_ref[...] + dbias)


def last(d, w, x, dx1, vectors):
    rows, width = x.shape
    block = math.gcd(rows, 256)
    row = pl.BlockSpec((block, width), lambda i: (i, 0))
    return pl.pallas_call(
        last_kernel,
        grid=(rows // block,),
        in_specs=[
            pl.BlockSpec(d.shape[:3] + (block,), lambda i: (0, 0, 0, i)),
            fixed(w.shape),
            row,
            row,
            fixed(vectors.shape),
        ],
        out_specs=[row, fixed((1, width)), fixed((1, width))],
        out_shape=[
            jax.ShapeDtypeStruct((rows, width), BF16),
            jax.ShapeDtypeStruct((1, width), F32),
            jax.ShapeDtypeStruct((1, width), F32),
        ],
        compiler_params=params(),
        name="last",
    )(d, w, x, dx1, vectors)


class Here:
    def __init__(self):
        wide, self.y = lax.axis_index("wide"), lax.axis_index("blk")
        self.core, self.x, self.z = wide % 2, wide // 2 % 2, wide // 4

    def device(self, z=None, x=None, core=None, y=None):
        z = self.z if z is None else z
        x = self.x if x is None else x
        core = self.core if core is None else core
        return (z * 4 + x * 2 + core, self.y if y is None else y)

    def other_core(self):
        return self.device(core=1 - self.core)

    def opposite(self):
        return self.device(core=1 - self.core, y=1 - self.y)

    def at(self, kind, k):
        z = self.z
        if kind == "column":
            return {"z": (z, z + 1 - 2 * (z % 2), (z + 2) % 4, 3 - z)[k]}
        x = 1 - self.x if k % 2 else self.x
        y = 1 - self.y if k // 2 else self.y
        return {"plane": {"x": x, "y": y}, "x": {"x": x}, "y": {"y": 1 - self.y if k else self.y}}[kind]

    def partner(self, kind, k):
        return self.device(**self.at(kind, k))

    def partners(self):
        every = [self.partner(kind, k) for kind in ("plane", "column") for k in (1, 2, 3)]
        return [self.other_core()] + every

    def part(self, ref, axes, kind, k):
        where = self.at(kind, k)
        return ref.at[tuple(where.get(axis, slice(None)) for axis in axes)]


def greet(others):
    barrier = pltpu.get_barrier_semaphore()
    for other in others:
        pl.semaphore_signal(barrier, inc=1, device_id=other, device_id_type=MESH)
    pl.semaphore_wait(barrier, len(others))


def remote(source, target, sems, at, to):
    return pltpu.make_async_remote_copy(
        src_ref=source,
        dst_ref=target,
        send_sem=sems[0].at[at],
        recv_sem=sems[1].at[at],
        device_id=to,
        device_id_type=MESH,
    )


class Sum:
    def __init__(self, here, stages, give, keep, refs):
        self.here, self.stages, self.give = here, stages, give
        count = len(stages)
        self.held, self.came = list(refs[: count + 1]), refs[count + 1 : 2 * count + 2]
        self.sems = refs[2 * count + 2 : 2 * count + 4]
        self.keep = self.held[0] if keep is None else keep
        self.axes = ["zxy"]
        for stage in stages:
            gone = {"plane": "xy", "column": "z"}.get(stage, stage)
            self.axes.append("".join(axis for axis in self.axes[-1] if axis not in gone))

    def copies(self, stage):
        here = self.here
        if stage == 0:
            return [remote(self.give, self.came[0], self.sems, 0, here.other_core())]
        kind = self.stages[stage - 1]
        return [
            remote(
                here.part(self.held[stage - 1], self.axes[stage - 1], kind, k),
                self.came[stage].at[k - 1],
                self.sems,
                3 * stage - 3 + k,
                here.partner(kind, k),
            )
            for k in range(1, self.came[stage].shape[0] + 1)
        ]

    def start(self, stage):
        for copy in self.copies(stage):
            copy.start()

    def wait(self, stage):
        for copy in self.copies(stage):
            copy.wait()

    def add(self, stage, landed=False):
        if not landed:
            self.wait(stage)
        if stage == 0:
            terms = [self.keep, self.came[0]]
        else:
            kind = self.stages[stage - 1]
            terms = [self.here.part(self.held[stage - 1], self.axes[stage - 1], kind, 0)]
            terms += [self.came[stage].at[k] for k in range(self.came[stage].shape[0])]
        if stage == len(self.stages):
            return sum(term[...].astype(F32) for term in terms)
        target = self.held[stage]

        def body(i, _):
            target[i] = sum(term[i].astype(F32) for term in terms).astype(target.dtype)
            return 0

        lax.fori_loop(0, target.shape[0], body, 0)

    def go(self, stage):
        self.add(stage)
        self.start(stage + 1)


def sum_scratch(stages, tail, kind=BF16):
    left = {"z": 4, "x": 2, "y": 2}
    held, came = [tuple(left.values())], [tuple(left.values())]
    for stage in stages:
        partners = {"plane": 3, "column": 3}.get(stage, 1)
        for axis in {"plane": "xy", "column": "z"}.get(stage, stage):
            left.pop(axis)
        held.append(tuple(left.values()))
        came.append((partners,) + held[-1])
    held[-1] = (1,)
    shapes = [pltpu.VMEM(shape + tail, kind) for shape in held[:-1] + [(1,)] + came]
    shapes[len(stages)] = pltpu.VMEM((8, 128), kind)
    return shapes + [pltpu.SemaphoreType.DMA((3 * len(stages) + 1,))] * 2


BATCH = 4


def head_back(here, h, ins, far_out, far_in, far_sems, kept):
    e_far, e_near, do_ref, o_ref, linv_ref, q_ref, k_ref, k_far, v_far, v_near = ins
    low, do = scaled_gradient(do_ref, o_ref, linv_ref, 0)
    q = q_ref[h]
    slot = h % BATCH
    keys = k_far.shape[2]
    bk = key_block(keys)
    acc = None
    for i in range(keys // bk):
        cut = slice(i * bk, (i + 1) * bk)
        part, d_k, d_v = block_back(
            e_far[0, cut, :], low, do, q, k_far[0, :, cut], v_far[0, :, cut]
        )
        acc = part if acc is None else acc + part
        far_out[slot, 0, :, cut] = d_k.astype(BF16)
        far_out[slot, 1, :, cut] = d_v.astype(BF16)
    remote(far_out.at[slot], far_in.at[h], far_sems, h, here.other_core()).start()
    for i in range(keys // bk):
        cut = slice(i * bk, (i + 1) * bk)
        part, kept[slot, 1, :, cut], kept[slot, 2, :, cut] = block_back(
            e_near[0, cut, :], low, do, q, k_ref[h, :, cut], v_near[0, :, cut]
        )
        acc = acc + part
    kept[slot, 0] = acc


DOWN_STAGES = [("plane", "column"), ("x", "column", "y")]
UP_STAGES = [("column", "plane"), ("column", "plane"), ("plane", "column"), ("x", "column", "y")]
TWO = ("plane", "column")


def backward_all_kernel(*refs):
    attn, refs = refs[:10], refs[10:]
    gains_ref, scale_ref, h_ref, *refs = refs
    keep_up, keep_down, keep_out, give_out, came_up, came_down, own_ref, *refs = refs
    d_ref, sum_q_ref, sum_k_ref, keep_c, give_c, *refs = refs
    up_out, down_out, out_out, qkv_a, some_b, swap_ref, *refs = refs
    far_out, far_in, far_send, far_recv, kept, load_sem, swap_send, swap_recv, *refs = refs
    here = Here()
    swap = remote(own_ref, swap_ref, (swap_send, swap_recv), 0, here.opposite())
    step = pl.program_id(0)
    far_sems = (far_send, far_recv)

    def take(stages, give=None):
        nonlocal refs
        count = 2 * len(stages) + 4
        mine, refs = refs[:count], refs[count:]
        return Sum(here, stages, give, None, mine)

    half = keep_down.shape[-1] // 2
    downs, ups, loads = [], [], []
    for i, stages in enumerate(DOWN_STAGES):
        cut = (slice(None),) * 4 + (pl.ds(i * half, half),)
        downs.append(take(stages))
        loads += [(keep_down.at[cut], downs[-1].held[0]), (came_down.at[cut], downs[-1].came[0])]
    for i, stages in enumerate(UP_STAGES):
        ups.append(take(stages))
        loads += [(keep_up.at[i], ups[-1].held[0]), (came_up.at[i], ups[-1].came[0])]
    out = take(TWO, give_out)
    loads.append((keep_out, out.held[0]))
    loads = [pltpu.make_async_copy(*load, load_sem.at[i]) for i, load in enumerate(loads)]
    give_a, give_b, *refs = refs
    a, b = take(TWO, give_a), take(("x",), give_b)

    @pl.when(step == 0)
    def _():
        greet(here.partners() + [here.opposite()])
        out.start(0)

        @pl.when(here.core != here.y)
        def _():
            swap.start()

        for load in loads:
            load.start()

    def far_copy(h):
        return remote(far_out.at[h % BATCH], far_in.at[h], far_sems, h, here.other_core())

    @pl.when((step % BATCH == 0) & (step > 0))
    def _():
        base = step - BATCH
        for i in range(BATCH):
            far_copy(base + i).wait()
        for i in range(0, BATCH, 2):
            two = pl.ds(base + i, 2)
            some = slice(i, i + 2)
            d_k = kept[some, 1] + far_in[two, 0].astype(F32)
            d_v = kept[some, 2] + far_in[two, 1].astype(F32)
            d, sum_q, sum_k = head_backs(
                kept[some, 0],
                d_k,
                d_v,
                attn[5][two],
                attn[6][two],
                gains_ref[some],
                scale_ref[0, some],
                scale_ref[1, some],
            )
            d_ref[:, some] = d
            sum_q_ref[some] = sum_q
            sum_k_ref[some] = sum_k
        grad = mul(h_ref[...], d_ref[...].reshape(-1, d_ref.shape[-1]), NT)
        for i, (keep, give) in enumerate(
            ((a.held[0], give_a), (b.held[0], give_b), (keep_c, give_c))
        ):

            @pl.when(step == BATCH * (i + 1))
            def _():
                spread(grad, here.core, keep, give, 8)
                if i < 2:
                    (a, b)[i].start(0)

    @pl.when(step < H)
    def _():
        head_back(here, step, attn, far_out, far_in, far_sems, kept)

    def enter(total, first):
        for load in loads[first : first + 2]:
            load.wait()
        total.add(0, landed=True)

    @pl.when(step == 0)
    def _():
        enter(downs[1], 2)
        downs[1].start(1)
        enter(ups[3], 10)
        ups[3].start(1)
        enter(ups[0], 4)
        ups[0].start(1)
        enter(ups[1], 6)
        ups[1].start(1)

    @pl.when(step == 1)
    def _():
        enter(downs[0], 0)
        enter(ups[2], 8)
        loads[12].wait()
        out.add(0)

    @pl.when(step == 3)
    def _():
        for total in (downs[0], ups[2], out):
            total.start(1)

    @pl.when(step == 5)
    def _():
        downs[1].go(1)
        ups[3].go(1)

    @pl.when(step == 6)
    def _():
        ups[0].go(1)
        ups[1].go(1)
        a.add(0)

    @pl.when(step == 8)
    def _():
        for total in (downs[0], ups[2], out):
            total.go(1)
        a.start(1)

    @pl.when(step == 9)
    def _():
        downs[1].go(2)
        ups[3].go(2)
        b.go(0)

    @pl.when(step == 10)
    def _():
        a.go(1)

    @pl.when(step == H)
    def _():
        wide = up_out.shape[1] // len(ups)
        for i, total in enumerate(ups):
            unfold(up_out, total.add(len(total.stages)), i * wide)
        for i, total in enumerate(downs):
            down_out[:, i * half : (i + 1) * half] = total.add(len(total.stages))
        unfold(out_out, out.add(2))
        unfold(qkv_a, a.add(2))
        some_b[...] = b.add(1).astype(BF16)

        @pl.when(here.core != here.y)
        def _():
            swap.wait()


def once(shape):
    return pl.BlockSpec(shape, lambda *_: (0,) * len(shape), pipeline_mode=pl.Buffered(1))


def backward_all(
    e_far, e_near, d_o, o, linv, q, k, k_far, v_far, v, gains, scales, h_t, grads, output
):
    _, keys, rows = e_far.shape
    width = h_t.shape[0]

    def head(*tail):
        return pl.BlockSpec((1,) + tail, lambda s: (jnp.minimum(s, H - 1),) + (0,) * len(tail))

    def batch(s):
        return jnp.maximum(s // BATCH - 1, 0)

    gain = pl.BlockSpec((BATCH, HD, 1), lambda s: (batch(s), 0, 0))
    specs = [head(keys, rows), head(keys, rows), head(HD, rows), head(HD, rows), head(8, rows)]
    specs += [once(q.shape), once(k.shape), head(HD, keys), head(HD, keys), head(HD, keys)]
    specs.append(pl.BlockSpec((BATCH, HD, 8), lambda s: (batch(s), 0, 0)))
    specs.append(pl.BlockSpec((2, BATCH, 1, rows), lambda s: (0, batch(s), 0, 0)))
    specs.append(once(h_t.shape))
    specs += [ANYWHERE] * 7
    shard, chunk = width // 32, grads[0].shape[-1]
    down_rows, half = grads[1].shape[-2], width // 2
    part = (16, 3 * BATCH * HD * 3 // 2)
    third = jax.ShapeDtypeStruct((4, 2, 2) + part, BF16)
    outs = [
        jax.ShapeDtypeStruct((3, H, HD, rows), BF16),
        jax.ShapeDtypeStruct((H, HD, 1), F32),
        jax.ShapeDtypeStruct((H, HD, 1), F32),
        third,
        third,
        jax.ShapeDtypeStruct((shard, len(UP_STAGES) * chunk * 2 // 3), F32),
        jax.ShapeDtypeStruct((down_rows, width), F32),
        jax.ShapeDtypeStruct((shard, width), F32),
        jax.ShapeDtypeStruct((shard, 3 * BATCH * HD), F32),
        jax.ShapeDtypeStruct((4, 2) + part, BF16),
    ]
    out_specs = [pl.BlockSpec((3, BATCH, HD, rows), lambda s: (0, batch(s), 0, 0)), gain, gain]
    out_specs += [once(a.shape) for a in outs[3:]] + [ANYWHERE]
    outs.append(jax.ShapeDtypeStruct(output.shape, BF16))
    scratch = [
        pltpu.VMEM((BATCH, 2, HD, keys), BF16),
        pltpu.VMEM((H, 2, HD, keys), BF16),
        pltpu.SemaphoreType.DMA((H,)),
        pltpu.SemaphoreType.DMA((H,)),
        pltpu.VMEM((BATCH, 3, HD, rows), F32),
        pltpu.SemaphoreType.DMA((13,)),
        pltpu.SemaphoreType.DMA((1,)),
        pltpu.SemaphoreType.DMA((1,)),
    ]
    for stages in DOWN_STAGES:
        scratch += sum_scratch(stages, (down_rows, half))
    for stages in UP_STAGES:
        scratch += sum_scratch(stages, (16, chunk))
    scratch += sum_scratch(TWO, (16, width * 3 // 2))
    scratch += [pltpu.VMEM((4, 2, 2) + part, BF16)] * 2
    scratch += sum_scratch(TWO, part) + sum_scratch(("x",), part)
    return pl.pallas_call(
        backward_all_kernel,
        grid=(H + 1,),
        in_specs=specs,
        out_specs=out_specs,
        out_shape=outs,
        scratch_shapes=scratch,
        compiler_params=pltpu.CompilerParams(
            vmem_limit_bytes=61 * 2**20, collective_id=0, has_side_effects=True
        ),
        name="backward_all",
    )(e_far, e_near, d_o, o, linv, q, k, k_far, v_far, v, gains, scales, h_t, *grads, output)


def front_kernel(*refs):
    all_ref, vec_ref, here_ref, w_ref, *refs = refs
    h_ref, q_ref, k_ref, v_ref, scale_ref, x_ref, mq_ref, near_ref, far_ref, gains_ref, *refs = refs
    k_far, v_far, *refs = refs
    w_t, came, len_came, len_send, len_recv, row_send, row_recv, k_send, k_recv, v_send, v_recv = refs
    here = Here()
    step = pl.program_id(0)
    steps = pl.num_programs(0)
    block, width = here_ref.shape
    rows = all_ref.shape[0]
    swapped = here.core != here.y
    opposite = here.device(core=here.y, y=here.core)

    def move(i):
        cut = pl.ds(i * block, block)
        return remote(all_ref.at[cut], came.at[cut], (row_send, row_recv), i, opposite)

    move_lengths = remote(vec_ref, len_came, (len_send, len_recv), 0, opposite)

    def give(i):
        cut = (slice(None), slice(None), pl.ds(pl.multiple_of(i * block, block), block))
        to = here.other_core()
        return [
            remote(k_ref.at[cut], k_far.at[cut], (k_send, k_recv), i, to),
            remote(v_ref.at[cut], v_far.at[cut], (v_send, v_recv), i, to),
        ]

    @pl.when(step == 0)
    def _():
        greet([here.other_core(), here.device(core=1 - here.core, y=1 - here.y)])

        @pl.when(swapped)
        def _():
            move_lengths.start()
            for i in range(rows // block):
                move(i).start()

        for i in range(0, w_ref.shape[1], width // 3):
            w_t[i : i + width // 3, :] = w_ref[:, i : i + width // 3].T

        @pl.when(swapped)
        def _():
            move_lengths.wait()

        @pl.when(jnp.logical_not(swapped))
        def _():
            len_came[...] = vec_ref[...]

        gains_ref[...] = gains_table(vec_ref[...])
        lengths = len_came[LENGTHS : LENGTHS + 1, :]
        row = lax.broadcasted_iota(jnp.int32, (AUG, rows), 0)
        spot = lax.broadcasted_iota(jnp.int32, (AUG, rows), 1).astype(F32)

        def inside(first):
            found = jnp.zeros((AUG, rows), jnp.int32)
            begin = jnp.zeros((1, 1), F32)
            where = spot + (first * 1).astype(F32)
            for c in range(SEQS):
                end = begin + lengths[:, c : c + 1]
                hit = (row == c) & (where >= begin) & (where < end)
                found = jnp.where(hit, 1, found)
                begin = end
            return found

        near = inside(here.core * rows)
        near_ref[...] = near.astype(F32).astype(BF16)
        mq_ref[...] = jnp.where(near == 1, 0.0, BLOCKED).astype(BF16)
        far_ref[...] = inside((1 - here.core) * rows).astype(F32).astype(BF16)

    @pl.when(swapped)
    def _():
        move(step).wait()
        x_ref[...] = came[pl.ds(pl.multiple_of(step * block, block), block), :]

    @pl.when(jnp.logical_not(swapped))
    def _():
        x_ref[...] = here_ref[...]

    h = normed(x_ref[...], vec_ref[0:1, :], vec_ref[1:2, :])
    h_ref[...] = h.T
    q, k, v, scale_q, scale_k = heads_of(h, w_t, gains_ref)
    at = pl.ds(pl.multiple_of(step * block, block), block)
    k_ref[:, :, at] = k
    v_ref[:, :, at] = v
    for copy in give(step):
        copy.start()
    q_ref[...] = q
    scale_ref[0] = scale_q
    scale_ref[1] = scale_k

    @pl.when(step == steps - 1)
    def _():
        for i in range(rows // block):
            for copy in give(i):
                copy.wait()


SEQS = 6
LENGTHS = 6


def gains_table(vectors):
    width = vectors.shape[1]
    gain_q, gain_k = vectors[4:5, :], vectors[5:6, :]
    folded = gain_q * (LOG2E / math.sqrt(HD))
    table = [folded, gain_k, 1.0 / folded, 1.0 / gain_k, gain_q, gain_k]
    table.append(jnp.zeros((122, width), F32))
    return jnp.concatenate(table, axis=0).T[:, :8].reshape(H, HD, 8)


def front(tokens, vectors, w):
    rows, width = tokens.shape
    block = math.gcd(rows, 128)
    steps = rows // block
    row = pl.BlockSpec((block, width), lambda i: (i, 0))
    head = pl.BlockSpec((H, HD, block), lambda i: (0, 0, i))
    heads = jax.ShapeDtypeStruct((H, HD, rows), BF16)
    mask = jax.ShapeDtypeStruct((AUG, rows), BF16)
    return pl.pallas_call(
        front_kernel,
        grid=(steps,),
        in_specs=[ANYWHERE, once(vectors.shape), row, once(w.shape)],
        out_specs=[
            pl.BlockSpec((width, block), lambda i: (0, i)),
            head,
            once(heads.shape),
            once(heads.shape),
            pl.BlockSpec((2, H, 1, block), lambda i: (0, 0, 0, i)),
            row,
            once(mask.shape),
            once(mask.shape),
            once(mask.shape),
            once((H, HD, 8)),
            ANYWHERE,
            ANYWHERE,
        ],
        out_shape=[
            jax.ShapeDtypeStruct((width, rows), BF16),
            heads,
            heads,
            heads,
            jax.ShapeDtypeStruct((2, H, 1, rows), F32),
            jax.ShapeDtypeStruct((rows, width), BF16),
            mask,
            mask,
            mask,
            jax.ShapeDtypeStruct((H, HD, 8), F32),
            heads,
            heads,
        ],
        scratch_shapes=[
            pltpu.VMEM((w.shape[1], width), BF16),
            pltpu.VMEM((rows, width), BF16),
            pltpu.VMEM(vectors.shape, F32),
            pltpu.SemaphoreType.DMA((1,)),
            pltpu.SemaphoreType.DMA((1,)),
        ]
        + [pltpu.SemaphoreType.DMA((steps,))] * 6,
        compiler_params=params(collective_id=3, has_side_effects=True),
        cost_estimate=pl.CostEstimate(
            flops=2 * rows * w.size, bytes_accessed=12 * rows * width, transcendentals=0
        ),
        name="front",
    )(tokens, vectors, tokens, w)


REST_STAGES = [("column", "plane"), ("x", "column", "y")]
TABLE_STAGES = ("column", "plane")


def tail_kernel(*refs):
    d_ref, w_ref, x_ref, dx1_ref, vec_ref, *refs = refs
    sum_q_ref, sum_k_ref, dgain2_ref, dbias2_ref, keep_ref, some_ref, give_ref, *refs = refs
    out_ref, qkv_b, qkv_c, table_ref, *refs = refs
    made, vectors, keep_t, give_t, stay_sem, swap_send, swap_recv, *refs = refs
    here = Here()
    step = pl.program_id(0)
    steps = pl.num_programs(0)
    block = x_ref.shape[0]
    swapped = here.core != here.y
    opposite = here.device(core=here.y, y=here.core)
    parts, start = [], 0
    for stages in REST_STAGES:
        count = 2 * len(stages) + 4
        size = refs[0].shape[-1]
        cut = (slice(None),) * 4 + (pl.ds(start, size),)
        parts.append(Sum(here, stages, give_ref.at[cut], keep_ref.at[cut], refs[:count]))
        refs, start = refs[count:], start + size
    table = Sum(here, TABLE_STAGES, give_t, keep_t, refs[:8])
    other = Sum(here, REST_STAGES[1], None, None, refs[8:])
    other.held[1] = some_ref

    @pl.when(step == 0)
    def _():
        greet(here.partners() + [here.device(core=1 - here.core, y=1 - here.y)])
        other.start(2)
        for part in parts:
            part.start(0)

    def stay(i):
        cut = pl.ds(i * block, block)
        return pltpu.make_async_copy(made.at[cut], out_ref.at[cut], stay_sem.at[i])

    def move(i):
        cut = pl.ds(i * block, block)
        return remote(made.at[cut], out_ref.at[cut], (swap_send, swap_recv), i, opposite)

    new, dgain, dbias = token_grads(
        d_ref[...], w_ref[...], x_ref[...], dx1_ref[...], vec_ref[0:1, :]
    )
    made[pl.ds(pl.multiple_of(step * block, block), block), :] = new
    first = step == 0
    vectors[0:1, :] = jnp.where(first, dgain, vectors[0:1, :] + dgain)
    vectors[1:2, :] = jnp.where(first, dbias, vectors[1:2, :] + dbias)

    @pl.when(swapped)
    def _():
        move(step).start()

    @pl.when(jnp.logical_not(swapped))
    def _():
        stay(step).start()

    @pl.when(step == 0)
    def _():
        for part in parts:
            part.go(0)

    @pl.when(step == 2)
    def _():
        parts[1].go(1)

    @pl.when(step == steps - 1)
    def _():
        width = x_ref.shape[1]
        rows = [vectors[0:1, :], vectors[1:2, :], dgain2_ref[...], dbias2_ref[...]]
        rows.append(jnp.zeros((124, width), F32))
        columns = jnp.concatenate(rows, axis=0).T
        lane = lax.broadcasted_iota(jnp.int32, columns.shape, 1)
        columns = jnp.where(lane == 4, sum_q_ref[...].reshape(width, 1), columns)
        columns = jnp.where(lane == 5, sum_k_ref[...].reshape(width, 1), columns)
        columns = columns.reshape(8, 2, 2, width // 32, 128)
        mine = here.core == 0
        keep_t[...] = jnp.where(mine, columns[:, 0], columns[:, 1]).reshape(keep_t.shape)
        give_t[...] = jnp.where(mine, columns[:, 1], columns[:, 0]).reshape(keep_t.shape)
        table.start(0)
        parts[0].go(1)
        table.go(0)
        other.go(2)
        table.go(1)
        parts[1].go(2)
        unfold(qkv_b, other.add(3))
        table_ref[...] = table.add(2)
        unfold(qkv_c, jnp.concatenate([part.add(len(part.stages)) for part in parts], axis=-1))

        @pl.when(swapped)
        def _():
            for i in range(steps):
                move(i).wait()

        @pl.when(jnp.logical_not(swapped))
        def _():
            for i in range(steps):
                stay(i).wait()


def tail(d, w, x, dx1, vectors, sum_q, sum_k, dgain2, dbias2, keep, some, give):
    rows, width = x.shape
    block = math.gcd(rows, 256)
    steps = rows // block
    row = pl.BlockSpec((block, width), lambda i: (i, 0))
    shard = width // 32
    part = keep.shape[-2:]
    return pl.pallas_call(
        tail_kernel,
        grid=(steps,),
        in_specs=[
            pl.BlockSpec(d.shape[:3] + (block,), lambda i: (0, 0, 0, i)),
            once(w.shape),
            row,
            row,
            once(vectors.shape),
            once(sum_q.shape),
            once(sum_k.shape),
            once(dgain2.shape),
            once(dbias2.shape),
            once(keep.shape),
            once(some.shape),
            ANYWHERE,
        ],
        out_specs=[ANYWHERE] + [once((shard, 3 * BATCH * HD))] * 2 + [once((shard, 128))],
        out_shape=[
            jax.ShapeDtypeStruct((rows, width), BF16),
            jax.ShapeDtypeStruct((shard, 3 * BATCH * HD), F32),
            jax.ShapeDtypeStruct((shard, 3 * BATCH * HD), F32),
            jax.ShapeDtypeStruct((shard, 128), F32),
        ],
        scratch_shapes=[
            pltpu.VMEM((rows, width), BF16),
            pltpu.VMEM((8, width), F32),
            pltpu.VMEM((4, 2, 2, shard, 128), F32),
            pltpu.VMEM((4, 2, 2, shard, 128), F32),
            pltpu.SemaphoreType.DMA((steps,)),
            pltpu.SemaphoreType.DMA((steps,)),
            pltpu.SemaphoreType.DMA((steps,)),
            *sum_scratch(REST_STAGES[0], (part[0], part[1] // 3)),
            *sum_scratch(REST_STAGES[1], (part[0], part[1] * 2 // 3)),
            *sum_scratch(TABLE_STAGES, (shard, 128), F32),
            *sum_scratch(REST_STAGES[1], part),
        ],
        compiler_params=pltpu.CompilerParams(
            vmem_limit_bytes=VMEM_LIMIT, collective_id=1, has_side_effects=True
        ),
        name="tail",
    )(d, w, x, dx1, vectors, sum_q, sum_k, dgain2, dbias2, keep, some, give)


def finish_kernel(here_ref, came_ref, tokens_ref, *refs):
    qkvs, ins, outs = refs[:3], refs[3:6], refs[6:]
    here = Here()
    swapped = here.core != here.y

    @pl.when(swapped)
    def _():
        outs[0][...] = came_ref[...]

    @pl.when(jnp.logical_not(swapped))
    def _():
        outs[0][...] = here_ref[...]

    outs[1][...] = tokens_ref[...]
    some = BATCH * HD

    @pl.when(pl.program_id(0) == 0)
    def _():
        for g in range(3):
            for part in range(3):
                at = (part * 3 + g) * some
                outs[2][:, at : at + some] = qkvs[g][:, part * some : (part + 1) * some]
        for source, target in zip(ins, outs[3:]):
            target[...] = source[...]


def finish(output, came, grad_tokens, qkvs, out, up, down):
    rows, width = output.shape
    steps = 2
    small = [jax.ShapeDtypeStruct((out.shape[0], 9 * BATCH * HD), F32), out, up, down]
    row = pl.BlockSpec((rows // steps, width), lambda i: (i, 0))
    return pl.pallas_call(
        finish_kernel,
        grid=(steps,),
        in_specs=[row] * 3 + [once(a.shape) for a in (*qkvs, out, up, down)],
        out_specs=[row] * 2 + [once(a.shape) for a in small],
        out_shape=[
            jax.ShapeDtypeStruct(a.shape, a.dtype) for a in (output, grad_tokens, *small)
        ],
        compiler_params=params(),
        name="finish",
    )(output, came, grad_tokens, *qkvs, out, up, down)


def segments(lengths, group, mine, rows):
    count = lengths.shape[1]
    at = jnp.arange(count)
    ends = jnp.sum(jnp.where(at[:, None] <= at[None, :], lengths[0][:, None], 0), axis=0)
    spots = jnp.arange(group, dtype=jnp.int32)
    segment = jnp.sum((spots[None, :] >= ends[:, None]).astype(jnp.int32), axis=0)
    is_in = jnp.arange(AUG)[:, None] == segment[None, :]
    mask_k = is_in.astype(BF16)
    mask_q = jnp.where(is_in, 0.0, BLOCKED).astype(BF16)
    mask_q = lax.dynamic_slice_in_dim(mask_q, mine * rows, rows, axis=1)
    return mask_q, mask_k


def ungroup(grads):
    parts = [g.reshape(-1, 3, BATCH * HD) for g in grads]
    return jnp.concatenate(parts, axis=2).reshape(parts[0].shape[0], -1)


def on_chips(tokens, vectors, lengths, w_qkv, w_out, w_up, w_down, cotangent):
    rows, width = tokens.shape
    h_t, q, k, v, scales, tokens, mask_q, mask_near, mask_far, gains, k_far, v_far = front(
        tokens, vectors, w_qkv
    )
    parts = [(k, v, mask_near), (k_far, v_far, mask_far)]
    o, linv, e_near, e_far, came = attend(q, mask_q, parts, cotangent)
    output, dx1, d_o, dgain2, dbias2, *grads = middle(
        tokens, o.reshape(width, rows), cotangent, w_out, vectors, w_up, w_down, came
    )
    d_o = d_o.reshape(H, HD, rows)
    d, sum_q, sum_k, keep, give, up, down, out, qkv_a, some, output_came = backward_all(
        e_far, e_near, d_o, o, linv, q, k, k_far, v_far, v, gains, scales, h_t, grads, output
    )
    grad_tokens, qkv_b, qkv_c, table = tail(
        d, w_qkv, tokens, dx1, vectors, sum_q, sum_k, dgain2, dbias2, keep, some, give
    )
    sums = [table[:, i] for i in (0, 1, 4, 5, 2, 3)]
    output, grad_tokens, sum_w_qkv, out, up, down = finish(
        output, output_came, grad_tokens, [qkv_a, qkv_b, qkv_c], out, up, down
    )
    return output, grad_tokens, sums, sum_w_qkv, out, up, down


def anywhere(tokens, vectors, lengths, w_qkv, w_out, w_up, w_down, cotangent):
    rows, width = tokens.shape
    parts = lax.axis_size("blk")
    mask_q, mask_k = segments(lengths, rows * parts, lax.axis_index("blk"), rows)
    h_t, q, k, v, scales = project(tokens, vectors, w_qkv.T, gains_table(vectors))
    k_all = lax.all_gather(k, "blk", axis=2, tiled=True)
    v_all = lax.all_gather(v, "blk", axis=2, tiled=True)
    o, linv, e_all = attend(q, mask_q, [(k_all, v_all, mask_k)])
    output, dx1, d_o, dgain2, dbias2, up, down, out = middle(
        tokens, o.reshape(width, rows), cotangent, w_out, vectors, w_up, w_down
    )
    d_o = d_o.reshape(H, HD, rows)
    d_q, d_k, d_v = attend_back(e_all, d_o, o, linv, q, k_all, v_all)
    pair = jnp.stack([d_k, d_v]).reshape(2, H, HD, parts, rows)
    pair = jnp.transpose(pair, (3, 0, 1, 2, 4)).astype(BF16)
    pair = lax.psum_scatter(pair, "blk", scatter_dimension=0, tiled=False).astype(F32)
    d, sum_q, sum_k, grad = post(
        d_q, pair[0], pair[1], q, k, gains_table(vectors), scales, h_t
    )
    grad_tokens, dgain1, dbias1 = last(d, w_qkv, tokens, dx1, vectors)
    scatter = functools.partial(lax.psum_scatter, axis_name=AXES, scatter_dimension=0, tiled=True)
    sums = [
        scatter(g.reshape(width)) for g in (dgain1, dbias1, sum_q, sum_k, dgain2, dbias2)
    ]
    grad = ungroup(jnp.split(grad, H // BATCH, axis=1))
    return output, grad_tokens, sums, scatter(grad), scatter(out), scatter(up), scatter(down)


def shards(
    tokens,
    lengths,
    ln1_gain,
    ln1_bias,
    w_qkv,
    q_gain,
    k_gain,
    w_out,
    ln2_gain,
    ln2_bias,
    w_up,
    w_down,
    cotangent,
):
    width = tokens.shape[1]
    lengths_row = jnp.pad(lengths[0].astype(F32), (0, width - lengths.shape[1]))
    rows = [ln1_gain, ln1_bias, ln2_gain, ln2_bias, q_gain, k_gain, lengths_row]
    at = lax.broadcasted_iota(jnp.int32, (8, width), 0)
    vectors = jnp.zeros((8, width), F32)
    for i, row in enumerate(rows):
        vectors = jnp.where(at == i, row[None, :], vectors)
    known = lax.axis_size("blk") == 2 and lax.axis_size("wide") == 16
    run = on_chips if known else anywhere
    output, grad_tokens, sums, s_qkv, s_out, s_up, s_down = run(
        tokens, vectors, lengths, w_qkv, w_out, w_up, w_down, cotangent
    )
    return (
        output,
        grad_tokens,
        sums[0],
        sums[1],
        s_qkv,
        sums[2],
        sums[3],
        s_out,
        sums[4],
        sums[5],
        s_up,
        s_down,
    )


def solution(mesh):
    split = P(AXES, None)
    in_specs = (split, P("wide", None)) + (P(),) * 10 + (split,)
    vector = P(AXES)
    out_specs = (
        split,
        split,
        vector,
        vector,
        split,
        vector,
        vector,
        split,
        vector,
        vector,
        split,
        split,
    )
    return jax.shard_map(shards, mesh=mesh, in_specs=in_specs, out_specs=out_specs, check_vma=False)
```
